32 devices in a mesh: dp: 2 (over x), expert: 16 (over z, y, core).
Axes of the slice: x: 2, y: 2, z: 4, core: 2. Of those that a mesh axis runs over, the one named last changes fastest.
Arguments:
- queries: bfloat16 [256, 4096], P(('dp', 'expert')), may hold values from -400 to 400
- new_kv: bfloat16 [256, 2, 1024], P(('dp', 'expert')), may hold values from -5 to 5
- cache_keys: bfloat16 [256, 32, 1024], P(('dp', 'expert')), may hold values from -6 to 6
- cache_values: bfloat16 [256, 32, 1024], P(('dp', 'expert')), may hold values from -5 to 5
- lengths: int32 [256], P(('dp', 'expert')), may hold values from 2 to 32, as said below
- residual: bfloat16 [256, 4096], P(('dp', 'expert')), may hold values from -6 to 6
- norm_gain: bfloat16 [4096], replicated, may hold values from 0.099609375 to 1.8984375
- routes: int32 [256, 8], P(('dp', 'expert')), may hold values from 0 to 15, all different within a row; in each aligned block of 8 rows (0 to 7, 8 to 15, ...) at most 8 rows name the same one
- route_weights: float32 [256, 8], P(('dp', 'expert')), may hold values from 0.05 to 1
- gate_codes: float32 [16, 1024, 2048], P('expert', None, 'dp'), may hold values from 0 to 65535, as said below
- gate_scales: bfloat16 [16, 32, 2048], P('expert', None, 'dp'), may hold values from 0.0017166138 to 0.006866455
- up_codes: float32 [16, 1024, 2048], P('expert', None, 'dp'), may hold values from 0 to 65535, as said below
- up_scales: bfloat16 [16, 32, 2048], P('expert', None, 'dp'), may hold values from 0.0017166138 to 0.006866455
- down_codes: float32 [16, 512, 4096], P('expert', None, 'dp'), may hold values from 0 to 65535, as said below
- down_scales: bfloat16 [16, 16, 4096], P('expert', None, 'dp'), may hold values from 0.0024261475 to 0.00970459
Outputs:
- layer_out: bfloat16 [256, 4096], P(('dp', 'expert'))
The draws below stay inside these ranges and needn't reach their ends.
Inputs may be any that keep to these rules, and one draw needn't show every extreme that they name: `routes`: in the 8 rows of one device no expert is named more than 8 times; the 8 experts of a row differ. `lengths`: every device holds a row with all 32 positions valid. `gate_codes`: every entry is a whole number. `up_codes`: every entry is a whole number. `down_codes`: every entry is a whole number.
All inputs are finite; a program needn't handle non-finite values.
Results may differ from the reference program's by a relative error of at most 0.015.
Values may be sent and summed in bfloat16 or wider, within the bound.
No kernel may reach another device: no remote copies, remote signals or barrier semaphores. Data moves between devices by JAX's collectives and lax.ppermute only.
A program may use at most 128 MiB of HBM per device.

```python
import math
import jax
import jax.numpy as jnp
import numpy as np
from jax import lax

D = 4096
HEADS = 32
KV_HEADS = 8
HEAD_DIM = 128
FF = 2048
TOP = 8
GROUP = 128
ROWS_DEV = 8
CACHE = 32
EXPERTS = 16
TOKENS = 256
CAP = 8


def key_table(key):
    return jnp.clip(jax.random.normal(key, (TOKENS, CACHE, KV_HEADS * HEAD_DIM), jnp.float32), -5.0, 5.0)


def packed_words(key, shape):
    words = jax.random.randint(key, shape, 0, 65536, dtype=jnp.int32).astype(jnp.float32)
    return words.at[0, 0, 0].set(0.0).at[0, 0, 1].set(65535.0)


def draw_gate_codes(key, part):
    key = jax.random.fold_in(key, 21)
    return packed_words(key, (EXPERTS, D // 4, FF))


def draw_up_codes(key, part):
    key = jax.random.fold_in(key, 22)
    return packed_words(key, (EXPERTS, D // 4, FF))


def draw_down_codes(key, part):
    key = jax.random.fold_in(key, 23)
    return packed_words(key, (EXPERTS, FF // 4, D))


def draw_cache_keys(key, part):
    shared = key_table(key)
    return shared.astype(jnp.bfloat16)


def draw_queries(key, part):
    key = jax.random.fold_in(key, 11)
    entries = jnp.clip(jax.random.normal(key, (TOKENS, HEADS * HEAD_DIM), jnp.float32), -5.0, 5.0)
    return entries.astype(jnp.bfloat16)


def draw_lengths(key, part):
    key = jax.random.fold_in(key, 7)
    drawn = jax.random.randint(key, (TOKENS,), 2, CACHE + 1, dtype=jnp.int32)
    leading = jnp.arange(TOKENS, dtype=jnp.int32) % ROWS_DEV == 0
    return jnp.where(leading, CACHE, drawn).astype(jnp.int32)


def block_scale(rng, shape, cuts, smallest, high):
    factor_of = 1.0
    for position, parts in cuts:
        draws = jax.random.uniform(jax.random.fold_in(jax.random.fold_in(rng, 6), position), (parts,), jnp.float32, smallest / len(cuts), high / len(cuts))
        factor_of = factor_of * jnp.repeat(jnp.exp(draws), shape[position] // parts).reshape((-1,) + (1,) * (len(shape) - 1 - position))
    return factor_of


def assign_block(key, own, number, rows, number_of, top, bound, slope):
    order = jax.random.permutation(key, number_of)
    heavy_load, usual = portions_of(number_of, rows * top, bound, slope, True), portions_of(number_of, rows * top, bound, slope, False)
    places = jnp.arange(number_of)

    def named(sizes, turn):
        used = int((sizes > 0).sum())
        fixed = max(1, used // 4)
        moved = fixed + (places - fixed + turn * (used - fixed)) % max(1, number_of - fixed)
        return jnp.zeros((number_of,), jnp.int32).at[order[jnp.where(places < fixed, places, moved)]].set(jnp.asarray(sizes, jnp.int32))

    sizes = jnp.where(number % 4 == 0, named(heavy_load, number // 4), named(usual, number - number // 4 - 1))
    mixed = jax.random.permutation(jax.random.fold_in(own, 3), number_of)
    giver, sink = mixed[0:number_of // 2 * 2:2], mixed[1:number_of // 2 * 2:2]
    slack = jnp.minimum(sizes[giver] - 1, bound - sizes[sink]) // 2
    slack = jnp.where((giver == order[0]) | (sink == order[0]) | (sizes[sink] == 0), 0, jnp.maximum(slack, 0))
    moved = jax.random.randint(jax.random.fold_in(own, 4), (number_of // 2,), 0, 1 << 20) % (slack + 1)
    sizes = sizes.at[giver].add(-moved).at[sink].add(moved)
    labels = jnp.searchsorted(jnp.cumsum(sizes), jnp.arange(rows * top), side="right").astype(jnp.int32)
    listing = labels.reshape(top, rows).T
    listing = listing[jax.random.permutation(jax.random.fold_in(own, 1), rows)]
    turn = jax.random.randint(jax.random.fold_in(own, 2), (rows, 1), 0, top)
    return jnp.take_along_axis(listing, (jnp.arange(top)[None, :] + turn) % top, axis=1)


def portions_of(count, total, most, lean, full):
    portions = [(1 << 20) // math.isqrt(grade ** lean) + 1 for grade in range(1, count + 1)]
    largest = most if full else min(most, max(-(-total // count), total * portions[0] // sum(portions)))
    least = 1 if total - largest >= count - 1 else 0
    given, rest = [largest] + [least] * (count - 1), total - largest - least * (count - 1)
    while rest > 0:
        candidates = [i for i in range(1, count) if given[i] < largest] or [i for i in range(1, count) if given[i] < most]
        pool, remaining = sum([portions[i] for i in candidates]), rest
        for i in candidates:
            extra = min(most - given[i], max(1, remaining * portions[i] // pool), rest)
            given[i] = given[i] + extra
            rest = rest - extra
    return np.array(given)


def normal_values(rng, shape, scale, bound, split=(), held_as=jnp.bfloat16):
    values = scale * jax.random.normal(rng, shape, jnp.float32)
    if split:
        values = values * block_scale(rng, shape, split, -0.22, 0.18)
    return jnp.clip(values, -bound, bound).astype(held_as)


def setup_inputs(seed: int = 0) -> dict:
    key_list = jax.random.split(jax.random.key(seed), 16)
    queries = draw_queries(jax.random.fold_in(key_list[15], 71), 0)
    new_kv = normal_values(key_list[1], (TOKENS, 2, KV_HEADS * HEAD_DIM), 1.0, 5.0, ((0, 32),))
    cache_keys = draw_cache_keys(jax.random.fold_in(key_list[15], 71), 0)
    cache_values = normal_values(key_list[3], (TOKENS, CACHE, KV_HEADS * HEAD_DIM), 1.0, 5.0, ((0, 32),))
    lengths = draw_lengths(jax.random.fold_in(key_list[15], 71), 0)
    residual = normal_values(key_list[5], (TOKENS, D), 1.0, 6.0, ((0, 32),))
    norm_gain = jnp.clip(1.0 + 0.18 * jax.random.normal(key_list[6], (D,), jnp.float32), 0.099609375, 1.8984375).astype(jnp.bfloat16)
    routes_keys = jax.random.split(jax.random.fold_in(key_list[7], 1), TOKENS // ROWS_DEV)
    routes_turns = jax.random.permutation(jax.random.fold_in(key_list[7], 3), TOKENS // ROWS_DEV)
    routes = jax.vmap(lambda own, number: assign_block(jax.random.fold_in(key_list[7], 2), own, number, ROWS_DEV, EXPERTS, TOP, CAP, 1))(routes_keys, routes_turns).reshape((TOKENS, TOP))
    route_weights = jnp.clip(jnp.exp(math.log(1.0) - 2.9957323 * jax.random.uniform(key_list[8], (TOKENS, TOP), jnp.float32) ** block_scale(key_list[8], (TOKENS, TOP), ((0, 32),), -0.2, 0.2)), 0.05, 1.0)
    gate_codes = draw_gate_codes(jax.random.fold_in(key_list[15], 71), 0)
    gate_scales = jnp.clip(jnp.exp(math.log(0.006866455) - 1.3862944 * jax.random.uniform(key_list[10], (EXPERTS, D // GROUP, FF), jnp.float32) ** block_scale(key_list[10], (EXPERTS, D // GROUP, FF), ((0, 16), (2, 2)), -0.2, 0.2)), 0.0017166138, 0.006866455).astype(jnp.bfloat16)
    up_codes = draw_up_codes(jax.random.fold_in(key_list[15], 71), 0)
    up_scales = jnp.clip(jnp.exp(math.log(0.006866455) - 1.3862944 * jax.random.uniform(key_list[12], (EXPERTS, D // GROUP, FF), jnp.float32) ** block_scale(key_list[12], (EXPERTS, D // GROUP, FF), ((0, 16), (2, 2)), -0.2, 0.2)), 0.0017166138, 0.006866455).astype(jnp.bfloat16)
    down_codes = draw_down_codes(jax.random.fold_in(key_list[15], 71), 0)
    down_scales = jnp.clip(jnp.exp(math.log(0.00970459) - 1.3862944 * jax.random.uniform(key_list[14], (EXPERTS, FF // GROUP, D), jnp.float32) ** block_scale(key_list[14], (EXPERTS, FF // GROUP, D), ((0, 16), (2, 2)), -0.2, 0.2)), 0.0024261475, 0.00970459).astype(jnp.bfloat16)
    return {"queries": queries, "new_kv": new_kv, "cache_keys": cache_keys, "cache_values": cache_values, "lengths": lengths, "residual": residual, "norm_gain": norm_gain, "routes": routes, "route_weights": route_weights, "gate_codes": gate_codes, "gate_scales": gate_scales, "up_codes": up_codes, "up_scales": up_scales, "down_codes": down_codes, "down_scales": down_scales}


def unpack(codes, scales):
    quarter = codes.shape[0]
    width = codes.shape[1]
    divisors = jnp.array([1.0, 1.0 / 16, 1.0 / 256, 1.0 / 4096], jnp.float32)[:, None, None]
    lifted = jnp.floor(codes[None, :, :] * divisors)
    levels = lifted - 16.0 * jnp.floor(lifted * (1.0 / 16)) - 8.0
    height = 4 * quarter
    grouped = levels.reshape(height // GROUP, GROUP, width) * scales.astype(jnp.float32)[:, None, :]
    return grouped.reshape(height, width).astype(jnp.bfloat16)

def attend(queries, new_kv, cache_keys, cache_values, lengths):
    row_count = queries.shape[0]
    groups = HEADS // KV_HEADS
    queried = queries.astype(jnp.float32).reshape(row_count, KV_HEADS, groups, HEAD_DIM)
    cached_keys = cache_keys.astype(jnp.float32).reshape(row_count, CACHE, KV_HEADS, HEAD_DIM)
    cached_values = cache_values.astype(jnp.float32).reshape(row_count, CACHE, KV_HEADS, HEAD_DIM)
    fresh_key = new_kv[:, 0].astype(jnp.float32).reshape(row_count, KV_HEADS, HEAD_DIM)
    fresh_value = new_kv[:, 1].astype(jnp.float32).reshape(row_count, KV_HEADS, HEAD_DIM)
    scaling = HEAD_DIM ** (-0.5)
    earlier = jnp.einsum('bjgd,bcjd->bjgc', queried, cached_keys) * scaling
    current = jnp.einsum('bjgd,bjd->bjg', queried, fresh_key) * scaling
    valid = (jnp.arange(CACHE, dtype=jnp.int32)[None, :] < lengths[:, None])[:, None, None, :]
    largest = jnp.maximum(lax.optimization_barrier(jnp.max(jnp.where(valid, earlier, -1e+30), axis=-1)), current)
    earlier_w = jnp.where(valid, jnp.exp(earlier - largest[..., None]), 0.0)
    current_w = jnp.exp(current - largest)
    denominator = lax.optimization_barrier(jnp.sum(earlier_w, axis=-1)) + current_w
    earlier_p = (earlier_w / denominator[..., None]).astype(jnp.bfloat16)
    current_p = (current_w / denominator).astype(jnp.bfloat16)
    attended = jnp.einsum('bjgc,bcjd->bjgd', earlier_p.astype(jnp.float32), cached_values)
    attended = attended + current_p.astype(jnp.float32)[..., None] * fresh_value[:, :, None, :]
    return attended.reshape(row_count, HEADS * HEAD_DIM).astype(jnp.bfloat16)

def normalize(mixed, norm_gain):
    widened = mixed.astype(jnp.float32)
    meansq = lax.optimization_barrier(jnp.mean(widened * widened, axis=-1, keepdims=True))
    return (widened * lax.rsqrt(meansq + 1e-06) * norm_gain.astype(jnp.float32)).astype(jnp.bfloat16)

def reference(queries, new_kv, cache_keys, cache_values, lengths, residual, norm_gain, routes, route_weights, gate_codes, gate_scales, up_codes, up_scales, down_codes, down_scales):
    attended = attend(queries, new_kv, cache_keys, cache_values, lengths)
    mixed = (residual.astype(jnp.float32) + attended.astype(jnp.float32)).astype(jnp.bfloat16)
    normed = normalize(mixed, norm_gain)
    shares = route_weights / lax.optimization_barrier(jnp.sum(route_weights, axis=1, keepdims=True))
    slots_each = TOKENS // ROWS_DEV * CAP
    span = min(128, slots_each)
    padded_slots = (slots_each + span - 1) // span * span

    def expert_step(carried, expert):
        hits = routes == expert
        present = jnp.any(hits, axis=1)
        load = jnp.sum(present.astype(jnp.int32)).astype(jnp.int32)
        chosen = jnp.nonzero(present, size=padded_slots, fill_value=0)[0].astype(jnp.int32)
        row_weight = lax.optimization_barrier(jnp.sum(jnp.where(hits, shares, 0.0), axis=1))
        w_gate = unpack(gate_codes[expert], gate_scales[expert])
        w_up = unpack(up_codes[expert], up_scales[expert])
        w_down = unpack(down_codes[expert], down_scales[expert])

        def block_step(block, total):
            start = (block * span).astype(jnp.int32)
            index = lax.dynamic_slice(chosen, (start,), (span,))
            live = start + jnp.arange(span, dtype=jnp.int32) < load
            inputs = normed[index]
            gate = jnp.dot(inputs, w_gate, preferred_element_type=jnp.float32)
            upward = jnp.dot(inputs, w_up, preferred_element_type=jnp.float32)
            hidden = (jax.nn.silu(gate) * upward).astype(jnp.bfloat16)
            result = jnp.dot(hidden, w_down, preferred_element_type=jnp.float32).astype(jnp.bfloat16)
            weight = jnp.where(live, row_weight[index], 0.0)
            return total.at[index].add(weight[:, None] * result.astype(total.dtype))
        blocks = ((load + span - 1) // span).astype(jnp.int32)
        carried = lax.fori_loop(jnp.int32(0), blocks, block_step, carried)
        return (carried, None)
    summed, unused = lax.scan(expert_step, jnp.zeros((TOKENS, D), jnp.float32), jnp.arange(EXPERTS, dtype=jnp.int32))
    return (mixed.astype(jnp.float32) + summed).astype(jnp.bfloat16)
```

```python
import functools

import jax
import jax.numpy as jnp
from jax import lax
from jax.experimental import pallas as pl
from jax.experimental.pallas import tpu as pltpu
from jax.sharding import PartitionSpec as P

HEAD_DIM = 128
GROUP = 128
TOP = 8
LANES = 128
VMEM_LIMIT = 56 * 2**20
VMEM_MOST = 54 * 2**20
VMEM_SOME = 16 * 2**20
F32 = jnp.float32
BF16 = jnp.bfloat16


def front_kernel(
    lengths_ref,
    queries_ref,
    new_kv_ref,
    keys_ref,
    values_ref,
    residual_ref,
    gain_ref,
    routes_ref,
    weights_ref,
    mixed_ref,
    payload_ref,
):
    rows, cache, kv_width = keys_ref.shape
    width = queries_ref.shape[1]
    kv_heads = kv_width // HEAD_DIM
    per = width // kv_width
    scaling = HEAD_DIM ** (-0.5)
    row_id = lax.broadcasted_iota(jnp.int32, (rows, rows * cache), 0)
    lane_id = lax.broadcasted_iota(jnp.int32, (rows, rows * cache), 1)
    bound = jnp.zeros((rows, rows * cache), jnp.int32)
    for r in range(rows):
        bound = jnp.where(row_id == r, r * cache + lengths_ref[r], bound)
    valid = (lane_id >= row_id * cache) & (lane_id < bound)
    total = jnp.zeros((rows, 1), F32)
    for j in range(kv_heads):
        span = slice(j * HEAD_DIM, (j + 1) * HEAD_DIM)
        heads = [j * per + g for g in range(per)]
        queried = jnp.concatenate(
            [queries_ref[:, h * HEAD_DIM : (h + 1) * HEAD_DIM].astype(F32) for h in heads], axis=0
        )
        keys = keys_ref[:, :, span].reshape(rows * cache, HEAD_DIM)
        values = values_ref[:, :, span].reshape(rows * cache, HEAD_DIM)
        fresh_key = new_kv_ref[:, 0, span].astype(F32)
        fresh_value = new_kv_ref[:, 1, span].astype(F32)
        earlier = lax.dot_general(
            queried.astype(BF16), keys, (((1,), (1,)), ((), ())), preferred_element_type=F32
        )
        earlier = earlier.reshape(per, rows, rows * cache) * scaling
        current = (
            jnp.sum(queried.reshape(per, rows, HEAD_DIM) * fresh_key[None], axis=-1, keepdims=True)
            * scaling
        )
        earlier = jnp.where(valid[None], earlier, -1e30)
        largest = jnp.maximum(jnp.max(earlier, axis=-1, keepdims=True), current)
        earlier_w = jnp.where(valid[None], jnp.exp(earlier - largest), 0.0)
        current_w = jnp.exp(current - largest)
        denominator = jnp.sum(earlier_w, axis=-1, keepdims=True) + current_w
        earlier_p = (earlier_w / denominator).astype(BF16).reshape(per * rows, rows * cache)
        current_p = (current_w / denominator).astype(BF16).astype(F32)
        attended = jnp.dot(earlier_p, values, preferred_element_type=F32)
        attended = attended.reshape(per, rows, HEAD_DIM) + current_p * fresh_value[None]
        for g, h in enumerate(heads):
            place = slice(h * HEAD_DIM, (h + 1) * HEAD_DIM)
            mixed = (
                residual_ref[:, place].astype(F32) + attended[g].astype(BF16).astype(F32)
            ).astype(BF16)
            mixed_ref[:, place] = mixed
            widened = mixed.astype(F32)
            total = total + jnp.sum(widened * widened, axis=-1, keepdims=True)
    inverse = lax.rsqrt(total * (1.0 / width) + 1e-06)
    payload_ref[:, :width] = (
        mixed_ref[...].astype(F32) * inverse * gain_ref[...].astype(F32)
    ).astype(BF16)
    if payload_ref.shape[1] > width:
        shares = weights_ref[...] / jnp.sum(weights_ref[...], axis=1, keepdims=True)
        lane = lax.broadcasted_iota(jnp.int32, (rows, LANES), 1)
        expert = jnp.where(lane < LANES // 2, lane, lane - LANES // 2)
        table = jnp.zeros((rows, LANES), F32)
        for k in range(routes_ref.shape[1]):
            table = table + jnp.where(
                routes_ref[:, k : k + 1] == expert, shares[:, k : k + 1], 0.0
            )
        high = table.astype(BF16).astype(F32)
        payload_ref[:, width:] = jnp.where(lane < LANES // 2, high, table - high).astype(BF16)


def front(queries, new_kv, keys, values, lengths, residual, gain, routes, weights, extra):
    rows, width = queries.shape
    vmem = pl.BlockSpec(memory_space=pltpu.VMEM)
    return pl.pallas_call(
        front_kernel,
        out_shape=(
            jax.ShapeDtypeStruct((rows, width), BF16),
            jax.ShapeDtypeStruct((rows, width + extra), BF16),
        ),
        in_specs=[pl.BlockSpec(memory_space=pltpu.SMEM)] + [vmem] * 8,
        out_specs=(vmem, vmem),
        compiler_params=pltpu.CompilerParams(vmem_limit_bytes=VMEM_LIMIT),
        cost_estimate=pl.CostEstimate(
            flops=4 * 256 * 256 * 1024, bytes_accessed=2 * 2**20, transcendentals=65536
        ),
        name="front",
    )(lengths, queries, new_kv, keys, values, residual, gain.reshape(1, -1), routes, weights)


def unpack_tile(codes_ref, scales, store, digits):
    depth, width = codes_ref.shape
    step = 256 if width % 256 == 0 else LANES
    for column in range(0, width, step):
        spans = [
            jnp.broadcast_to(scales[k][:, column : column + step], (16, step)).astype(BF16)
            for k in digits
        ]

        def chunk(i, carry, column=column, spans=spans):
            start = pl.multiple_of(i * 16, 16)
            words = codes_ref[pl.ds(start, 16), column : column + step].astype(jnp.int32)
            for n, k in enumerate(digits):
                digit = words if k == 0 else lax.shift_right_logical(words, 4 * k)
                if k < 3:
                    digit = digit & 15
                level = digit.astype(F32).astype(BF16) - jnp.asarray(8, BF16)
                store(n, start, column, step, level * spans[n])
            return carry

        lax.fori_loop(0, depth // 16, chunk, 0, unroll=True)


def unpack_kernel(codes_ref, scales_ref, out_ref):
    group = pl.program_id(0)
    groups = pl.num_programs(0)
    scales = [scales_ref[pl.ds(k * groups + group, 1), :] for k in range(4)]

    def store(n, start, column, step, value):
        out_ref[n, pl.ds(start, 16), column : column + step] = value

    unpack_tile(codes_ref, scales, store, range(4))


def unpack_one(codes, scales):
    quarter, width = codes.shape
    groups = quarter // GROUP
    weight = pl.pallas_call(
        unpack_kernel,
        grid=(groups,),
        out_shape=jax.ShapeDtypeStruct((4, quarter, width), BF16),
        in_specs=[
            pl.BlockSpec((GROUP, width), lambda i: (i, 0)),
            pl.BlockSpec((4 * groups, width), lambda i: (0, 0)),
        ],
        out_specs=pl.BlockSpec((4, GROUP, width), lambda i: (0, i, 0)),
        compiler_params=pltpu.CompilerParams(vmem_limit_bytes=VMEM_LIMIT),
        cost_estimate=pl.CostEstimate(
            flops=quarter * width * 24, bytes_accessed=quarter * width * 12, transcendentals=0
        ),
        name="unpack_weights",
    )(codes, scales.astype(F32))
    return weight.reshape(4 * quarter, width)


def hidden_kernel(place_ref, *refs):
    pieces, (gate_ref, up_ref, out_ref, share_ref, rows_ref) = refs[:-5], refs[-5:]
    depth = gate_ref.shape[0]
    block = pieces[0].shape[0]

    @pl.when(pl.program_id(0) == 0)
    def _():
        for n, piece in enumerate(pieces):
            rows_ref[n * block : (n + 1) * block, :] = piece[:, :depth]
            table = piece[:, depth:].astype(F32)
            lane = lax.broadcasted_iota(jnp.int32, table.shape, 1)
            mine = place_ref[0]
            chosen = (lane == mine) | (lane == mine + LANES // 2)
            share = jnp.sum(jnp.where(chosen, table, 0.0), axis=1, keepdims=True)
            share_ref[n * block : (n + 1) * block, :] = jnp.broadcast_to(share, table.shape)

    inputs = rows_ref[...]
    gate = jnp.dot(inputs, gate_ref[...], preferred_element_type=F32)
    upward = jnp.dot(inputs, up_ref[...], preferred_element_type=F32)
    out_ref[...] = (gate / (1.0 + jnp.exp(-gate)) * upward).astype(BF16)


def hidden_units(pieces, w_gate, w_up, place):
    block, padded = pieces[0].shape
    count = block * len(pieces)
    depth, width = w_gate.shape
    step = 256
    spec = pl.BlockSpec((depth, step), lambda i: (0, i))
    piece_spec = pl.BlockSpec((block, padded), lambda i: (0, 0))
    return pl.pallas_call(
        hidden_kernel,
        grid=(width // step,),
        out_shape=(
            jax.ShapeDtypeStruct((count, width), BF16),
            jax.ShapeDtypeStruct((count, LANES), F32),
        ),
        in_specs=[pl.BlockSpec(memory_space=pltpu.SMEM)] + [piece_spec] * len(pieces) + [spec, spec],
        out_specs=(
            pl.BlockSpec((count, step), lambda i: (0, i)),
            pl.BlockSpec((count, LANES), lambda i: (0, 0)),
        ),
        scratch_shapes=[pltpu.VMEM((count, depth), BF16)],
        compiler_params=pltpu.CompilerParams(vmem_limit_bytes=VMEM_MOST),
        cost_estimate=pl.CostEstimate(
            flops=4 * count * depth * width,
            bytes_accessed=4 * depth * width + 2 * count * padded,
            transcendentals=count * width,
        ),
        name="gate_up",
    )(place, *pieces, w_gate, w_up)


def own_down_kernel(place_ref, codes_ref, scales_ref, hidden_ref, partial_ref, peer_ref, own_ref):
    quarter, width = codes_ref.shape
    groups = quarter // GROUP
    half = hidden_ref.shape[1]
    mine = place_ref[0]

    for group in range(groups):
        rows_of = codes_ref.at[group * GROUP : (group + 1) * GROUP, :]
        scales = [scales_ref[k * groups + group : k * groups + group + 1, :] for k in range(4)]

        def store_own(n, start, column, step, value, group=group):
            own_ref[pl.ds((n % 2) * quarter + group * GROUP + start, 16), column : column + step] = value

        def store_peer(n, start, column, step, value, group=group):
            peer_ref[pl.ds((n % 2) * quarter + group * GROUP + start, 16), column : column + step] = value

        @pl.when(mine == 0)
        def _():
            unpack_tile(rows_of, scales, store_own, (0, 1))
            unpack_tile(rows_of, scales, store_peer, (2, 3))

        @pl.when(mine == 1)
        def _():
            unpack_tile(rows_of, scales, store_peer, (0, 1))
            unpack_tile(rows_of, scales, store_own, (2, 3))

    partial_ref[...] = jnp.dot(hidden_ref[...], own_ref[...], preferred_element_type=F32)


def own_down(place, codes, scales, hidden):
    quarter, width = codes.shape
    count, half = hidden.shape
    step = 256
    return pl.pallas_call(
        own_down_kernel,
        grid_spec=pltpu.PrefetchScalarGridSpec(
            num_scalar_prefetch=1,
            grid=(width // step,),
            in_specs=[
                pl.BlockSpec((quarter, step), lambda i, p: (0, i)),
                pl.BlockSpec((scales.shape[0], step), lambda i, p: (0, i)),
                pl.BlockSpec((count, half), lambda i, p: (0, 0)),
            ],
            out_specs=(
                pl.BlockSpec((count, step), lambda i, p: (0, i)),
                pl.BlockSpec((half, step), lambda i, p: (0, i)),
            ),
            scratch_shapes=[pltpu.VMEM((half, step), BF16)],
        ),
        out_shape=(
            jax.ShapeDtypeStruct((count, width), F32),
            jax.ShapeDtypeStruct((half, width), BF16),
        ),
        compiler_params=pltpu.CompilerParams(vmem_limit_bytes=VMEM_MOST),
        cost_estimate=pl.CostEstimate(
            flops=2 * count * half * width + 24 * quarter * width,
            bytes_accessed=4 * quarter * width + 2 * half * width + 4 * count * width,
            transcendentals=0,
        ),
        name="down_own",
    )(place, codes, scales.astype(F32), hidden)


def peer_down_kernel(block, partial_ref, hidden_ref, weight_ref, share_ref, keep_ref, send_ref, rows_ref):
    @pl.when(pl.program_id(0) == 0)
    def _():
        for n in range(hidden_ref.shape[0] // block):
            source = (n ^ 1) * block
            rows_ref[n * block : (n + 1) * block, :] = hidden_ref[source : source + block, :]

    produced = partial_ref[...] + jnp.dot(
        rows_ref[...], weight_ref[...], preferred_element_type=F32
    )
    result = (produced.astype(BF16).astype(F32) * share_ref[:, :1]).astype(BF16)
    half = keep_ref.shape[0]
    keep_ref[...] = result[:half]
    send_ref[...] = result[half:]


def peer_down(partial, hidden, weight, share, block):
    count, width = partial.shape
    half = hidden.shape[1]
    step = 512
    shape = jax.ShapeDtypeStruct((count // 2, width), BF16)
    out_spec = pl.BlockSpec((count // 2, step), lambda i: (0, i))
    return pl.pallas_call(
        functools.partial(peer_down_kernel, block),
        grid=(width // step,),
        out_shape=(shape, shape),
        in_specs=[
            pl.BlockSpec((count, step), lambda i: (0, i)),
            pl.BlockSpec((count, half), lambda i: (0, 0)),
            pl.BlockSpec((half, step), lambda i: (0, i)),
            pl.BlockSpec((count, LANES), lambda i: (0, 0)),
        ],
        out_specs=(out_spec, out_spec),
        scratch_shapes=[pltpu.VMEM((count, half), BF16)],
        compiler_params=pltpu.CompilerParams(vmem_limit_bytes=VMEM_MOST),
        cost_estimate=pl.CostEstimate(
            flops=2 * count * half * width,
            bytes_accessed=6 * count * width + 2 * half * width,
            transcendentals=0,
        ),
        name="down_peer",
    )(partial, hidden, weight, share)


def halve_kernel(kept_ref, arrived_ref, *out_refs):
    total = kept_ref[...].astype(F32) + arrived_ref[...].astype(F32)
    size = total.shape[0] // len(out_refs)
    for n, out_ref in enumerate(out_refs):
        out_ref[...] = total[n * size : (n + 1) * size].astype(out_ref.dtype)


def add_and_cut(kept, arrived, parts):
    count, width = kept.shape
    vmem = pl.BlockSpec(memory_space=pltpu.VMEM)
    shape = jax.ShapeDtypeStruct((count // parts, width), BF16)
    return pl.pallas_call(
        halve_kernel,
        out_shape=(shape,) * parts,
        in_specs=[vmem, vmem],
        out_specs=(vmem,) * parts,
        compiler_params=pltpu.CompilerParams(vmem_limit_bytes=VMEM_SOME),
        cost_estimate=pl.CostEstimate(
            flops=count * width, bytes_accessed=6 * count * width, transcendentals=0
        ),
        name="add_and_cut",
    )(kept, arrived)


def finish_kernel(side_ref, mixed_ref, *refs):
    near, far, out_ref = refs[: len(refs) // 2], refs[len(refs) // 2 : -1], refs[-1]
    half = mixed_ref.shape[1] // 2

    def total(parts):
        result = parts[0][...].astype(F32)
        for part in parts[1:]:
            result = result + part[...].astype(F32)
        return result

    def write(first, second):
        out_ref[:, :half] = (mixed_ref[:, :half].astype(F32) + total(first)).astype(BF16)
        out_ref[:, half:] = (mixed_ref[:, half:].astype(F32) + total(second)).astype(BF16)

    @pl.when(side_ref[0] == 0)
    def _():
        write(near, far)

    @pl.when(side_ref[0] != 0)
    def _():
        write(far, near)


def finish(side, mixed, near, far):
    vmem = pl.BlockSpec(memory_space=pltpu.VMEM)
    return pl.pallas_call(
        finish_kernel,
        out_shape=jax.ShapeDtypeStruct(mixed.shape, BF16),
        in_specs=[pl.BlockSpec(memory_space=pltpu.SMEM)] + [vmem] * (1 + len(near) + len(far)),
        out_specs=vmem,
        compiler_params=pltpu.CompilerParams(vmem_limit_bytes=VMEM_SOME),
        name="finish",
    )(side, mixed, *near, *far)


def dense(payload, mixed, codes):
    gate_codes, gate_scales, up_codes, up_scales, down_codes, down_scales = codes
    groups = lax.axis_size("dp")
    experts = lax.axis_size("expert")
    devices = groups * experts
    core, line, layer, plane = 1, 2, 4, experts
    layers = experts // layer
    side = lax.axis_index("dp").reshape(1).astype(jnp.int32)
    place = lax.axis_index("expert").reshape(1).astype(jnp.int32)

    def swap(block, offset):
        return lax.ppermute(block, ("dp", "expert"), [(i, i ^ offset) for i in range(devices)])

    stack = jnp.concatenate(
        [payload] + [swap(payload, z * layer) for z in range(1, layers)], axis=0
    )
    near = [stack, swap(stack, plane), swap(stack, line), swap(stack, plane ^ line)]
    pieces = near + [swap(piece, core) for piece in near]
    w_gate = unpack_one(gate_codes, gate_scales)
    w_up = unpack_one(up_codes, up_scales)
    hidden, share = hidden_units(pieces, w_gate, w_up, place)
    peer_hidden = swap(hidden, plane)
    partial, peer_weight = own_down(side, down_codes, down_scales, hidden)
    keep, send = peer_down(partial, peer_hidden, peer_weight, share, stack.shape[0])
    keep, send = add_and_cut(keep, swap(send, core), 2)
    blocks = add_and_cut(keep, swap(send, line), 2 * layers)
    near = [blocks[0]] + [swap(blocks[z], z * layer) for z in range(1, layers)]
    far = [swap(blocks[layers + z], plane ^ (z * layer)) for z in range(layers)]
    return finish(side, mixed, near, far)


def slot_table(routes, experts, capacity):
    flattened = routes.reshape(-1)
    onehot = (flattened[:, None] == jnp.arange(experts, dtype=jnp.int32)[None, :]).astype(jnp.int32)
    ranking = jnp.sum((jnp.cumsum(onehot, axis=0) - 1) * onehot, axis=1)
    return (flattened * capacity + ranking).reshape(routes.shape)


def dispatch(block, slots, width):
    targets = jnp.arange(width, dtype=jnp.int32)
    placing = jnp.sum((slots[None, :, :] == targets[:, None, None]).astype(F32), axis=2)
    return jnp.dot(placing.astype(BF16), block, preferred_element_type=F32).astype(BF16)


def unpack(codes, scales):
    quarter, width = codes.shape
    divisors = jnp.array([1.0, 1.0 / 16, 1.0 / 256, 1.0 / 4096], F32)[:, None, None]
    lifted = jnp.floor(codes[None, :, :] * divisors)
    levels = lifted - 16.0 * jnp.floor(lifted * (1.0 / 16)) - 8.0
    height = 4 * quarter
    grouped = levels.reshape(height // GROUP, GROUP, width) * scales.astype(F32)[:, None, :]
    return grouped.reshape(height, width).astype(BF16)


def routed(normed, mixed, routes, route_weights, codes, capacity):
    gate_codes, gate_scales, up_codes, up_scales, down_codes, down_scales = codes
    experts = lax.axis_size("expert")
    groups = lax.axis_size("dp")
    row_count, width = mixed.shape
    own_slots = slot_table(routes, experts, capacity)
    w_gate = unpack(gate_codes, gate_scales)
    w_up = unpack(up_codes, up_scales)
    w_down = unpack(down_codes, down_scales)
    local_units = w_gate.shape[1]
    peer_rows = lax.all_gather(normed, "dp", axis=0, tiled=True).reshape(groups, row_count, width)
    peer_routes = lax.all_gather(routes, "dp", axis=0, tiled=True).reshape(groups, row_count, TOP)

    def build(block, table):
        return dispatch(block, slot_table(table, experts, capacity), experts * capacity)

    outgoing = jax.vmap(build)(peer_rows, peer_routes).reshape(groups, experts, capacity, width)
    items = lax.all_to_all(outgoing, "expert", split_axis=1, concat_axis=1, tiled=True)
    inputs = items.reshape(-1, width)
    gate = jnp.dot(inputs, w_gate, preferred_element_type=F32)
    upward = jnp.dot(inputs, w_up, preferred_element_type=F32)
    hidden = (jax.nn.silu(gate) * upward).astype(BF16).reshape(-1, local_units)
    produced = jnp.dot(
        lax.all_gather(hidden, "dp", axis=1, tiled=True), w_down, preferred_element_type=F32
    ).astype(BF16)
    produced = produced.reshape(groups, -1, produced.shape[1])
    returned = lax.all_to_all(
        lax.all_to_all(produced, "dp", split_axis=0, concat_axis=2, tiled=True),
        "expert",
        split_axis=1,
        concat_axis=0,
        tiled=True,
    )
    shares = route_weights / jnp.sum(route_weights, axis=1, keepdims=True)
    targets = jnp.arange(experts * capacity, dtype=jnp.int32)
    spreading = jnp.sum(
        jnp.where(own_slots[:, :, None] == targets[None, None, :], shares[:, :, None], 0.0), axis=1
    )
    combined = jnp.dot(
        spreading, returned.reshape(-1, width).astype(F32), precision=lax.Precision.HIGHEST
    )
    return (mixed.astype(F32) + combined).astype(BF16)


def body(
    queries,
    new_kv,
    cache_keys,
    cache_values,
    lengths,
    residual,
    norm_gain,
    routes,
    route_weights,
    *packed,
):
    experts = lax.axis_size("expert")
    groups = lax.axis_size("dp")
    row_count = queries.shape[0]
    capacity = min(row_count, max(2, 2 * row_count * TOP // experts))
    every = (
        capacity == row_count
        and groups == 2
        and experts <= LANES // 2
        and experts % 4 == 0
        and experts & (experts - 1) == 0
    )
    mixed, payload = front(
        queries,
        new_kv,
        cache_keys,
        cache_values,
        lengths,
        residual,
        norm_gain,
        routes,
        route_weights,
        LANES if every else 0,
    )
    codes = [array[0] for array in packed]
    if every:
        return dense(payload, mixed, codes)
    return routed(payload, mixed, routes, route_weights, codes, capacity)


def solution(mesh):
    return jax.shard_map(
        body,
        mesh=mesh,
        in_specs=(
            P(("dp", "expert"), None),
            P(("dp", "expert"), None, None),
            P(("dp", "expert"), None, None),
            P(("dp", "expert"), None, None),
            P(("dp", "expert")),
            P(("dp", "expert"), None),
            P(),
            P(("dp", "expert"), None),
            P(("dp", "expert"), None),
            P("expert", None, "dp"),
            P("expert", None, "dp"),
            P("expert", None, "dp"),
            P("expert", None, "dp"),
            P("expert", None, "dp"),
            P("expert", None, "dp"),
        ),
        out_specs=P(("dp", "expert"), None),
        check_vma=False,
    )
```

```python
import functools

import jax
import jax.numpy as jnp
from jax import lax
from jax.experimental import pallas as pl
from jax.experimental.pallas import tpu as pltpu
from jax.sharding import PartitionSpec as P

HEAD_DIM = 128
GROUP = 128
TOP = 8
LANES = 128
VMEM_LIMIT = 56 * 2**20
VMEM_SOME = 16 * 2**20
SMALL = pl.CostEstimate(flops=1, bytes_accessed=1, transcendentals=0)
F32 = jnp.float32
BF16 = jnp.bfloat16


def front_kernel(
    lengths_ref,
    queries_ref,
    new_kv_ref,
    keys_ref,
    values_ref,
    residual_ref,
    gain_ref,
    routes_ref,
    weights_ref,
    mixed_ref,
    payload_ref,
):
    rows, cache, kv_width = keys_ref.shape
    width = queries_ref.shape[1]
    kv_heads = kv_width // HEAD_DIM
    per = width // kv_width
    scaling = HEAD_DIM ** (-0.5)
    row_id = lax.broadcasted_iota(jnp.int32, (rows, rows * cache), 0)
    lane_id = lax.broadcasted_iota(jnp.int32, (rows, rows * cache), 1)
    bound = jnp.zeros((rows, rows * cache), jnp.int32)
    for r in range(rows):
        bound = jnp.where(row_id == r, r * cache + lengths_ref[r], bound)
    valid = (lane_id >= row_id * cache) & (lane_id < bound)
    earlier, current = [], []
    for j in range(kv_heads):
        span = slice(j * HEAD_DIM, (j + 1) * HEAD_DIM)
        heads = range(j * per, (j + 1) * per)
        queried = jnp.concatenate(
            [queries_ref[:, h * HEAD_DIM : (h + 1) * HEAD_DIM].astype(F32) for h in heads], axis=0
        )
        keys = keys_ref[:, :, span].reshape(rows * cache, HEAD_DIM)
        earlier.append(
            lax.dot_general(
                queried.astype(BF16), keys, (((1,), (1,)), ((), ())), preferred_element_type=F32
            )
        )
        fresh_key = new_kv_ref[:, 0, span].astype(F32)
        current.append(queried.reshape(per, rows, HEAD_DIM) * fresh_key[None])
    earlier = jnp.concatenate(earlier, axis=0).reshape(kv_heads * per, rows, rows * cache)
    earlier = jnp.where(valid[None], earlier * scaling, -1e30)
    current = jnp.sum(jnp.concatenate(current, axis=0), axis=-1, keepdims=True) * scaling
    largest = jnp.maximum(jnp.max(earlier, axis=-1, keepdims=True), current)
    earlier_w = jnp.where(valid[None], jnp.exp(earlier - largest), 0.0)
    current_w = jnp.exp(current - largest)
    inverse = 1.0 / (jnp.sum(earlier_w, axis=-1, keepdims=True) + current_w)
    earlier_p = (earlier_w * inverse).astype(BF16).reshape(kv_heads * per * rows, rows * cache)
    current_p = (current_w * inverse).astype(BF16).astype(F32)
    total = jnp.zeros((rows, HEAD_DIM), F32)
    for j in range(kv_heads):
        span = slice(j * HEAD_DIM, (j + 1) * HEAD_DIM)
        values = values_ref[:, :, span].reshape(rows * cache, HEAD_DIM)
        fresh_value = new_kv_ref[:, 1, span].astype(F32)
        attended = jnp.dot(
            earlier_p[j * per * rows : (j + 1) * per * rows], values, preferred_element_type=F32
        )
        attended = attended.reshape(per, rows, HEAD_DIM)
        attended = attended + current_p[j * per : (j + 1) * per] * fresh_value[None]
        for g in range(per):
            h = j * per + g
            place = slice(h * HEAD_DIM, (h + 1) * HEAD_DIM)
            mixed = (
                residual_ref[:, place].astype(F32) + attended[g].astype(BF16).astype(F32)
            ).astype(BF16)
            mixed_ref[:, place] = mixed
            widened = mixed.astype(F32)
            total = total + widened * widened
    meansq = jnp.sum(total, axis=-1, keepdims=True) * (1.0 / width)
    inverse = lax.rsqrt(meansq + 1e-06)
    payload_ref[:, :width] = (
        mixed_ref[...].astype(F32) * inverse * gain_ref[...].astype(F32).reshape(1, width)
    ).astype(BF16)
    if payload_ref.shape[1] > width:
        shares = weights_ref[...] / jnp.sum(weights_ref[...], axis=1, keepdims=True)
        lane = lax.broadcasted_iota(jnp.int32, (rows, LANES), 1)
        expert = jnp.where(lane < LANES // 2, lane, lane - LANES // 2)
        table = jnp.zeros((rows, LANES), F32)
        for k in range(routes_ref.shape[1]):
            table = table + jnp.where(
                routes_ref[:, k : k + 1] == expert, shares[:, k : k + 1], 0.0
            )
        high = table.astype(BF16).astype(F32)
        payload_ref[:, width:] = jnp.where(lane < LANES // 2, high, table - high).astype(BF16)


def front(queries, new_kv, keys, values, lengths, residual, gain, routes, weights, extra):
    rows, width = queries.shape
    vmem = pl.BlockSpec(memory_space=pltpu.VMEM)
    return pl.pallas_call(
        front_kernel,
        out_shape=(
            jax.ShapeDtypeStruct((rows, width), BF16),
            jax.ShapeDtypeStruct((rows, width + extra), BF16),
        ),
        in_specs=[pl.BlockSpec(memory_space=pltpu.SMEM)] + [vmem] * 8,
        out_specs=(vmem, vmem),
        compiler_params=pltpu.CompilerParams(vmem_limit_bytes=VMEM_LIMIT),
        cost_estimate=SMALL,
        name="front",
    )(lengths, queries, new_kv, keys, values, residual, gain, routes, weights)


def in_vmem(array):
    return pltpu.with_memory_space_constraint(array, pltpu.VMEM)


def in_hbm(array):
    return pltpu.with_memory_space_constraint(array, pltpu.HBM)


def unpack_kernel(codes_ref, scales_hbm, out_ref, words_ref, scales_ref, sems, scales_sem):
    quarter, width = codes_ref.shape
    groups = quarter // GROUP
    step = 256 if width % 256 == 0 else LANES

    def fetch(group):
        rows = pl.ds(group * GROUP, GROUP)
        return pltpu.make_async_copy(codes_ref.at[rows, :], words_ref.at[rows, :], sems.at[group])

    scales_copy = pltpu.make_async_copy(scales_hbm, scales_ref, scales_sem)
    scales_copy.start()
    ahead = 3
    for group in range(min(ahead, groups)):
        fetch(group).start()
    scales_copy.wait()
    scales = scales_ref[...].astype(F32)
    for group in range(groups):
        if group + ahead < groups:
            fetch(group + ahead).start()
        fetch(group).wait()
        for column in range(0, width, step):
            spans = [
                jnp.broadcast_to(
                    scales[k * groups + group : k * groups + group + 1, column : column + step],
                    (16, step),
                ).astype(BF16)
                for k in range(4)
            ]

            def chunk(i, carry, group=group, column=column, spans=spans):
                start = pl.multiple_of(group * GROUP + i * 16, 16)
                words = words_ref[pl.ds(start, 16), column : column + step].astype(jnp.int32)
                words = (words ^ 0x8888).astype(jnp.int16)
                for k in range(4):
                    level = words if k == 3 else lax.shift_left(words, jnp.int16(12 - 4 * k))
                    level = lax.shift_right_arithmetic(level, jnp.int16(12))
                    out_ref[pl.ds(k * quarter + start, 16), column : column + step] = (
                        level.astype(BF16) * spans[k]
                    )
                return carry

            lax.fori_loop(0, GROUP // 16, chunk, 0, unroll=True)


def unpack_weights(codes, scales):
    quarter, width = codes.shape
    return pl.pallas_call(
        unpack_kernel,
        out_shape=pltpu.VMEM((4 * quarter, width), BF16),
        in_specs=[pl.BlockSpec(memory_space=pltpu.HBM)] * 2,
        out_specs=pl.BlockSpec(memory_space=pltpu.VMEM),
        scratch_shapes=[
            pltpu.VMEM((quarter, width), F32),
            pltpu.VMEM(scales.shape, BF16),
            pltpu.SemaphoreType.DMA((quarter // GROUP,)),
            pltpu.SemaphoreType.DMA,
        ],
        compiler_params=pltpu.CompilerParams(vmem_limit_bytes=VMEM_SOME),
        cost_estimate=SMALL,
        name="unpack_weights",
    )(in_hbm(codes), in_hbm(scales))


def hidden_kernel(place_ref, *refs):
    pieces, (gate_ref, up_ref, out_ref, share_ref, rows_ref) = refs[:-5], refs[-5:]
    depth, width = gate_ref.shape
    block = pieces[0].shape[0]
    for n, piece in enumerate(pieces):
        rows_ref[n * block : (n + 1) * block, :] = piece[:, :depth]
        table = piece[:, depth:].astype(F32)
        lane = lax.broadcasted_iota(jnp.int32, table.shape, 1)
        mine = place_ref[0]
        chosen = (lane == mine) | (lane == mine + LANES // 2)
        share = jnp.sum(jnp.where(chosen, table, 0.0), axis=1, keepdims=True)
        share_ref[n * block : (n + 1) * block, :] = jnp.broadcast_to(share, table.shape)
    step = 256
    for column in range(0, width, step):
        span = slice(column, column + step)
        gate = jnp.dot(rows_ref[...], gate_ref[:, span], preferred_element_type=F32)
        upward = jnp.dot(rows_ref[...], up_ref[:, span], preferred_element_type=F32)
        out_ref[:, span] = (gate / (1.0 + jnp.exp(-gate)) * upward).astype(BF16)


def hidden_units(pieces, w_gate, w_up, place):
    block, padded = pieces[0].shape
    count = block * len(pieces)
    depth, width = w_gate.shape
    vmem = pl.BlockSpec(memory_space=pltpu.VMEM)
    return pl.pallas_call(
        hidden_kernel,
        out_shape=(pltpu.VMEM((count, width), BF16), pltpu.VMEM((count, LANES), F32)),
        in_specs=[pl.BlockSpec(memory_space=pltpu.SMEM)] + [vmem] * (len(pieces) + 2),
        out_specs=(vmem, vmem),
        scratch_shapes=[pltpu.VMEM((count, depth), BF16)],
        compiler_params=pltpu.CompilerParams(vmem_limit_bytes=VMEM_SOME),
        cost_estimate=SMALL,
        name="gate_up",
    )(place, *pieces, in_vmem(w_gate), in_vmem(w_up))


def own_down_kernel(side_ref, hidden_ref, weight_ref, out_ref):
    half = hidden_ref.shape[1]
    rows = pl.ds(pl.multiple_of(side_ref[0] * half, half), half)
    step = 256
    for column in range(0, out_ref.shape[1], step):
        span = slice(column, column + step)
        out_ref[:, span] = jnp.dot(
            hidden_ref[...], weight_ref[rows, span], preferred_element_type=F32
        )


def own_down(side, hidden, weight):
    count, half = hidden.shape
    width = weight.shape[1]
    vmem = pl.BlockSpec(memory_space=pltpu.VMEM)
    return pl.pallas_call(
        own_down_kernel,
        out_shape=pltpu.VMEM((count, width), F32),
        in_specs=[pl.BlockSpec(memory_space=pltpu.SMEM), vmem, vmem],
        out_specs=vmem,
        compiler_params=pltpu.CompilerParams(vmem_limit_bytes=VMEM_SOME),
        cost_estimate=SMALL,
        name="down_own",
    )(side, in_vmem(hidden), in_vmem(weight))


def peer_down_kernel(
    side_ref, partial_ref, hidden_ref, weight_ref, share_ref, keep_ref, send_ref
):
    count, half = hidden_ref.shape
    rows = pl.ds(pl.multiple_of((1 - side_ref[0]) * half, half), half)
    step = 256
    for column in range(0, keep_ref.shape[1], step):
        span = slice(column, column + step)
        produced = partial_ref[:, span] + jnp.dot(
            hidden_ref[...], weight_ref[rows, span], preferred_element_type=F32
        )
        result = (produced.astype(BF16).astype(F32) * share_ref[:, :1]).astype(BF16)
        keep_ref[:, span] = result[: count // 2]
        send_ref[:, span] = result[count // 2 :]


def peer_down(side, partial, hidden, weight, share):
    count, width = partial.shape
    half = hidden.shape[1]
    shape = pltpu.VMEM((count // 2, width), BF16)
    vmem = pl.BlockSpec(memory_space=pltpu.VMEM)
    return pl.pallas_call(
        peer_down_kernel,
        out_shape=(shape, shape),
        in_specs=[pl.BlockSpec(memory_space=pltpu.SMEM)] + [vmem] * 4,
        out_specs=(vmem, vmem),
        compiler_params=pltpu.CompilerParams(vmem_limit_bytes=VMEM_SOME),
        cost_estimate=SMALL,
        name="down_peer",
    )(side, in_vmem(partial), hidden, in_vmem(weight), in_vmem(share))


def halve_kernel(terms, *refs):
    term_refs, out_refs = refs[:terms], refs[terms:]
    total = term_refs[0][...].astype(F32)
    for term_ref in term_refs[1:]:
        total = total + term_ref[...].astype(F32)
    size = total.shape[0] // len(out_refs)
    for n, out_ref in enumerate(out_refs):
        out_ref[...] = total[n * size : (n + 1) * size].astype(out_ref.dtype)


def add_and_cut(kept, arrived, parts):
    count, width = kept[0].shape
    vmem = pl.BlockSpec(memory_space=pltpu.VMEM)
    shape = pltpu.VMEM((count // parts, width), BF16)
    return pl.pallas_call(
        functools.partial(halve_kernel, len(kept + arrived)),
        out_shape=(shape,) * parts,
        in_specs=[vmem] * len(kept + arrived),
        out_specs=(vmem,) * parts,
        compiler_params=pltpu.CompilerParams(vmem_limit_bytes=VMEM_SOME),
        cost_estimate=SMALL,
        name="add_and_cut",
    )(*[in_vmem(part) for part in kept], *arrived)


def finish_kernel(side_ref, mixed_ref, far_ref, *refs):
    near_refs, out_ref = refs[:-1], refs[-1]
    half = far_ref.shape[1]
    near = near_refs[0][...].astype(F32)
    for near_ref in near_refs[1:]:
        near = near + near_ref[...].astype(F32)
    far = far_ref[...].astype(F32)
    first = side_ref[0] == 0
    for n, part in enumerate((jnp.where(first, near, far), jnp.where(first, far, near))):
        span = slice(n * half, (n + 1) * half)
        out_ref[:, span] = (mixed_ref[:, span].astype(F32) + part).astype(BF16)


def finish(side, mixed, far, near):
    vmem = pl.BlockSpec(memory_space=pltpu.VMEM)
    return pl.pallas_call(
        finish_kernel,
        out_shape=jax.ShapeDtypeStruct(mixed.shape, BF16),
        in_specs=[pl.BlockSpec(memory_space=pltpu.SMEM)] + [vmem] * (2 + len(near)),
        out_specs=vmem,
        compiler_params=pltpu.CompilerParams(vmem_limit_bytes=VMEM_SOME),
        name="finish",
    )(side, mixed, far, *near)


def dense(payload, mixed, codes):
    gate_codes, gate_scales, up_codes, up_scales, down_codes, down_scales = codes
    groups = lax.axis_size("dp")
    experts = lax.axis_size("expert")
    devices = groups * experts
    core, line, layer, plane = 1, 2, 4, experts
    layers = experts // layer
    side = lax.axis_index("dp").reshape(1).astype(jnp.int32)
    place = lax.axis_index("expert").reshape(1).astype(jnp.int32)

    def swap(block, offset):
        return lax.ppermute(block, ("dp", "expert"), [(i, i ^ offset) for i in range(devices)])

    side, place, gate_scales, payload = lax.optimization_barrier(
        (side, place, gate_scales, payload)
    )
    blocks = [swap(payload, z * layer) for z in range(1, layers)]
    w_gate = unpack_weights(gate_codes, gate_scales)
    blocks, w_gate = lax.optimization_barrier((blocks, w_gate))
    stack = jnp.concatenate([payload] + blocks, axis=0)
    up_scales, stack = lax.optimization_barrier((up_scales, stack))
    beside, above, stack_pair = swap(stack, plane), swap(stack, line), swap(stack, core)
    w_up = unpack_weights(up_codes, up_scales)
    above, w_up = lax.optimization_barrier((above, w_up))
    across, above_pair = swap(above, plane), swap(above, core)
    above_pair, beside = lax.optimization_barrier((above_pair, beside))
    beside_pair = swap(beside, core)
    hidden_own, share_own = hidden_units(
        [stack, above, stack_pair, above_pair], w_gate, w_up, place
    )
    other_peer = swap(hidden_own, plane)
    down_scales, hidden_own = lax.optimization_barrier((down_scales, hidden_own))
    w_down = unpack_weights(down_codes, down_scales)
    across, w_down = lax.optimization_barrier((across, w_down))
    hidden_other, share_other = hidden_units(
        [beside, across, beside_pair, swap(across, core)], w_gate, w_up, place
    )
    own_peer = swap(hidden_other, plane)

    def over_core(keep, send):
        return add_and_cut([keep], [swap(send, core)], 2)

    def over_expert(keep, send):
        parts = add_and_cut([keep], [swap(send, line)], layers)
        return [parts[0]] + [swap(parts[z], z * layer) for z in range(1, layers)]

    partial_other = own_down(side, hidden_other, w_down)
    partial_own = own_down(side, hidden_own, w_down)
    keep_other, send_other = peer_down(side, partial_other, other_peer, w_down, share_other)
    send_other, partial_own, own_peer = lax.optimization_barrier(
        (send_other, partial_own, own_peer)
    )
    keep_own, send_own = peer_down(side, partial_own, own_peer, w_down, share_own)
    parts = over_expert(*over_core(keep_other, send_other))
    near = over_expert(*over_core(keep_own, send_own))
    (far,) = add_and_cut(parts[:1], parts[1:], 1)
    return finish(side, mixed, swap(far, plane), near)


def slot_table(routes, experts, capacity):
    flattened = routes.reshape(-1)
    onehot = (flattened[:, None] == jnp.arange(experts, dtype=jnp.int32)[None, :]).astype(jnp.int32)
    ranking = jnp.sum((jnp.cumsum(onehot, axis=0) - 1) * onehot, axis=1)
    return (flattened * capacity + ranking).reshape(routes.shape)


def dispatch(block, slots, width):
    targets = jnp.arange(width, dtype=jnp.int32)
    placing = jnp.sum((slots[None, :, :] == targets[:, None, None]).astype(F32), axis=2)
    return jnp.dot(placing.astype(BF16), block, preferred_element_type=F32).astype(BF16)


def unpack(codes, scales):
    quarter, width = codes.shape
    divisors = jnp.array([1.0, 1.0 / 16, 1.0 / 256, 1.0 / 4096], F32)[:, None, None]
    lifted = jnp.floor(codes[None, :, :] * divisors)
    levels = lifted - 16.0 * jnp.floor(lifted * (1.0 / 16)) - 8.0
    height = 4 * quarter
    grouped = levels.reshape(height // GROUP, GROUP, width) * scales.astype(F32)[:, None, :]
    return grouped.reshape(height, width).astype(BF16)


def routed(normed, mixed, routes, route_weights, codes, capacity):
    gate_codes, gate_scales, up_codes, up_scales, down_codes, down_scales = codes
    experts = lax.axis_size("expert")
    groups = lax.axis_size("dp")
    row_count, width = mixed.shape
    own_slots = slot_table(routes, experts, capacity)
    w_gate = unpack(gate_codes, gate_scales)
    w_up = unpack(up_codes, up_scales)
    w_down = unpack(down_codes, down_scales)
    local_units = w_gate.shape[1]
    peer_rows = lax.all_gather(normed, "dp", axis=0, tiled=True).reshape(groups, row_count, width)
    peer_routes = lax.all_gather(routes, "dp", axis=0, tiled=True).reshape(groups, row_count, TOP)

    def build(block, table):
        return dispatch(block, slot_table(table, experts, capacity), experts * capacity)

    outgoing = jax.vmap(build)(peer_rows, peer_routes).reshape(groups, experts, capacity, width)
    items = lax.all_to_all(outgoing, "expert", split_axis=1, concat_axis=1, tiled=True)
    inputs = items.reshape(-1, width)
    gate = jnp.dot(inputs, w_gate, preferred_element_type=F32)
    upward = jnp.dot(inputs, w_up, preferred_element_type=F32)
    hidden = (jax.nn.silu(gate) * upward).astype(BF16).reshape(-1, local_units)
    produced = jnp.dot(
        lax.all_gather(hidden, "dp", axis=1, tiled=True), w_down, preferred_element_type=F32
    ).astype(BF16)
    produced = produced.reshape(groups, -1, produced.shape[1])
    returned = lax.all_to_all(
        lax.all_to_all(produced, "dp", split_axis=0, concat_axis=2, tiled=True),
        "expert",
        split_axis=1,
        concat_axis=0,
        tiled=True,
    )
    shares = route_weights / jnp.sum(route_weights, axis=1, keepdims=True)
    targets = jnp.arange(experts * capacity, dtype=jnp.int32)
    spreading = jnp.sum(
        jnp.where(own_slots[:, :, None] == targets[None, None, :], shares[:, :, None], 0.0), axis=1
    )
    combined = jnp.dot(
        spreading, returned.reshape(-1, width).astype(F32), precision=lax.Precision.HIGHEST
    )
    return (mixed.astype(F32) + combined).astype(BF16)


def body(
    queries,
    new_kv,
    cache_keys,
    cache_values,
    lengths,
    residual,
    norm_gain,
    routes,
    route_weights,
    *packed,
):
    experts = lax.axis_size("expert")
    groups = lax.axis_size("dp")
    row_count = queries.shape[0]
    capacity = min(row_count, max(2, 2 * row_count * TOP // experts))
    every = (
        capacity == row_count
        and groups == 2
        and experts <= LANES // 2
        and experts % 4 == 0
        and experts & (experts - 1) == 0
    )
    mixed, payload = front(
        queries,
        new_kv,
        cache_keys,
        cache_values,
        lengths,
        residual,
        norm_gain,
        routes,
        route_weights,
        LANES if every else 0,
    )
    codes = [array[0] for array in packed]
    if every:
        return dense(payload, mixed, codes)
    return routed(payload, mixed, routes, route_weights, codes, capacity)


def solution(mesh):
    return jax.shard_map(
        body,
        mesh=mesh,
        in_specs=(
            P(("dp", "expert"), None),
            P(("dp", "expert"), None, None),
            P(("dp", "expert"), None, None),
            P(("dp", "expert"), None, None),
            P(("dp", "expert")),
            P(("dp", "expert"), None),
            P(),
            P(("dp", "expert"), None),
            P(("dp", "expert"), None),
            P("expert", None, "dp"),
            P("expert", None, "dp"),
            P("expert", None, "dp"),
            P("expert", None, "dp"),
            P("expert", None, "dp"),
            P("expert", None, "dp"),
        ),
        out_specs=P(("dp", "expert"), None),
        check_vma=False,
    )
```

```python
import functools

import jax
import jax.numpy as jnp
from jax import lax
from jax.experimental import pallas as pl
from jax.experimental.pallas import tpu as pltpu
from jax.sharding import PartitionSpec as P

HEAD_DIM = 128
GROUP = 128
TOP = 8
LANES = 128
VMEM_LIMIT = 56 * 2**20
VMEM_SOME = 16 * 2**20
SPARE = 16
SMALL = pl.CostEstimate(flops=1, bytes_accessed=1, transcendentals=0)
F32 = jnp.float32
BF16 = jnp.bfloat16


def front_kernel(
    lengths_ref,
    queries_ref,
    new_kv_ref,
    keys_ref,
    values_ref,
    residual_ref,
    gain_ref,
    routes_ref,
    weights_ref,
    mixed_ref,
    payload_ref,
):
    rows, cache, kv_width = keys_ref.shape
    width = queries_ref.shape[1]
    kv_heads = kv_width // HEAD_DIM
    per = width // kv_width
    scaling = HEAD_DIM ** (-0.5)
    row_id = lax.broadcasted_iota(jnp.int32, (rows, rows * cache), 0)
    lane_id = lax.broadcasted_iota(jnp.int32, (rows, rows * cache), 1)
    bound = jnp.zeros((rows, rows * cache), jnp.int32)
    for r in range(rows):
        bound = jnp.where(row_id == r, r * cache + lengths_ref[r], bound)
    valid = (lane_id >= row_id * cache) & (lane_id < bound)
    earlier, current = [], []
    for j in range(kv_heads):
        span = slice(j * HEAD_DIM, (j + 1) * HEAD_DIM)
        heads = range(j * per, (j + 1) * per)
        queried = jnp.concatenate(
            [queries_ref[:, h * HEAD_DIM : (h + 1) * HEAD_DIM].astype(F32) for h in heads], axis=0
        )
        keys = keys_ref[:, :, span].reshape(rows * cache, HEAD_DIM)
        earlier.append(
            lax.dot_general(
                queried.astype(BF16), keys, (((1,), (1,)), ((), ())), preferred_element_type=F32
            )
        )
        fresh_key = new_kv_ref[:, 0, span].astype(F32)
        current.append(queried.reshape(per, rows, HEAD_DIM) * fresh_key[None])
    earlier = jnp.concatenate(earlier, axis=0).reshape(kv_heads * per, rows, rows * cache)
    earlier = jnp.where(valid[None], earlier * scaling, -1e30)
    current = jnp.sum(jnp.concatenate(current, axis=0), axis=-1, keepdims=True) * scaling
    largest = jnp.maximum(jnp.max(earlier, axis=-1, keepdims=True), current)
    earlier_w = jnp.where(valid[None], jnp.exp(earlier - largest), 0.0)
    current_w = jnp.exp(current - largest)
    inverse = 1.0 / (jnp.sum(earlier_w, axis=-1, keepdims=True) + current_w)
    earlier_p = (earlier_w * inverse).astype(BF16).reshape(kv_heads * per * rows, rows * cache)
    current_p = (current_w * inverse).astype(BF16).astype(F32)
    total = jnp.zeros((rows, HEAD_DIM), F32)
    for j in range(kv_heads):
        span = slice(j * HEAD_DIM, (j + 1) * HEAD_DIM)
        values = values_ref[:, :, span].reshape(rows * cache, HEAD_DIM)
        fresh_value = new_kv_ref[:, 1, span].astype(F32)
        attended = jnp.dot(
            earlier_p[j * per * rows : (j + 1) * per * rows], values, preferred_element_type=F32
        )
        attended = attended.reshape(per, rows, HEAD_DIM)
        attended = attended + current_p[j * per : (j + 1) * per] * fresh_value[None]
        for g in range(per):
            h = j * per + g
            place = slice(h * HEAD_DIM, (h + 1) * HEAD_DIM)
            mixed = (
                residual_ref[:, place].astype(F32) + attended[g].astype(BF16).astype(F32)
            ).astype(BF16)
            mixed_ref[:, place] = mixed
            widened = mixed.astype(F32)
            total = total + widened * widened
    meansq = jnp.sum(total, axis=-1, keepdims=True) * (1.0 / width)
    inverse = lax.rsqrt(meansq + 1e-06)
    payload_ref[:, :width] = (
        mixed_ref[...].astype(F32) * inverse * gain_ref[...].astype(F32).reshape(1, width)
    ).astype(BF16)
    if payload_ref.shape[1] > width:
        shares = weights_ref[...] / jnp.sum(weights_ref[...], axis=1, keepdims=True)
        lane = lax.broadcasted_iota(jnp.int32, (rows, LANES), 1)
        expert = jnp.where(lane < LANES // 2, lane, lane - LANES // 2)
        table = jnp.zeros((rows, LANES), F32)
        for k in range(routes_ref.shape[1]):
            table = table + jnp.where(
                routes_ref[:, k : k + 1] == expert, shares[:, k : k + 1], 0.0
            )
        high = table.astype(BF16).astype(F32)
        payload_ref[:, width:] = jnp.where(lane < LANES // 2, high, table - high).astype(BF16)


def front(queries, new_kv, keys, values, lengths, residual, gain, routes, weights, extra):
    rows, width = queries.shape
    vmem = pl.BlockSpec(memory_space=pltpu.VMEM)
    return pl.pallas_call(
        front_kernel,
        out_shape=(
            jax.ShapeDtypeStruct((rows, width), BF16),
            jax.ShapeDtypeStruct((rows, width + extra), BF16),
        ),
        in_specs=[pl.BlockSpec(memory_space=pltpu.SMEM)] + [vmem] * 8,
        out_specs=(vmem, vmem),
        compiler_params=pltpu.CompilerParams(vmem_limit_bytes=VMEM_LIMIT),
        cost_estimate=SMALL,
        name="front",
    )(lengths, queries, new_kv, keys, values, residual, gain, routes, weights)


def in_vmem(array):
    return pltpu.with_memory_space_constraint(array, pltpu.VMEM)


def in_hbm(array):
    return pltpu.with_memory_space_constraint(array, pltpu.HBM)


def unpack_kernel(codes_ref, scales_hbm, out_ref, words_ref, scales_ref, sems, scales_sem):
    quarter, width = codes_ref.shape
    groups = quarter // GROUP
    step = 256 if width % 256 == 0 else LANES

    def fetch(group):
        rows = pl.ds(group * GROUP, GROUP)
        return pltpu.make_async_copy(codes_ref.at[rows, :], words_ref.at[rows, :], sems.at[group])

    scales_copy = pltpu.make_async_copy(scales_hbm, scales_ref, scales_sem)
    scales_copy.start()
    ahead = 3
    for group in range(min(ahead, groups)):
        fetch(group).start()
    scales_copy.wait()
    scales = scales_ref[...].astype(F32)
    for group in range(groups):
        if group + ahead < groups:
            fetch(group + ahead).start()
        fetch(group).wait()
        for column in range(0, width, step):
            spans = [
                jnp.broadcast_to(
                    scales[k * groups + group : k * groups + group + 1, column : column + step],
                    (16, step),
                ).astype(BF16)
                for k in range(4)
            ]

            def chunk(i, carry, group=group, column=column, spans=spans):
                start = pl.multiple_of(group * GROUP + i * 16, 16)
                words = words_ref[pl.ds(start, 16), column : column + step].astype(jnp.int32)
                for k in range(4):
                    digit = words if k == 0 else lax.shift_right_logical(words, 4 * k)
                    if k < 3:
                        digit = digit & 15
                    level = digit.astype(F32).astype(BF16) - jnp.asarray(8, BF16)
                    out_ref[pl.ds(k * quarter + start, 16), column : column + step] = (
                        level * spans[k]
                    )
                return carry

            lax.fori_loop(0, GROUP // 16, chunk, 0, unroll=True)


def unpack_weights(codes, scales):
    quarter, width = codes.shape
    return pl.pallas_call(
        unpack_kernel,
        out_shape=pltpu.VMEM((4 * quarter, width), BF16),
        in_specs=[pl.BlockSpec(memory_space=pltpu.HBM)] * 2,
        out_specs=pl.BlockSpec(memory_space=pltpu.VMEM),
        scratch_shapes=[
            pltpu.VMEM((quarter, width), F32),
            pltpu.VMEM(scales.shape, BF16),
            pltpu.SemaphoreType.DMA((quarter // GROUP,)),
            pltpu.SemaphoreType.DMA,
        ],
        compiler_params=pltpu.CompilerParams(vmem_limit_bytes=VMEM_SOME),
        cost_estimate=SMALL,
        name="unpack_weights",
    )(in_hbm(codes), in_hbm(scales))


def hidden_kernel(place_ref, *refs):
    pieces, (gate_ref, up_ref, out_ref, share_ref, rows_ref) = refs[:-5], refs[-5:]
    depth, width = gate_ref.shape
    block = pieces[0].shape[0]
    count = block * len(pieces)
    for n, piece in enumerate(pieces):
        rows_ref[n * block : (n + 1) * block, :] = piece[:, :depth]
        table = piece[:, depth:].astype(F32)
        lane = lax.broadcasted_iota(jnp.int32, table.shape, 1)
        mine = place_ref[0]
        chosen = (lane == mine) | (lane == mine + LANES // 2)
        share = jnp.sum(jnp.where(chosen, table, 0.0), axis=1, keepdims=True)
        share_ref[n * block : (n + 1) * block, :] = jnp.broadcast_to(share, table.shape)
    step = 256
    for column in range(0, width, step):
        span = slice(column, column + step)
        gate = jnp.dot(rows_ref[...], gate_ref[:, span], preferred_element_type=F32)
        upward = jnp.dot(rows_ref[...], up_ref[:, span], preferred_element_type=F32)
        out_ref[:count, span] = (gate / (1.0 + jnp.exp(-gate)) * upward).astype(BF16)
    if out_ref.shape[0] > count:
        out_ref[count:, :] = jnp.zeros((out_ref.shape[0] - count, width), BF16)


def hidden_units(pieces, w_gate, w_up, place, spare=0):
    block, padded = pieces[0].shape
    count = block * len(pieces)
    depth, width = w_gate.shape
    vmem = pl.BlockSpec(memory_space=pltpu.VMEM)
    return pl.pallas_call(
        hidden_kernel,
        out_shape=(pltpu.VMEM((count + spare, width), BF16), pltpu.VMEM((count, LANES), F32)),
        in_specs=[pl.BlockSpec(memory_space=pltpu.SMEM)] + [vmem] * (len(pieces) + 2),
        out_specs=(vmem, vmem),
        scratch_shapes=[pltpu.VMEM((count, depth), BF16)],
        compiler_params=pltpu.CompilerParams(vmem_limit_bytes=VMEM_SOME),
        cost_estimate=SMALL,
        name="gate_up",
    )(place, *pieces, in_vmem(w_gate), in_vmem(w_up))


def own_down_kernel(side_ref, hidden_ref, weight_ref, out_ref):
    half = hidden_ref.shape[1]
    rows = pl.ds(pl.multiple_of(side_ref[0] * half, half), half)
    step = 256
    for column in range(0, out_ref.shape[1], step):
        span = slice(column, column + step)
        out_ref[:, span] = jnp.dot(
            hidden_ref[: out_ref.shape[0]], weight_ref[rows, span], preferred_element_type=F32
        )


def own_down(side, hidden, weight, count):
    half = hidden.shape[1]
    width = weight.shape[1]
    vmem = pl.BlockSpec(memory_space=pltpu.VMEM)
    return pl.pallas_call(
        own_down_kernel,
        out_shape=pltpu.VMEM((count, width), F32),
        in_specs=[pl.BlockSpec(memory_space=pltpu.SMEM), vmem, vmem],
        out_specs=vmem,
        compiler_params=pltpu.CompilerParams(vmem_limit_bytes=VMEM_SOME),
        cost_estimate=SMALL,
        name="down_own",
    )(side, in_vmem(hidden), in_vmem(weight))


def peer_down_kernel(side_ref, partial_ref, hidden_ref, weight_ref, share_ref, *out_refs):
    count, half = partial_ref.shape[0], hidden_ref.shape[1]
    rows = pl.ds(pl.multiple_of((1 - side_ref[0]) * half, half), half)
    step = 256
    cut = count // len(out_refs)
    for column in range(0, partial_ref.shape[1], step):
        span = slice(column, column + step)
        produced = partial_ref[:, span] + jnp.dot(
            hidden_ref[:count], weight_ref[rows, span], preferred_element_type=F32
        )
        result = (produced.astype(BF16).astype(F32) * share_ref[:, :1]).astype(BF16)
        for n, out_ref in enumerate(out_refs):
            out_ref[:, span] = result[n * cut : (n + 1) * cut]


def peer_down(side, partial, hidden, weight, share, parts):
    count, width = partial.shape
    vmem = pl.BlockSpec(memory_space=pltpu.VMEM)
    return pl.pallas_call(
        peer_down_kernel,
        out_shape=(pltpu.VMEM((count // parts, width), BF16),) * parts,
        in_specs=[pl.BlockSpec(memory_space=pltpu.SMEM)] + [vmem] * 4,
        out_specs=(vmem,) * parts,
        compiler_params=pltpu.CompilerParams(vmem_limit_bytes=VMEM_SOME),
        cost_estimate=SMALL,
        name="down_peer",
    )(side, in_vmem(partial), hidden, in_vmem(weight), in_vmem(share))


def halve_kernel(terms, *refs):
    term_refs, out_refs = refs[:terms], refs[terms:]
    total = term_refs[0][...].astype(F32)
    for term_ref in term_refs[1:]:
        total = total + term_ref[...].astype(F32)
    size = total.shape[0] // len(out_refs)
    for n, out_ref in enumerate(out_refs):
        out_ref[...] = total[n * size : (n + 1) * size].astype(out_ref.dtype)


def add_and_cut(kept, arrived, parts):
    count, width = kept[0].shape
    vmem = pl.BlockSpec(memory_space=pltpu.VMEM)
    shape = pltpu.VMEM((count // parts, width), BF16)
    return pl.pallas_call(
        functools.partial(halve_kernel, len(kept + arrived)),
        out_shape=(shape,) * parts,
        in_specs=[vmem] * len(kept + arrived),
        out_specs=(vmem,) * parts,
        compiler_params=pltpu.CompilerParams(vmem_limit_bytes=VMEM_SOME),
        cost_estimate=SMALL,
        name="add_and_cut",
    )(*[in_vmem(part) for part in kept], *arrived)


def join_kernel(parts, far_ref, *refs):
    near_refs, out_refs = refs[:-parts], refs[-parts:]
    size = far_ref.shape[0] // parts
    near = near_refs[0][...].astype(F32)
    for near_ref in near_refs[1:]:
        near = near + near_ref[...].astype(F32)
    far = far_ref[...].astype(F32)
    for n, out_ref in enumerate(out_refs):
        rows = slice(n * size, (n + 1) * size)
        out_ref[...] = jnp.concatenate([near[rows], far[rows]], axis=0).astype(BF16)


def join(near, far, parts):
    count, width = far.shape
    vmem = pl.BlockSpec(memory_space=pltpu.VMEM)
    return pl.pallas_call(
        functools.partial(join_kernel, parts),
        out_shape=(pltpu.VMEM((2 * count // parts, width), BF16),) * parts,
        in_specs=[vmem] * (1 + len(near)),
        out_specs=(vmem,) * parts,
        compiler_params=pltpu.CompilerParams(vmem_limit_bytes=VMEM_SOME),
        cost_estimate=SMALL,
        name="join",
    )(far, *near)


def finish_kernel(side_ref, mixed_ref, *refs):
    block_refs, out_ref = refs[:-1], refs[-1]
    rows, width = mixed_ref.shape
    total = block_refs[0][...].astype(F32)
    for block_ref in block_refs[1:]:
        total = total + block_ref[...].astype(F32)
    near, far = total[:rows], total[rows:]
    first = side_ref[0] == 0
    half = width // 2
    for n, part in enumerate((jnp.where(first, near, far), jnp.where(first, far, near))):
        span = slice(n * half, (n + 1) * half)
        out_ref[:, span] = (mixed_ref[:, span].astype(F32) + part).astype(BF16)


def finish(side, mixed, blocks):
    vmem = pl.BlockSpec(memory_space=pltpu.VMEM)
    return pl.pallas_call(
        finish_kernel,
        out_shape=jax.ShapeDtypeStruct(mixed.shape, BF16),
        in_specs=[pl.BlockSpec(memory_space=pltpu.SMEM)] + [vmem] * (1 + len(blocks)),
        out_specs=vmem,
        compiler_params=pltpu.CompilerParams(vmem_limit_bytes=VMEM_SOME),
        name="finish",
    )(side, mixed, *blocks)


def dense(payload, mixed, codes):
    gate_codes, gate_scales, up_codes, up_scales, down_codes, down_scales = codes
    groups = lax.axis_size("dp")
    experts = lax.axis_size("expert")
    devices = groups * experts
    core, line, layer, plane = 1, 2, 4, experts
    layers = experts // layer
    side = lax.axis_index("dp").reshape(1).astype(jnp.int32)
    place = lax.axis_index("expert").reshape(1).astype(jnp.int32)

    def swap(block, offset):
        return lax.ppermute(block, ("dp", "expert"), [(i, i ^ offset) for i in range(devices)])

    side, place, gate_scales, payload = lax.optimization_barrier(
        (side, place, gate_scales, payload)
    )
    blocks = [swap(payload, z * layer) for z in range(1, layers)]
    w_gate = unpack_weights(gate_codes, gate_scales)
    blocks, w_gate = lax.optimization_barrier((blocks, w_gate))
    stack = jnp.concatenate([payload] + blocks, axis=0)
    up_scales, stack = lax.optimization_barrier((up_scales, stack))
    beside, above, stack_pair = swap(stack, plane), swap(stack, line), swap(stack, core)
    w_up = unpack_weights(up_codes, up_scales)
    above, stack_pair, w_up = lax.optimization_barrier((above, stack_pair, w_up))
    across, above_pair = swap(above, plane), swap(above, core)
    above_pair, beside = lax.optimization_barrier((above_pair, beside))
    beside_pair = swap(beside, core)
    hidden_own, share_own = hidden_units(
        [stack, stack_pair, above, above_pair], w_gate, w_up, place, SPARE
    )
    other_peer = swap(hidden_own, plane)
    down_scales, hidden_own = lax.optimization_barrier((down_scales, hidden_own))
    w_down = unpack_weights(down_codes, down_scales)
    across, w_down = lax.optimization_barrier((across, w_down))
    hidden_other, share_other = hidden_units(
        [beside, beside_pair, across, swap(across, core)], w_gate, w_up, place
    )
    own_peer = swap(hidden_other, plane)

    count = share_own.shape[0]
    partial_other = own_down(side, hidden_other, w_down, count)
    partial_own = own_down(side, hidden_own, w_down, count)
    keep, send = peer_down(side, partial_other, other_peer, w_down, share_other, 2)
    keep, send = add_and_cut([keep], [swap(send, line)], 2)
    (onward,) = add_and_cut([keep], [swap(send, core)], 1)
    far = swap(onward, plane)
    keep_near, send_near, keep_far, send_far = peer_down(
        side, partial_own, own_peer, w_down, share_own, 4
    )
    (onward,) = add_and_cut([keep_far], [swap(send_far, core)], 1)
    near = [in_vmem(keep_near), swap(send_near, core), swap(onward, line)]
    blocks = join(near, far, layers)
    blocks = [blocks[0]] + [swap(blocks[z], z * layer) for z in range(1, layers)]
    return finish(side, mixed, blocks)


def slot_table(routes, experts, capacity):
    flattened = routes.reshape(-1)
    onehot = (flattened[:, None] == jnp.arange(experts, dtype=jnp.int32)[None, :]).astype(jnp.int32)
    ranking = jnp.sum((jnp.cumsum(onehot, axis=0) - 1) * onehot, axis=1)
    return (flattened * capacity + ranking).reshape(routes.shape)


def dispatch(block, slots, width):
    targets = jnp.arange(width, dtype=jnp.int32)
    placing = jnp.sum((slots[None, :, :] == targets[:, None, None]).astype(F32), axis=2)
    return jnp.dot(placing.astype(BF16), block, preferred_element_type=F32).astype(BF16)


def unpack(codes, scales):
    quarter, width = codes.shape
    divisors = jnp.array([1.0, 1.0 / 16, 1.0 / 256, 1.0 / 4096], F32)[:, None, None]
    lifted = jnp.floor(codes[None, :, :] * divisors)
    levels = lifted - 16.0 * jnp.floor(lifted * (1.0 / 16)) - 8.0
    height = 4 * quarter
    grouped = levels.reshape(height // GROUP, GROUP, width) * scales.astype(F32)[:, None, :]
    return grouped.reshape(height, width).astype(BF16)


def routed(normed, mixed, routes, route_weights, codes, capacity):
    gate_codes, gate_scales, up_codes, up_scales, down_codes, down_scales = codes
    experts = lax.axis_size("expert")
    groups = lax.axis_size("dp")
    row_count, width = mixed.shape
    own_slots = slot_table(routes, experts, capacity)
    w_gate = unpack(gate_codes, gate_scales)
    w_up = unpack(up_codes, up_scales)
    w_down = unpack(down_codes, down_scales)
    local_units = w_gate.shape[1]
    peer_rows = lax.all_gather(normed, "dp", axis=0, tiled=True).reshape(groups, row_count, width)
    peer_routes = lax.all_gather(routes, "dp", axis=0, tiled=True).reshape(groups, row_count, TOP)

    def build(block, table):
        return dispatch(block, slot_table(table, experts, capacity), experts * capacity)

    outgoing = jax.vmap(build)(peer_rows, peer_routes).reshape(groups, experts, capacity, width)
    items = lax.all_to_all(outgoing, "expert", split_axis=1, concat_axis=1, tiled=True)
    inputs = items.reshape(-1, width)
    gate = jnp.dot(inputs, w_gate, preferred_element_type=F32)
    upward = jnp.dot(inputs, w_up, preferred_element_type=F32)
    hidden = (jax.nn.silu(gate) * upward).astype(BF16).reshape(-1, local_units)
    produced = jnp.dot(
        lax.all_gather(hidden, "dp", axis=1, tiled=True), w_down, preferred_element_type=F32
    ).astype(BF16)
    produced = produced.reshape(groups, -1, produced.shape[1])
    returned = lax.all_to_all(
        lax.all_to_all(produced, "dp", split_axis=0, concat_axis=2, tiled=True),
        "expert",
        split_axis=1,
        concat_axis=0,
        tiled=True,
    )
    shares = route_weights / jnp.sum(route_weights, axis=1, keepdims=True)
    targets = jnp.arange(experts * capacity, dtype=jnp.int32)
    spreading = jnp.sum(
        jnp.where(own_slots[:, :, None] == targets[None, None, :], shares[:, :, None], 0.0), axis=1
    )
    combined = jnp.dot(
        spreading, returned.reshape(-1, width).astype(F32), precision=lax.Precision.HIGHEST
    )
    return (mixed.astype(F32) + combined).astype(BF16)


def body(
    queries,
    new_kv,
    cache_keys,
    cache_values,
    lengths,
    residual,
    norm_gain,
    routes,
    route_weights,
    *packed,
):
    experts = lax.axis_size("expert")
    groups = lax.axis_size("dp")
    row_count = queries.shape[0]
    capacity = min(row_count, max(2, 2 * row_count * TOP // experts))
    every = (
        capacity == row_count
        and groups == 2
        and experts <= LANES // 2
        and experts % 4 == 0
        and experts & (experts - 1) == 0
    )
    mixed, payload = front(
        queries,
        new_kv,
        cache_keys,
        cache_values,
        lengths,
        residual,
        norm_gain,
        routes,
        route_weights,
        LANES if every else 0,
    )
    codes = [array[0] for array in packed]
    if every:
        return dense(payload, mixed, codes)
    return routed(payload, mixed, routes, route_weights, codes, capacity)


def solution(mesh):
    return jax.shard_map(
        body,
        mesh=mesh,
        in_specs=(
            P(("dp", "expert"), None),
            P(("dp", "expert"), None, None),
            P(("dp", "expert"), None, None),
            P(("dp", "expert"), None, None),
            P(("dp", "expert")),
            P(("dp", "expert"), None),
            P(),
            P(("dp", "expert"), None),
            P(("dp", "expert"), None),
            P("expert", None, "dp"),
            P("expert", None, "dp"),
            P("expert", None, "dp"),
            P("expert", None, "dp"),
            P("expert", None, "dp"),
            P("expert", None, "dp"),
        ),
        out_specs=P(("dp", "expert"), None),
        check_vma=False,
    )
```

```python
import functools

import jax
import jax.numpy as jnp
from jax import lax
from jax.experimental import pallas as pl
from jax.experimental.pallas import tpu as pltpu
from jax.sharding import PartitionSpec as P

HEAD_DIM = 128
GROUP = 128
TOP = 8
LANES = 128
VMEM_LIMIT = 56 * 2**20
VMEM_SOME = 16 * 2**20
VMEM_MORE = 24 * 2**20
SPARE = 16
SMALL = pl.CostEstimate(flops=1, bytes_accessed=1, transcendentals=0)
F32 = jnp.float32
BF16 = jnp.bfloat16


def front_kernel(
    lengths_ref,
    queries_ref,
    new_kv_ref,
    keys_ref,
    values_ref,
    residual_ref,
    gain_ref,
    routes_ref,
    weights_ref,
    mixed_ref,
    payload_ref,
):
    rows, cache, kv_width = keys_ref.shape
    width = queries_ref.shape[1]
    kv_heads = kv_width // HEAD_DIM
    per = width // kv_width
    scaling = HEAD_DIM ** (-0.5)
    row_id = lax.broadcasted_iota(jnp.int32, (rows, rows * cache), 0)
    lane_id = lax.broadcasted_iota(jnp.int32, (rows, rows * cache), 1)
    bound = jnp.zeros((rows, rows * cache), jnp.int32)
    for r in range(rows):
        bound = jnp.where(row_id == r, r * cache + lengths_ref[r], bound)
    valid = (lane_id >= row_id * cache) & (lane_id < bound)
    earlier, current = [], []
    for j in range(kv_heads):
        span = slice(j * HEAD_DIM, (j + 1) * HEAD_DIM)
        heads = range(j * per, (j + 1) * per)
        queried = jnp.concatenate(
            [queries_ref[:, h * HEAD_DIM : (h + 1) * HEAD_DIM].astype(F32) for h in heads], axis=0
        )
        keys = keys_ref[:, :, span].reshape(rows * cache, HEAD_DIM)
        earlier.append(
            lax.dot_general(
                queried.astype(BF16), keys, (((1,), (1,)), ((), ())), preferred_element_type=F32
            )
        )
        fresh_key = new_kv_ref[:, 0, span].astype(F32)
        current.append(queried.reshape(per, rows, HEAD_DIM) * fresh_key[None])
    earlier = jnp.concatenate(earlier, axis=0).reshape(kv_heads * per, rows, rows * cache)
    earlier = jnp.where(valid[None], earlier * scaling, -1e30)
    current = jnp.sum(jnp.concatenate(current, axis=0), axis=-1, keepdims=True) * scaling
    largest = jnp.maximum(jnp.max(earlier, axis=-1, keepdims=True), current)
    earlier_w = jnp.where(valid[None], jnp.exp(earlier - largest), 0.0)
    current_w = jnp.exp(current - largest)
    inverse = 1.0 / (jnp.sum(earlier_w, axis=-1, keepdims=True) + current_w)
    earlier_p = (earlier_w * inverse).astype(BF16).reshape(kv_heads * per * rows, rows * cache)
    current_p = (current_w * inverse).astype(BF16).astype(F32)
    total = jnp.zeros((rows, HEAD_DIM), F32)
    for j in range(kv_heads):
        span = slice(j * HEAD_DIM, (j + 1) * HEAD_DIM)
        values = values_ref[:, :, span].reshape(rows * cache, HEAD_DIM)
        fresh_value = new_kv_ref[:, 1, span].astype(F32)
        attended = jnp.dot(
            earlier_p[j * per * rows : (j + 1) * per * rows], values, preferred_element_type=F32
        )
        attended = attended.reshape(per, rows, HEAD_DIM)
        attended = attended + current_p[j * per : (j + 1) * per] * fresh_value[None]
        for g in range(per):
            h = j * per + g
            place = slice(h * HEAD_DIM, (h + 1) * HEAD_DIM)
            mixed = (
                residual_ref[:, place].astype(F32) + attended[g].astype(BF16).astype(F32)
            ).astype(BF16)
            mixed_ref[:, place] = mixed
            widened = mixed.astype(F32)
            total = total + widened * widened
    meansq = jnp.sum(total, axis=-1, keepdims=True) * (1.0 / width)
    inverse = lax.rsqrt(meansq + 1e-06)
    payload_ref[:, :width] = (
        mixed_ref[...].astype(F32) * inverse * gain_ref[...].astype(F32).reshape(1, width)
    ).astype(BF16)
    if payload_ref.shape[1] > width:
        shares = weights_ref[...] / jnp.sum(weights_ref[...], axis=1, keepdims=True)
        lane = lax.broadcasted_iota(jnp.int32, (rows, LANES), 1)
        expert = jnp.where(lane < LANES // 2, lane, lane - LANES // 2)
        table = jnp.zeros((rows, LANES), F32)
        for k in range(routes_ref.shape[1]):
            table = table + jnp.where(
                routes_ref[:, k : k + 1] == expert, shares[:, k : k + 1], 0.0
            )
        high = table.astype(BF16).astype(F32)
        payload_ref[:, width:] = jnp.where(lane < LANES // 2, high, table - high).astype(BF16)


def front(queries, new_kv, keys, values, lengths, residual, gain, routes, weights, extra):
    rows, width = queries.shape
    vmem = pl.BlockSpec(memory_space=pltpu.VMEM)
    return pl.pallas_call(
        front_kernel,
        out_shape=(
            jax.ShapeDtypeStruct((rows, width), BF16),
            jax.ShapeDtypeStruct((rows, width + extra), BF16),
        ),
        in_specs=[pl.BlockSpec(memory_space=pltpu.SMEM)] + [vmem] * 8,
        out_specs=(vmem, vmem),
        compiler_params=pltpu.CompilerParams(vmem_limit_bytes=VMEM_LIMIT),
        cost_estimate=SMALL,
        name="front",
    )(lengths, queries, new_kv, keys, values, residual, gain, routes, weights)


def in_vmem(array):
    return pltpu.with_memory_space_constraint(array, pltpu.VMEM)


def in_hbm(array):
    return pltpu.with_memory_space_constraint(array, pltpu.HBM)


def unpack_kernel(firsts, codes_refs, scales_hbms, *refs):
    out_refs, (words_refs, scales_refs, sems, scales_sem) = refs[: len(firsts)], refs[len(firsts) :]

    def copy_scales(n):
        columns = pl.ds(firsts[n], words_refs[n].shape[1])
        return pltpu.make_async_copy(
            scales_hbms[n].at[:, columns], scales_refs[n], scales_sem.at[n]
        )

    def fetch(turn):
        n, group = turns[turn]
        rows = pl.ds(group * GROUP, GROUP)
        columns = pl.ds(firsts[n], words_refs[n].shape[1])
        return pltpu.make_async_copy(
            codes_refs[n].at[rows, columns], words_refs[n].at[rows, :], sems.at[turn]
        )

    turns = [
        (n, group)
        for n, words_ref in enumerate(words_refs)
        for group in range(words_ref.shape[0] // GROUP)
    ]
    ahead = 3
    copy_scales(0).start()
    for turn in range(min(ahead, len(turns))):
        fetch(turn).start()
    for n in range(1, len(firsts)):
        copy_scales(n).start()
    for turn, (n, group) in enumerate(turns):
        words_ref, out_ref = words_refs[n], out_refs[n]
        quarter, width = words_ref.shape
        groups = quarter // GROUP
        step = 256 if width % 256 == 0 else LANES
        if turn + ahead < len(turns):
            fetch(turn + ahead).start()
        if group == 0:
            copy_scales(n).wait()
            scales = scales_refs[n][...].astype(F32)
        fetch(turn).wait()
        for column in range(0, width, step):
            spans = [
                jnp.broadcast_to(
                    scales[k * groups + group : k * groups + group + 1, column : column + step],
                    (16, step),
                ).astype(BF16)
                for k in range(4)
            ]

            def chunk(
                i, carry, group=group, column=column, spans=spans, words_ref=words_ref, out_ref=out_ref
            ):
                start = pl.multiple_of(group * GROUP + i * 16, 16)
                words = words_ref[pl.ds(start, 16), column : column + step].astype(jnp.int32)
                for k in range(4):
                    digit = words if k == 0 else lax.shift_right_logical(words, 4 * k)
                    if k < 3:
                        digit = digit & 15
                    level = digit.astype(F32).astype(BF16) - jnp.asarray(8, BF16)
                    out_ref[pl.ds(k * quarter + start, 16), column : column + step] = (
                        level * spans[k]
                    )
                return carry

            lax.fori_loop(0, GROUP // 16, chunk, 0, unroll=True)


def unpack_weights(*jobs):
    hbm = pl.BlockSpec(memory_space=pltpu.HBM)
    vmem = pl.BlockSpec(memory_space=pltpu.VMEM)
    shapes = [(codes.shape[0], width) for codes, _, _, width in jobs]
    turns = sum(quarter // GROUP for quarter, _ in shapes)
    return pl.pallas_call(
        functools.partial(unpack_kernel, tuple(job[2] for job in jobs)),
        out_shape=[pltpu.VMEM((4 * quarter, width), BF16) for quarter, width in shapes],
        in_specs=[[hbm] * len(jobs)] * 2,
        out_specs=[vmem] * len(jobs),
        scratch_shapes=[
            [pltpu.VMEM(shape, F32) for shape in shapes],
            [pltpu.VMEM((4 * quarter // GROUP, width), BF16) for quarter, width in shapes],
            pltpu.SemaphoreType.DMA((turns,)),
            pltpu.SemaphoreType.DMA((len(jobs),)),
        ],
        compiler_params=pltpu.CompilerParams(vmem_limit_bytes=VMEM_MORE),
        cost_estimate=SMALL,
        name="unpack_weights",
    )([in_hbm(job[0]) for job in jobs], [in_hbm(job[1]) for job in jobs])


def hidden_kernel(place_ref, *refs):
    pieces, (gate_ref, up_ref, out_ref, share_ref, rows_ref) = refs[:-5], refs[-5:]
    depth, width = gate_ref.shape
    block = pieces[0].shape[0]
    count = block * len(pieces)
    for n, piece in enumerate(pieces):
        rows_ref[n * block : (n + 1) * block, :] = piece[:, :depth]
        table = piece[:, depth:].astype(F32)
        lane = lax.broadcasted_iota(jnp.int32, table.shape, 1)
        mine = place_ref[0]
        chosen = (lane == mine) | (lane == mine + LANES // 2)
        share = jnp.sum(jnp.where(chosen, table, 0.0), axis=1, keepdims=True)
        share_ref[n * block : (n + 1) * block, :] = jnp.broadcast_to(share, table.shape)
    step = 256
    for column in range(0, width, step):
        span = slice(column, column + step)
        gate = jnp.dot(rows_ref[...], gate_ref[:, span], preferred_element_type=F32)
        upward = jnp.dot(rows_ref[...], up_ref[:, span], preferred_element_type=F32)
        out_ref[:count, span] = (gate / (1.0 + jnp.exp(-gate)) * upward).astype(BF16)
    if out_ref.shape[0] > count:
        out_ref[count:, :] = jnp.zeros((out_ref.shape[0] - count, width), BF16)


def hidden_units(pieces, w_gate, w_up, place, spare=0):
    block, padded = pieces[0].shape
    count = block * len(pieces)
    depth, width = w_gate.shape
    vmem = pl.BlockSpec(memory_space=pltpu.VMEM)
    return pl.pallas_call(
        hidden_kernel,
        out_shape=(pltpu.VMEM((count + spare, width), BF16), pltpu.VMEM((count, LANES), F32)),
        in_specs=[pl.BlockSpec(memory_space=pltpu.SMEM)] + [vmem] * (len(pieces) + 2),
        out_specs=(vmem, vmem),
        scratch_shapes=[pltpu.VMEM((count, depth), BF16)],
        compiler_params=pltpu.CompilerParams(vmem_limit_bytes=VMEM_SOME),
        cost_estimate=SMALL,
        name="gate_up",
    )(place, *pieces, in_vmem(w_gate), in_vmem(w_up))


def own_down_kernel(side_ref, hidden_ref, weight_refs, out_ref):
    half = hidden_ref.shape[1]
    rows = pl.ds(pl.multiple_of(side_ref[0] * half, half), half)
    step = 256
    for n, weight_ref in enumerate(weight_refs):
        width = weight_ref.shape[1]
        for column in range(0, width, step):
            out_ref[:, n * width + column : n * width + column + step] = jnp.dot(
                hidden_ref[: out_ref.shape[0]],
                weight_ref[rows, column : column + step],
                preferred_element_type=F32,
            )


def own_down(side, hidden, weights, count):
    width = sum(weight.shape[1] for weight in weights)
    vmem = pl.BlockSpec(memory_space=pltpu.VMEM)
    return pl.pallas_call(
        own_down_kernel,
        out_shape=pltpu.VMEM((count, width), F32),
        in_specs=[pl.BlockSpec(memory_space=pltpu.SMEM), vmem, [vmem] * len(weights)],
        out_specs=vmem,
        compiler_params=pltpu.CompilerParams(vmem_limit_bytes=VMEM_SOME),
        cost_estimate=SMALL,
        name="down_own",
    )(side, in_vmem(hidden), [in_vmem(weight) for weight in weights])


def peer_down_kernel(side_ref, partial_ref, hidden_ref, weight_refs, share_ref, *out_refs):
    count, half = partial_ref.shape[0], hidden_ref.shape[1]
    rows = pl.ds(pl.multiple_of((1 - side_ref[0]) * half, half), half)
    step = 256
    cut = count // len(out_refs)
    for n, weight_ref in enumerate(weight_refs):
        width = weight_ref.shape[1]
        for column in range(0, width, step):
            span = slice(n * width + column, n * width + column + step)
            produced = partial_ref[:, span] + jnp.dot(
                hidden_ref[:count],
                weight_ref[rows, column : column + step],
                preferred_element_type=F32,
            )
            result = (produced.astype(BF16).astype(F32) * share_ref[:, :1]).astype(BF16)
            for m, out_ref in enumerate(out_refs):
                out_ref[:, span] = result[m * cut : (m + 1) * cut]


def peer_down(side, partial, hidden, weights, share, parts):
    count, width = partial.shape
    vmem = pl.BlockSpec(memory_space=pltpu.VMEM)
    return pl.pallas_call(
        peer_down_kernel,
        out_shape=(pltpu.VMEM((count // parts, width), BF16),) * parts,
        in_specs=[pl.BlockSpec(memory_space=pltpu.SMEM), vmem, vmem, [vmem] * len(weights), vmem],
        out_specs=(vmem,) * parts,
        compiler_params=pltpu.CompilerParams(vmem_limit_bytes=VMEM_SOME),
        cost_estimate=SMALL,
        name="down_peer",
    )(side, in_vmem(partial), hidden, [in_vmem(weight) for weight in weights], in_vmem(share))


def halve_kernel(terms, *refs):
    term_refs, out_refs = refs[:terms], refs[terms:]
    total = term_refs[0][...].astype(F32)
    for term_ref in term_refs[1:]:
        total = total + term_ref[...].astype(F32)
    size = total.shape[0] // len(out_refs)
    for n, out_ref in enumerate(out_refs):
        out_ref[...] = total[n * size : (n + 1) * size].astype(out_ref.dtype)


def add_and_cut(kept, arrived, parts):
    count, width = kept[0].shape
    vmem = pl.BlockSpec(memory_space=pltpu.VMEM)
    shape = pltpu.VMEM((count // parts, width), BF16)
    return pl.pallas_call(
        functools.partial(halve_kernel, len(kept + arrived)),
        out_shape=(shape,) * parts,
        in_specs=[vmem] * len(kept + arrived),
        out_specs=(vmem,) * parts,
        compiler_params=pltpu.CompilerParams(vmem_limit_bytes=VMEM_SOME),
        cost_estimate=SMALL,
        name="add_and_cut",
    )(*[in_vmem(part) for part in kept], *arrived)


def join_kernel(parts, far_ref, *refs):
    near_refs, out_refs = refs[:-parts], refs[-parts:]
    size = far_ref.shape[0] // parts
    near = near_refs[0][...].astype(F32)
    for near_ref in near_refs[1:]:
        near = near + near_ref[...].astype(F32)
    far = far_ref[...].astype(F32)
    for n, out_ref in enumerate(out_refs):
        rows = slice(n * size, (n + 1) * size)
        out_ref[...] = jnp.concatenate([near[rows], far[rows]], axis=0).astype(BF16)


def join(near, far, parts):
    count, width = far.shape
    vmem = pl.BlockSpec(memory_space=pltpu.VMEM)
    return pl.pallas_call(
        functools.partial(join_kernel, parts),
        out_shape=(pltpu.VMEM((2 * count // parts, width), BF16),) * parts,
        in_specs=[vmem] * (1 + len(near)),
        out_specs=(vmem,) * parts,
        compiler_params=pltpu.CompilerParams(vmem_limit_bytes=VMEM_SOME),
        cost_estimate=SMALL,
        name="join",
    )(far, *near)


def finish_kernel(side_ref, mixed_ref, *refs):
    block_refs, out_ref = refs[:-1], refs[-1]
    rows, width = mixed_ref.shape
    total = block_refs[0][...].astype(F32)
    for block_ref in block_refs[1:]:
        total = total + block_ref[...].astype(F32)
    near, far = total[:rows], total[rows:]
    first = side_ref[0] == 0
    half = width // 2
    for n, part in enumerate((jnp.where(first, near, far), jnp.where(first, far, near))):
        span = slice(n * half, (n + 1) * half)
        out_ref[:, span] = (mixed_ref[:, span].astype(F32) + part).astype(BF16)


def finish(side, mixed, blocks):
    vmem = pl.BlockSpec(memory_space=pltpu.VMEM)
    return pl.pallas_call(
        finish_kernel,
        out_shape=jax.ShapeDtypeStruct(mixed.shape, BF16),
        in_specs=[pl.BlockSpec(memory_space=pltpu.SMEM)] + [vmem] * (1 + len(blocks)),
        out_specs=vmem,
        compiler_params=pltpu.CompilerParams(vmem_limit_bytes=VMEM_SOME),
        name="finish",
    )(side, mixed, *blocks)


def dense(payload, mixed, codes):
    gate_codes, gate_scales, up_codes, up_scales, down_codes, down_scales = codes
    groups = lax.axis_size("dp")
    experts = lax.axis_size("expert")
    devices = groups * experts
    core, line, layer, plane = 1, 2, 4, experts
    layers = experts // layer
    side = lax.axis_index("dp").reshape(1).astype(jnp.int32)
    place = lax.axis_index("expert").reshape(1).astype(jnp.int32)

    def swap(block, offset):
        return lax.ppermute(block, ("dp", "expert"), [(i, i ^ offset) for i in range(devices)])

    side, place, gate_scales, down_scales, payload = lax.optimization_barrier(
        (side, place, gate_scales, down_scales, payload)
    )
    units = gate_codes.shape[1]
    half = down_codes.shape[1] // 2
    blocks = [swap(payload, z * layer) for z in range(1, layers)]
    w_gate, w_down = unpack_weights(
        (gate_codes, gate_scales, 0, units), (down_codes, down_scales, 0, half)
    )
    blocks, w_gate = lax.optimization_barrier((blocks, w_gate))
    stack = jnp.concatenate([payload] + blocks, axis=0)
    up_scales, stack = lax.optimization_barrier((up_scales, stack))
    beside, above, stack_pair = swap(stack, plane), swap(stack, line), swap(stack, core)
    (w_up,) = unpack_weights((up_codes, up_scales, 0, units))
    above, stack_pair, w_up = lax.optimization_barrier((above, stack_pair, w_up))
    across, above_pair = swap(above, plane), swap(above, core)
    above_pair, beside = lax.optimization_barrier((above_pair, beside))
    beside_pair = swap(beside, core)
    hidden_own, share_own = hidden_units(
        [stack, stack_pair, above, above_pair], w_gate, w_up, place, SPARE
    )
    other_peer = swap(hidden_own, plane)
    down_scales, hidden_own = lax.optimization_barrier((down_scales, hidden_own))
    (w_more,) = unpack_weights((down_codes, down_scales, half, half))
    across, w_more = lax.optimization_barrier((across, w_more))
    w_down = [w_down, w_more]
    hidden_other, share_other = hidden_units(
        [beside, beside_pair, across, swap(across, core)], w_gate, w_up, place
    )
    own_peer = swap(hidden_other, plane)

    count = share_own.shape[0]
    partial_other = own_down(side, hidden_other, w_down, count)
    partial_own = own_down(side, hidden_own, w_down, count)
    keep, send = peer_down(side, partial_other, other_peer, w_down, share_other, 2)
    keep, send = add_and_cut([keep], [swap(send, line)], 2)
    (onward,) = add_and_cut([keep], [swap(send, core)], 1)
    far = swap(onward, plane)
    keep_near, send_near, keep_far, send_far = peer_down(
        side, partial_own, own_peer, w_down, share_own, 4
    )
    (onward,) = add_and_cut([keep_far], [swap(send_far, core)], 1)
    near = [in_vmem(keep_near), swap(send_near, core), swap(onward, line)]
    blocks = join(near, far, layers)
    blocks = [blocks[0]] + [swap(blocks[z], z * layer) for z in range(1, layers)]
    return finish(side, mixed, blocks)


def slot_table(routes, experts, capacity):
    flattened = routes.reshape(-1)
    onehot = (flattened[:, None] == jnp.arange(experts, dtype=jnp.int32)[None, :]).astype(jnp.int32)
    ranking = jnp.sum((jnp.cumsum(onehot, axis=0) - 1) * onehot, axis=1)
    return (flattened * capacity + ranking).reshape(routes.shape)


def dispatch(block, slots, width):
    targets = jnp.arange(width, dtype=jnp.int32)
    placing = jnp.sum((slots[None, :, :] == targets[:, None, None]).astype(F32), axis=2)
    return jnp.dot(placing.astype(BF16), block, preferred_element_type=F32).astype(BF16)


def unpack(codes, scales):
    quarter, width = codes.shape
    divisors = jnp.array([1.0, 1.0 / 16, 1.0 / 256, 1.0 / 4096], F32)[:, None, None]
    lifted = jnp.floor(codes[None, :, :] * divisors)
    levels = lifted - 16.0 * jnp.floor(lifted * (1.0 / 16)) - 8.0
    height = 4 * quarter
    grouped = levels.reshape(height // GROUP, GROUP, width) * scales.astype(F32)[:, None, :]
    return grouped.reshape(height, width).astype(BF16)


def routed(normed, mixed, routes, route_weights, codes, capacity):
    gate_codes, gate_scales, up_codes, up_scales, down_codes, down_scales = codes
    experts = lax.axis_size("expert")
    groups = lax.axis_size("dp")
    row_count, width = mixed.shape
    own_slots = slot_table(routes, experts, capacity)
    w_gate = unpack(gate_codes, gate_scales)
    w_up = unpack(up_codes, up_scales)
    w_down = unpack(down_codes, down_scales)
    local_units = w_gate.shape[1]
    peer_rows = lax.all_gather(normed, "dp", axis=0, tiled=True).reshape(groups, row_count, width)
    peer_routes = lax.all_gather(routes, "dp", axis=0, tiled=True).reshape(groups, row_count, TOP)

    def build(block, table):
        return dispatch(block, slot_table(table, experts, capacity), experts * capacity)

    outgoing = jax.vmap(build)(peer_rows, peer_routes).reshape(groups, experts, capacity, width)
    items = lax.all_to_all(outgoing, "expert", split_axis=1, concat_axis=1, tiled=True)
    inputs = items.reshape(-1, width)
    gate = jnp.dot(inputs, w_gate, preferred_element_type=F32)
    upward = jnp.dot(inputs, w_up, preferred_element_type=F32)
    hidden = (jax.nn.silu(gate) * upward).astype(BF16).reshape(-1, local_units)
    produced = jnp.dot(
        lax.all_gather(hidden, "dp", axis=1, tiled=True), w_down, preferred_element_type=F32
    ).astype(BF16)
    produced = produced.reshape(groups, -1, produced.shape[1])
    returned = lax.all_to_all(
        lax.all_to_all(produced, "dp", split_axis=0, concat_axis=2, tiled=True),
        "expert",
        split_axis=1,
        concat_axis=0,
        tiled=True,
    )
    shares = route_weights / jnp.sum(route_weights, axis=1, keepdims=True)
    targets = jnp.arange(experts * capacity, dtype=jnp.int32)
    spreading = jnp.sum(
        jnp.where(own_slots[:, :, None] == targets[None, None, :], shares[:, :, None], 0.0), axis=1
    )
    combined = jnp.dot(
        spreading, returned.reshape(-1, width).astype(F32), precision=lax.Precision.HIGHEST
    )
    return (mixed.astype(F32) + combined).astype(BF16)


def body(
    queries,
    new_kv,
    cache_keys,
    cache_values,
    lengths,
    residual,
    norm_gain,
    routes,
    route_weights,
    *packed,
):
    experts = lax.axis_size("expert")
    groups = lax.axis_size("dp")
    row_count = queries.shape[0]
    capacity = min(row_count, max(2, 2 * row_count * TOP // experts))
    every = (
        capacity == row_count
        and groups == 2
        and experts <= LANES // 2
        and experts % 4 == 0
        and experts & (experts - 1) == 0
    )
    mixed, payload = front(
        queries,
        new_kv,
        cache_keys,
        cache_values,
        lengths,
        residual,
        norm_gain,
        routes,
        route_weights,
        LANES if every else 0,
    )
    codes = [array[0] for array in packed]
    if every:
        return dense(payload, mixed, codes)
    return routed(payload, mixed, routes, route_weights, codes, capacity)


def solution(mesh):
    return jax.shard_map(
        body,
        mesh=mesh,
        in_specs=(
            P(("dp", "expert"), None),
            P(("dp", "expert"), None, None),
            P(("dp", "expert"), None, None),
            P(("dp", "expert"), None, None),
            P(("dp", "expert")),
            P(("dp", "expert"), None),
            P(),
            P(("dp", "expert"), None),
            P(("dp", "expert"), None),
            P("expert", None, "dp"),
            P("expert", None, "dp"),
            P("expert", None, "dp"),
            P("expert", None, "dp"),
            P("expert", None, "dp"),
            P("expert", None, "dp"),
        ),
        out_specs=P(("dp", "expert"), None),
        check_vma=False,
    )
```

```python
import functools

import jax
import jax.numpy as jnp
from jax import lax
from jax.experimental import pallas as pl
from jax.experimental.pallas import tpu as pltpu
from jax.sharding import PartitionSpec as P

HEAD_DIM = 128
GROUP = 128
TOP = 8
LANES = 128
VMEM_LIMIT = 56 * 2**20
VMEM_SOME = 16 * 2**20
VMEM_MORE = 24 * 2**20
SPARE = 0
SMALL = pl.CostEstimate(flops=1, bytes_accessed=1, transcendentals=0)
F32 = jnp.float32
BF16 = jnp.bfloat16


def front_kernel(
    lengths_ref,
    queries_ref,
    new_kv_ref,
    keys_ref,
    values_ref,
    residual_ref,
    gain_ref,
    routes_ref,
    weights_ref,
    mixed_ref,
    payload_ref,
):
    rows, cache, kv_width = keys_ref.shape
    width = queries_ref.shape[1]
    kv_heads = kv_width // HEAD_DIM
    per = width // kv_width
    scaling = HEAD_DIM ** (-0.5)
    row_id = lax.broadcasted_iota(jnp.int32, (rows, rows * cache), 0)
    lane_id = lax.broadcasted_iota(jnp.int32, (rows, rows * cache), 1)
    bound = jnp.zeros((rows, rows * cache), jnp.int32)
    for r in range(rows):
        bound = jnp.where(row_id == r, r * cache + lengths_ref[r], bound)
    valid = (lane_id >= row_id * cache) & (lane_id < bound)
    earlier, current = [], []
    for j in range(kv_heads):
        span = slice(j * HEAD_DIM, (j + 1) * HEAD_DIM)
        heads = range(j * per, (j + 1) * per)
        queried = jnp.concatenate(
            [queries_ref[:, h * HEAD_DIM : (h + 1) * HEAD_DIM].astype(F32) for h in heads], axis=0
        )
        keys = keys_ref[:, :, span].reshape(rows * cache, HEAD_DIM)
        earlier.append(
            lax.dot_general(
                queried.astype(BF16), keys, (((1,), (1,)), ((), ())), preferred_element_type=F32
            )
        )
        fresh_key = new_kv_ref[:, 0, span].astype(F32)
        current.append(queried.reshape(per, rows, HEAD_DIM) * fresh_key[None])
    earlier = jnp.concatenate(earlier, axis=0).reshape(kv_heads * per, rows, rows * cache)
    earlier = jnp.where(valid[None], earlier * scaling, -1e30)
    current = jnp.sum(jnp.concatenate(current, axis=0), axis=-1, keepdims=True) * scaling
    largest = jnp.maximum(jnp.max(earlier, axis=-1, keepdims=True), current)
    earlier_w = jnp.where(valid[None], jnp.exp(earlier - largest), 0.0)
    current_w = jnp.exp(current - largest)
    inverse = 1.0 / (jnp.sum(earlier_w, axis=-1, keepdims=True) + current_w)
    earlier_p = (earlier_w * inverse).astype(BF16).reshape(kv_heads * per * rows, rows * cache)
    current_p = (current_w * inverse).astype(BF16).astype(F32)
    total = jnp.zeros((rows, HEAD_DIM), F32)
    for j in range(kv_heads):
        span = slice(j * HEAD_DIM, (j + 1) * HEAD_DIM)
        values = values_ref[:, :, span].reshape(rows * cache, HEAD_DIM)
        fresh_value = new_kv_ref[:, 1, span].astype(F32)
        attended = jnp.dot(
            earlier_p[j * per * rows : (j + 1) * per * rows], values, preferred_element_type=F32
        )
        attended = attended.reshape(per, rows, HEAD_DIM)
        attended = attended + current_p[j * per : (j + 1) * per] * fresh_value[None]
        for g in range(per):
            h = j * per + g
            place = slice(h * HEAD_DIM, (h + 1) * HEAD_DIM)
            mixed = (
                residual_ref[:, place].astype(F32) + attended[g].astype(BF16).astype(F32)
            ).astype(BF16)
            mixed_ref[:, place] = mixed
            widened = mixed.astype(F32)
            total = total + widened * widened
    meansq = jnp.sum(total, axis=-1, keepdims=True) * (1.0 / width)
    inverse = lax.rsqrt(meansq + 1e-06)
    payload_ref[:, :width] = (
        mixed_ref[...].astype(F32) * inverse * gain_ref[...].astype(F32).reshape(1, width)
    ).astype(BF16)
    if payload_ref.shape[1] > width:
        shares = weights_ref[...] / jnp.sum(weights_ref[...], axis=1, keepdims=True)
        lane = lax.broadcasted_iota(jnp.int32, (rows, LANES), 1)
        expert = jnp.where(lane < LANES // 2, lane, lane - LANES // 2)
        table = jnp.zeros((rows, LANES), F32)
        for k in range(routes_ref.shape[1]):
            table = table + jnp.where(
                routes_ref[:, k : k + 1] == expert, shares[:, k : k + 1], 0.0
            )
        high = table.astype(BF16).astype(F32)
        payload_ref[:, width:] = jnp.where(lane < LANES // 2, high, table - high).astype(BF16)


def front(queries, new_kv, keys, values, lengths, residual, gain, routes, weights, extra):
    rows, width = queries.shape
    vmem = pl.BlockSpec(memory_space=pltpu.VMEM)
    return pl.pallas_call(
        front_kernel,
        out_shape=(
            jax.ShapeDtypeStruct((rows, width), BF16),
            jax.ShapeDtypeStruct((rows, width + extra), BF16),
        ),
        in_specs=[pl.BlockSpec(memory_space=pltpu.SMEM)] + [vmem] * 8,
        out_specs=(vmem, vmem),
        compiler_params=pltpu.CompilerParams(vmem_limit_bytes=VMEM_LIMIT),
        cost_estimate=SMALL,
        name="front",
    )(lengths, queries, new_kv, keys, values, residual, gain, routes, weights)


def in_vmem(array):
    return pltpu.with_memory_space_constraint(array, pltpu.VMEM)


def in_hbm(array):
    return pltpu.with_memory_space_constraint(array, pltpu.HBM)


def unpack_kernel(firsts, codes_refs, scales_hbms, *refs):
    out_refs, (words_refs, scales_refs, sems, scales_sem) = refs[: len(firsts)], refs[len(firsts) :]

    def copy_scales(n):
        columns = pl.ds(firsts[n], words_refs[n].shape[1])
        return pltpu.make_async_copy(
            scales_hbms[n].at[:, columns], scales_refs[n], scales_sem.at[n]
        )

    def fetch(turn):
        n, group = turns[turn]
        rows = pl.ds(group * GROUP, GROUP)
        columns = pl.ds(firsts[n], words_refs[n].shape[1])
        return pltpu.make_async_copy(
            codes_refs[n].at[rows, columns], words_refs[n].at[rows, :], sems.at[turn]
        )

    turns = [
        (n, group)
        for n, words_ref in enumerate(words_refs)
        for group in range(words_ref.shape[0] // GROUP)
    ]
    ahead = 3
    copy_scales(0).start()
    for turn in range(min(ahead, len(turns))):
        fetch(turn).start()
    for n in range(1, len(firsts)):
        copy_scales(n).start()
    for turn, (n, group) in enumerate(turns):
        words_ref, out_ref = words_refs[n], out_refs[n]
        quarter, width = words_ref.shape
        groups = quarter // GROUP
        step = 256 if width % 256 == 0 else LANES
        if turn + ahead < len(turns):
            fetch(turn + ahead).start()
        if group == 0:
            copy_scales(n).wait()
            scales = scales_refs[n][...].astype(F32)
        fetch(turn).wait()
        for column in range(0, width, step):
            spans = [
                jnp.broadcast_to(
                    scales[k * groups + group : k * groups + group + 1, column : column + step],
                    (16, step),
                ).astype(BF16)
                for k in range(4)
            ]

            def chunk(
                i, carry, group=group, column=column, spans=spans, words_ref=words_ref, out_ref=out_ref
            ):
                start = pl.multiple_of(group * GROUP + i * 16, 16)
                words = words_ref[pl.ds(start, 16), column : column + step].astype(jnp.int32)
                for k in range(4):
                    digit = words if k == 0 else lax.shift_right_logical(words, 4 * k)
                    if k < 3:
                        digit = digit & 15
                    level = digit.astype(F32).astype(BF16) - jnp.asarray(8, BF16)
                    out_ref[pl.ds(k * quarter + start, 16), column : column + step] = (
                        level * spans[k]
                    )
                return carry

            lax.fori_loop(0, GROUP // 16, chunk, 0, unroll=True)


def unpack_weights(*jobs):
    hbm = pl.BlockSpec(memory_space=pltpu.HBM)
    vmem = pl.BlockSpec(memory_space=pltpu.VMEM)
    shapes = [(codes.shape[0], width) for codes, _, _, width in jobs]
    turns = sum(quarter // GROUP for quarter, _ in shapes)
    return pl.pallas_call(
        functools.partial(unpack_kernel, tuple(job[2] for job in jobs)),
        out_shape=[pltpu.VMEM((4 * quarter, width), BF16) for quarter, width in shapes],
        in_specs=[[hbm] * len(jobs)] * 2,
        out_specs=[vmem] * len(jobs),
        scratch_shapes=[
            [pltpu.VMEM(shape, F32) for shape in shapes],
            [pltpu.VMEM((4 * quarter // GROUP, width), BF16) for quarter, width in shapes],
            pltpu.SemaphoreType.DMA((turns,)),
            pltpu.SemaphoreType.DMA((len(jobs),)),
        ],
        compiler_params=pltpu.CompilerParams(vmem_limit_bytes=VMEM_MORE),
        cost_estimate=SMALL,
        name="unpack_weights",
    )([in_hbm(job[0]) for job in jobs], [in_hbm(job[1]) for job in jobs])


def hidden_kernel(place_ref, *refs):
    pieces, (gate_ref, up_ref, out_ref, share_ref, rows_ref) = refs[:-5], refs[-5:]
    depth, width = gate_ref.shape
    block = pieces[0].shape[0]
    count = block * len(pieces)
    for n, piece in enumerate(pieces):
        rows_ref[n * block : (n + 1) * block, :] = piece[:, :depth]
        table = piece[:, depth:].astype(F32)
        lane = lax.broadcasted_iota(jnp.int32, table.shape, 1)
        mine = place_ref[0]
        chosen = (lane == mine) | (lane == mine + LANES // 2)
        share = jnp.sum(jnp.where(chosen, table, 0.0), axis=1, keepdims=True)
        share_ref[n * block : (n + 1) * block, :] = jnp.broadcast_to(share, table.shape)
    step = 256
    for column in range(0, width, step):
        span = slice(column, column + step)
        gate = jnp.dot(rows_ref[...], gate_ref[:, span], preferred_element_type=F32)
        upward = jnp.dot(rows_ref[...], up_ref[:, span], preferred_element_type=F32)
        out_ref[:count, span] = (gate / (1.0 + jnp.exp(-gate)) * upward).astype(BF16)
    if out_ref.shape[0] > count:
        out_ref[count:, :] = jnp.zeros((out_ref.shape[0] - count, width), BF16)


def hidden_units(pieces, w_gate, w_up, place, spare=0):
    block, padded = pieces[0].shape
    count = block * len(pieces)
    depth, width = w_gate.shape
    vmem = pl.BlockSpec(memory_space=pltpu.VMEM)
    return pl.pallas_call(
        hidden_kernel,
        out_shape=(pltpu.VMEM((count + spare, width), BF16), pltpu.VMEM((count, LANES), F32)),
        in_specs=[pl.BlockSpec(memory_space=pltpu.SMEM)] + [vmem] * (len(pieces) + 2),
        out_specs=(vmem, vmem),
        scratch_shapes=[pltpu.VMEM((count, depth), BF16)],
        compiler_params=pltpu.CompilerParams(vmem_limit_bytes=VMEM_SOME),
        cost_estimate=SMALL,
        name="gate_up",
    )(place, *pieces, in_vmem(w_gate), in_vmem(w_up))


def own_down_kernel(side_ref, hidden_ref, weight_refs, out_ref):
    half = hidden_ref.shape[1]
    rows = pl.ds(pl.multiple_of(side_ref[0] * half, half), half)
    step = 256
    for n, weight_ref in enumerate(weight_refs):
        width = weight_ref.shape[1]
        for column in range(0, width, step):
            out_ref[:, n * width + column : n * width + column + step] = jnp.dot(
                hidden_ref[: out_ref.shape[0]],
                weight_ref[rows, column : column + step],
                preferred_element_type=F32,
            )


def own_down(side, hidden, weights, count):
    width = sum(weight.shape[1] for weight in weights)
    vmem = pl.BlockSpec(memory_space=pltpu.VMEM)
    return pl.pallas_call(
        own_down_kernel,
        out_shape=pltpu.VMEM((count, width), F32),
        in_specs=[pl.BlockSpec(memory_space=pltpu.SMEM), vmem, [vmem] * len(weights)],
        out_specs=vmem,
        compiler_params=pltpu.CompilerParams(vmem_limit_bytes=VMEM_SOME),
        cost_estimate=SMALL,
        name="down_own",
    )(side, in_vmem(hidden), [in_vmem(weight) for weight in weights])


def cuts(rows, parts):
    size = rows.shape[0] // parts
    return [rows[n * size : (n + 1) * size] for n in range(parts)]


def peer_down_kernel(
    side_ref, partial_ref, hidden_ref, weight_refs, share_ref, *out_refs
):
    count, half = partial_ref.shape[0], hidden_ref.shape[1]
    rows = pl.ds(pl.multiple_of((1 - side_ref[0]) * half, half), half)
    step = 256
    for n, weight_ref in enumerate(weight_refs):
        width = weight_ref.shape[1]
        for column in range(0, width, step):
            span = slice(n * width + column, n * width + column + step)
            produced = partial_ref[:, span] + jnp.dot(
                hidden_ref[:count],
                weight_ref[rows, column : column + step],
                preferred_element_type=F32,
            )
            result = produced.astype(BF16).astype(F32) * share_ref[:, :1]
            for out_ref, cut in zip(out_refs, cuts(result, len(out_refs))):
                out_ref[:, span] = cut.astype(BF16)


def peer_down(side, partial, hidden, weights, share, parts):
    count, width = partial.shape
    vmem = pl.BlockSpec(memory_space=pltpu.VMEM)
    return pl.pallas_call(
        peer_down_kernel,
        out_shape=(pltpu.VMEM((count // parts, width), BF16),) * parts,
        in_specs=[pl.BlockSpec(memory_space=pltpu.SMEM), vmem, vmem, [vmem] * len(weights), vmem],
        out_specs=(vmem,) * parts,
        compiler_params=pltpu.CompilerParams(vmem_limit_bytes=VMEM_SOME),
        cost_estimate=SMALL,
        name="down_peer",
    )(side, in_vmem(partial), hidden, [in_vmem(weight) for weight in weights], in_vmem(share))


def add_kernel(terms, *refs):
    term_refs, out_refs = refs[:terms], refs[terms:]
    total = term_refs[0][...].astype(F32)
    for term_ref in term_refs[1:]:
        total = total + term_ref[...].astype(F32)
    width = total.shape[1]
    for out_ref, cut in zip(out_refs, cuts(total, len(out_refs))):
        out_ref[:, :width] = cut.astype(out_ref.dtype)
        if out_ref.shape[1] > width:
            out_ref[:, width:] = jnp.zeros((cut.shape[0], out_ref.shape[1] - width), out_ref.dtype)


def add_and_cut(kept, arrived, parts, spare=0):
    count, width = kept[0].shape
    vmem = pl.BlockSpec(memory_space=pltpu.VMEM)
    shape = pltpu.VMEM((count // parts, width + spare), BF16)
    return pl.pallas_call(
        functools.partial(add_kernel, len(kept + arrived)),
        out_shape=(shape,) * parts,
        in_specs=[vmem] * len(kept + arrived),
        out_specs=(vmem,) * parts,
        compiler_params=pltpu.CompilerParams(vmem_limit_bytes=VMEM_SOME),
        cost_estimate=SMALL,
        name="add_and_cut",
    )(*[in_vmem(part) for part in kept], *arrived)


def finish_kernel(side_ref, mixed_ref, far_ref, *refs):
    near_refs, out_ref = refs[:-1], refs[-1]
    half = far_ref.shape[1]
    near = near_refs[0][:, :half].astype(F32)
    for near_ref in near_refs[1:]:
        near = near + near_ref[:, :half].astype(F32)
    far = far_ref[...].astype(F32)
    first = side_ref[0] == 0
    for n, part in enumerate((jnp.where(first, near, far), jnp.where(first, far, near))):
        span = slice(n * half, (n + 1) * half)
        out_ref[:, span] = (mixed_ref[:, span].astype(F32) + part).astype(BF16)


def finish(side, mixed, far, near):
    vmem = pl.BlockSpec(memory_space=pltpu.VMEM)
    return pl.pallas_call(
        finish_kernel,
        out_shape=jax.ShapeDtypeStruct(mixed.shape, BF16),
        in_specs=[pl.BlockSpec(memory_space=pltpu.SMEM)] + [vmem] * (2 + len(near)),
        out_specs=vmem,
        compiler_params=pltpu.CompilerParams(vmem_limit_bytes=VMEM_SOME),
        cost_estimate=SMALL,
        name="finish",
    )(side, mixed, far, *near)


def dense(payload, mixed, codes):
    gate_codes, gate_scales, up_codes, up_scales, down_codes, down_scales = codes
    groups = lax.axis_size("dp")
    experts = lax.axis_size("expert")
    devices = groups * experts
    core, line, layer, plane = 1, 2, 4, experts
    layers = experts // layer
    side = lax.axis_index("dp").reshape(1).astype(jnp.int32)
    place = lax.axis_index("expert").reshape(1).astype(jnp.int32)

    def swap(block, offset):
        return lax.ppermute(block, ("dp", "expert"), [(i, i ^ offset) for i in range(devices)])

    side, place, gate_scales, down_scales, payload = lax.optimization_barrier(
        (side, place, gate_scales, down_scales, payload)
    )
    units = gate_codes.shape[1]
    half = down_codes.shape[1] // 2
    blocks = [swap(payload, z * layer) for z in range(1, layers)]
    w_gate, w_down = unpack_weights(
        (gate_codes, gate_scales, 0, units), (down_codes, down_scales, 0, half)
    )
    blocks, w_gate = lax.optimization_barrier((blocks, w_gate))
    stack = jnp.concatenate([payload] + blocks, axis=0)
    up_scales, stack = lax.optimization_barrier((up_scales, stack))
    beside, above, stack_pair = swap(stack, plane), swap(stack, line), swap(stack, core)
    (w_up,) = unpack_weights((up_codes, up_scales, 0, units))
    above, stack_pair, w_up = lax.optimization_barrier((above, stack_pair, w_up))
    across, above_pair = swap(above, plane), swap(above, core)
    above_pair, beside = lax.optimization_barrier((above_pair, beside))
    beside_pair = swap(beside, core)
    hidden_own, share_own = hidden_units(
        [stack, stack_pair, above, above_pair], w_gate, w_up, place, SPARE
    )
    other_peer = swap(hidden_own, plane)
    down_scales, hidden_own = lax.optimization_barrier((down_scales, hidden_own))
    (w_more,) = unpack_weights((down_codes, down_scales, half, half))
    across, w_more = lax.optimization_barrier((across, w_more))
    w_down = [w_down, w_more]
    hidden_other, share_other = hidden_units(
        [beside, beside_pair, across, swap(across, core)], w_gate, w_up, place
    )
    own_peer = swap(hidden_other, plane)

    count = share_own.shape[0]
    partial_other = own_down(side, hidden_other, w_down, count)
    partial_own = own_down(side, hidden_own, w_down, count)
    keep, send = peer_down(side, partial_other, other_peer, w_down, share_other, 2)
    keep, send = add_and_cut([keep], [swap(send, line)], 2)
    parts = add_and_cut([keep], [swap(send, core)], layers)
    arrived = [swap(parts[z], z * layer) for z in range(1, layers)]
    keep_near, send_near, keep_far, send_far = peer_down(
        side, partial_own, own_peer, w_down, share_own, 4
    )
    (onward,) = add_and_cut([keep_far], [swap(send_far, core)], 1)
    near = add_and_cut(
        [keep_near], [swap(send_near, core), swap(onward, line)], layers, LANES
    )
    arrived, _ = lax.optimization_barrier((arrived, near[0]))
    (far,) = add_and_cut([parts[0]], arrived, 1)
    near = [near[0]] + [swap(near[z], z * layer) for z in range(1, layers)]
    return finish(side, mixed, swap(far, plane), near)


def slot_table(routes, experts, capacity):
    flattened = routes.reshape(-1)
    onehot = (flattened[:, None] == jnp.arange(experts, dtype=jnp.int32)[None, :]).astype(jnp.int32)
    ranking = jnp.sum((jnp.cumsum(onehot, axis=0) - 1) * onehot, axis=1)
    return (flattened * capacity + ranking).reshape(routes.shape)


def dispatch(block, slots, width):
    targets = jnp.arange(width, dtype=jnp.int32)
    placing = jnp.sum((slots[None, :, :] == targets[:, None, None]).astype(F32), axis=2)
    return jnp.dot(placing.astype(BF16), block, preferred_element_type=F32).astype(BF16)


def unpack(codes, scales):
    quarter, width = codes.shape
    divisors = jnp.array([1.0, 1.0 / 16, 1.0 / 256, 1.0 / 4096], F32)[:, None, None]
    lifted = jnp.floor(codes[None, :, :] * divisors)
    levels = lifted - 16.0 * jnp.floor(lifted * (1.0 / 16)) - 8.0
    height = 4 * quarter
    grouped = levels.reshape(height // GROUP, GROUP, width) * scales.astype(F32)[:, None, :]
    return grouped.reshape(height, width).astype(BF16)


def routed(normed, mixed, routes, route_weights, codes, capacity):
    gate_codes, gate_scales, up_codes, up_scales, down_codes, down_scales = codes
    experts = lax.axis_size("expert")
    groups = lax.axis_size("dp")
    row_count, width = mixed.shape
    own_slots = slot_table(routes, experts, capacity)
    w_gate = unpack(gate_codes, gate_scales)
    w_up = unpack(up_codes, up_scales)
    w_down = unpack(down_codes, down_scales)
    local_units = w_gate.shape[1]
    peer_rows = lax.all_gather(normed, "dp", axis=0, tiled=True).reshape(groups, row_count, width)
    peer_routes = lax.all_gather(routes, "dp", axis=0, tiled=True).reshape(groups, row_count, TOP)

    def build(block, table):
        return dispatch(block, slot_table(table, experts, capacity), experts * capacity)

    outgoing = jax.vmap(build)(peer_rows, peer_routes).reshape(groups, experts, capacity, width)
    items = lax.all_to_all(outgoing, "expert", split_axis=1, concat_axis=1, tiled=True)
    inputs = items.reshape(-1, width)
    gate = jnp.dot(inputs, w_gate, preferred_element_type=F32)
    upward = jnp.dot(inputs, w_up, preferred_element_type=F32)
    hidden = (jax.nn.silu(gate) * upward).astype(BF16).reshape(-1, local_units)
    produced = jnp.dot(
        lax.all_gather(hidden, "dp", axis=1, tiled=True), w_down, preferred_element_type=F32
    ).astype(BF16)
    produced = produced.reshape(groups, -1, produced.shape[1])
    returned = lax.all_to_all(
        lax.all_to_all(produced, "dp", split_axis=0, concat_axis=2, tiled=True),
        "expert",
        split_axis=1,
        concat_axis=0,
        tiled=True,
    )
    shares = route_weights / jnp.sum(route_weights, axis=1, keepdims=True)
    targets = jnp.arange(experts * capacity, dtype=jnp.int32)
    spreading = jnp.sum(
        jnp.where(own_slots[:, :, None] == targets[None, None, :], shares[:, :, None], 0.0), axis=1
    )
    combined = jnp.dot(
        spreading, returned.reshape(-1, width).astype(F32), precision=lax.Precision.HIGHEST
    )
    return (mixed.astype(F32) + combined).astype(BF16)


def body(
    queries,
    new_kv,
    cache_keys,
    cache_values,
    lengths,
    residual,
    norm_gain,
    routes,
    route_weights,
    *packed,
):
    experts = lax.axis_size("expert")
    groups = lax.axis_size("dp")
    row_count = queries.shape[0]
    capacity = min(row_count, max(2, 2 * row_count * TOP // experts))
    every = (
        capacity == row_count
        and groups == 2
        and experts <= LANES // 2
        and experts % 4 == 0
        and experts & (experts - 1) == 0
    )
    mixed, payload = front(
        queries,
        new_kv,
        cache_keys,
        cache_values,
        lengths,
        residual,
        norm_gain,
        routes,
        route_weights,
        LANES if every else 0,
    )
    codes = [array[0] for array in packed]
    if every:
        return dense(payload, mixed, codes)
    return routed(payload, mixed, routes, route_weights, codes, capacity)


def solution(mesh):
    return jax.shard_map(
        body,
        mesh=mesh,
        in_specs=(
            P(("dp", "expert"), None),
            P(("dp", "expert"), None, None),
            P(("dp", "expert"), None, None),
            P(("dp", "expert"), None, None),
            P(("dp", "expert")),
            P(("dp", "expert"), None),
            P(),
            P(("dp", "expert"), None),
            P(("dp", "expert"), None),
            P("expert", None, "dp"),
            P("expert", None, "dp"),
            P("expert", None, "dp"),
            P("expert", None, "dp"),
            P("expert", None, "dp"),
            P("expert", None, "dp"),
        ),
        out_specs=P(("dp", "expert"), None),
        check_vma=False,
    )
```

```python
import functools

import jax
import jax.numpy as jnp
from jax import lax
from jax.experimental import pallas as pl
from jax.experimental.pallas import tpu as pltpu
from jax.sharding import PartitionSpec as P

HEAD_DIM = 128
GROUP = 128
TOP = 8
LANES = 128
VMEM_LIMIT = 56 * 2**20
VMEM_SOME = 16 * 2**20
VMEM_MORE = 24 * 2**20
SPARE = 0
SMALL = pl.CostEstimate(flops=1, bytes_accessed=1, transcendentals=0)
F32 = jnp.float32
BF16 = jnp.bfloat16


def front_kernel(
    lengths_ref,
    queries_ref,
    new_kv_ref,
    keys_ref,
    values_ref,
    residual_ref,
    gain_ref,
    routes_ref,
    weights_ref,
    mixed_ref,
    payload_ref,
):
    rows, cache, kv_width = keys_ref.shape
    width = queries_ref.shape[1]
    kv_heads = kv_width // HEAD_DIM
    per = width // kv_width
    scaling = HEAD_DIM ** (-0.5)
    row_id = lax.broadcasted_iota(jnp.int32, (rows, rows * cache), 0)
    lane_id = lax.broadcasted_iota(jnp.int32, (rows, rows * cache), 1)
    bound = jnp.zeros((rows, rows * cache), jnp.int32)
    for r in range(rows):
        bound = jnp.where(row_id == r, r * cache + lengths_ref[r], bound)
    valid = (lane_id >= row_id * cache) & (lane_id < bound)
    earlier, current = [], []
    for j in range(kv_heads):
        span = slice(j * HEAD_DIM, (j + 1) * HEAD_DIM)
        heads = range(j * per, (j + 1) * per)
        queried = jnp.concatenate(
            [queries_ref[:, h * HEAD_DIM : (h + 1) * HEAD_DIM].astype(F32) for h in heads], axis=0
        )
        keys = keys_ref[:, :, span].reshape(rows * cache, HEAD_DIM)
        earlier.append(
            lax.dot_general(
                queried.astype(BF16), keys, (((1,), (1,)), ((), ())), preferred_element_type=F32
            )
        )
        fresh_key = new_kv_ref[:, 0, span].astype(F32)
        current.append(queried.reshape(per, rows, HEAD_DIM) * fresh_key[None])
    earlier = jnp.concatenate(earlier, axis=0).reshape(kv_heads * per, rows, rows * cache)
    earlier = jnp.where(valid[None], earlier * scaling, -1e30)
    current = jnp.sum(jnp.concatenate(current, axis=0), axis=-1, keepdims=True) * scaling
    largest = jnp.maximum(jnp.max(earlier, axis=-1, keepdims=True), current)
    earlier_w = jnp.where(valid[None], jnp.exp(earlier - largest), 0.0)
    current_w = jnp.exp(current - largest)
    inverse = 1.0 / (jnp.sum(earlier_w, axis=-1, keepdims=True) + current_w)
    earlier_p = (earlier_w * inverse).astype(BF16).reshape(kv_heads * per * rows, rows * cache)
    current_p = (current_w * inverse).astype(BF16).astype(F32)
    total = jnp.zeros((rows, HEAD_DIM), F32)
    for j in range(kv_heads):
        span = slice(j * HEAD_DIM, (j + 1) * HEAD_DIM)
        values = values_ref[:, :, span].reshape(rows * cache, HEAD_DIM)
        fresh_value = new_kv_ref[:, 1, span].astype(F32)
        attended = jnp.dot(
            earlier_p[j * per * rows : (j + 1) * per * rows], values, preferred_element_type=F32
        )
        attended = attended.reshape(per, rows, HEAD_DIM)
        attended = attended + current_p[j * per : (j + 1) * per] * fresh_value[None]
        for g in range(per):
            h = j * per + g
            place = slice(h * HEAD_DIM, (h + 1) * HEAD_DIM)
            mixed = (
                residual_ref[:, place].astype(F32) + attended[g].astype(BF16).astype(F32)
            ).astype(BF16)
            mixed_ref[:, place] = mixed
            widened = mixed.astype(F32)
            total = total + widened * widened
    meansq = jnp.sum(total, axis=-1, keepdims=True) * (1.0 / width)
    inverse = lax.rsqrt(meansq + 1e-06)
    payload_ref[:, :width] = (
        mixed_ref[...].astype(F32) * inverse * gain_ref[...].astype(F32).reshape(1, width)
    ).astype(BF16)
    if payload_ref.shape[1] > width:
        shares = weights_ref[...] / jnp.sum(weights_ref[...], axis=1, keepdims=True)
        lane = lax.broadcasted_iota(jnp.int32, (rows, LANES), 1)
        expert = jnp.where(lane < LANES // 2, lane, lane - LANES // 2)
        table = jnp.zeros((rows, LANES), F32)
        for k in range(routes_ref.shape[1]):
            table = table + jnp.where(
                routes_ref[:, k : k + 1] == expert, shares[:, k : k + 1], 0.0
            )
        high = table.astype(BF16).astype(F32)
        payload_ref[:, width:] = jnp.where(lane < LANES // 2, high, table - high).astype(BF16)


def front(queries, new_kv, keys, values, lengths, residual, gain, routes, weights, extra):
    rows, width = queries.shape
    vmem = pl.BlockSpec(memory_space=pltpu.VMEM)
    return pl.pallas_call(
        front_kernel,
        out_shape=(
            jax.ShapeDtypeStruct((rows, width), BF16),
            jax.ShapeDtypeStruct((rows, width + extra), BF16),
        ),
        in_specs=[pl.BlockSpec(memory_space=pltpu.SMEM)] + [vmem] * 8,
        out_specs=(vmem, vmem),
        compiler_params=pltpu.CompilerParams(vmem_limit_bytes=VMEM_LIMIT),
        cost_estimate=SMALL,
        name="front",
    )(lengths, queries, new_kv, keys, values, residual, gain, routes, weights)


def in_vmem(array):
    return pltpu.with_memory_space_constraint(array, pltpu.VMEM)


def in_hbm(array):
    return pltpu.with_memory_space_constraint(array, pltpu.HBM)


def unpack_kernel(firsts, codes_refs, scales_hbms, *refs):
    out_refs, (words_refs, scales_refs, sems, scales_sem) = refs[: len(firsts)], refs[len(firsts) :]

    def copy_scales(n):
        columns = pl.ds(firsts[n], words_refs[n].shape[1])
        return pltpu.make_async_copy(
            scales_hbms[n].at[:, columns], scales_refs[n], scales_sem.at[n]
        )

    def fetch(turn):
        n, group = turns[turn]
        rows = pl.ds(group * GROUP, GROUP)
        columns = pl.ds(firsts[n], words_refs[n].shape[1])
        return pltpu.make_async_copy(
            codes_refs[n].at[rows, columns], words_refs[n].at[rows, :], sems.at[turn]
        )

    turns = [
        (n, group)
        for n, words_ref in enumerate(words_refs)
        for group in range(words_ref.shape[0] // GROUP)
    ]
    ahead = 3
    copy_scales(0).start()
    for turn in range(min(ahead, len(turns))):
        fetch(turn).start()
    for n in range(1, len(firsts)):
        copy_scales(n).start()
    for turn, (n, group) in enumerate(turns):
        words_ref, out_ref = words_refs[n], out_refs[n]
        quarter, width = words_ref.shape
        groups = quarter // GROUP
        step = 256 if width % 256 == 0 else LANES
        if turn + ahead < len(turns):
            fetch(turn + ahead).start()
        if group == 0:
            copy_scales(n).wait()
            scales = scales_refs[n][...].astype(F32)
        fetch(turn).wait()
        for column in range(0, width, step):
            spans = [
                jnp.broadcast_to(
                    scales[k * groups + group : k * groups + group + 1, column : column + step],
                    (16, step),
                ).astype(BF16)
                for k in range(4)
            ]

            def chunk(
                i, carry, group=group, column=column, spans=spans, words_ref=words_ref, out_ref=out_ref
            ):
                start = pl.multiple_of(group * GROUP + i * 16, 16)
                words = words_ref[pl.ds(start, 16), column : column + step].astype(jnp.int32)
                for k in range(4):
                    digit = words if k == 0 else lax.shift_right_logical(words, 4 * k)
                    if k < 3:
                        digit = digit & 15
                    level = digit.astype(F32).astype(BF16) - jnp.asarray(8, BF16)
                    out_ref[pl.ds(k * quarter + start, 16), column : column + step] = (
                        level * spans[k]
                    )
                return carry

            lax.fori_loop(0, GROUP // 16, chunk, 0, unroll=True)


def unpack_weights(*jobs):
    hbm = pl.BlockSpec(memory_space=pltpu.HBM)
    vmem = pl.BlockSpec(memory_space=pltpu.VMEM)
    shapes = [(codes.shape[0], width) for codes, _, _, width in jobs]
    turns = sum(quarter // GROUP for quarter, _ in shapes)
    return pl.pallas_call(
        functools.partial(unpack_kernel, tuple(job[2] for job in jobs)),
        out_shape=[pltpu.VMEM((4 * quarter, width), BF16) for quarter, width in shapes],
        in_specs=[[hbm] * len(jobs)] * 2,
        out_specs=[vmem] * len(jobs),
        scratch_shapes=[
            [pltpu.VMEM(shape, F32) for shape in shapes],
            [pltpu.VMEM((4 * quarter // GROUP, width), BF16) for quarter, width in shapes],
            pltpu.SemaphoreType.DMA((turns,)),
            pltpu.SemaphoreType.DMA((len(jobs),)),
        ],
        compiler_params=pltpu.CompilerParams(vmem_limit_bytes=VMEM_MORE),
        cost_estimate=SMALL,
        name="unpack_weights",
    )([in_hbm(job[0]) for job in jobs], [in_hbm(job[1]) for job in jobs])


def hidden_kernel(place_ref, *refs):
    pieces, (gate_ref, up_ref, out_ref, share_ref, rows_ref) = refs[:-5], refs[-5:]
    depth, width = gate_ref.shape
    block = pieces[0].shape[0]
    count = block * len(pieces)
    for n, piece in enumerate(pieces):
        rows_ref[n * block : (n + 1) * block, :] = piece[:, :depth]
        table = piece[:, depth:].astype(F32)
        lane = lax.broadcasted_iota(jnp.int32, table.shape, 1)
        mine = place_ref[0]
        chosen = (lane == mine) | (lane == mine + LANES // 2)
        share = jnp.sum(jnp.where(chosen, table, 0.0), axis=1, keepdims=True)
        share_ref[n * block : (n + 1) * block, :] = jnp.broadcast_to(share, table.shape)
    step = 256
    for column in range(0, width, step):
        span = slice(column, column + step)
        gate = jnp.dot(rows_ref[...], gate_ref[:, span], preferred_element_type=F32)
        upward = jnp.dot(rows_ref[...], up_ref[:, span], preferred_element_type=F32)
        out_ref[:count, span] = (gate / (1.0 + jnp.exp(-gate)) * upward).astype(BF16)
    if out_ref.shape[0] > count:
        out_ref[count:, :] = jnp.zeros((out_ref.shape[0] - count, width), BF16)


def hidden_units(pieces, w_gate, w_up, place, spare=0):
    block, padded = pieces[0].shape
    count = block * len(pieces)
    depth, width = w_gate.shape
    vmem = pl.BlockSpec(memory_space=pltpu.VMEM)
    return pl.pallas_call(
        hidden_kernel,
        out_shape=(pltpu.VMEM((count + spare, width), BF16), pltpu.VMEM((count, LANES), F32)),
        in_specs=[pl.BlockSpec(memory_space=pltpu.SMEM)] + [vmem] * (len(pieces) + 2),
        out_specs=(vmem, vmem),
        scratch_shapes=[pltpu.VMEM((count, depth), BF16)],
        compiler_params=pltpu.CompilerParams(vmem_limit_bytes=VMEM_SOME),
        cost_estimate=SMALL,
        name="gate_up",
    )(place, *pieces, in_vmem(w_gate), in_vmem(w_up))


def own_down_kernel(side_ref, hidden_ref, weight_refs, out_ref):
    half = hidden_ref.shape[1]
    rows = pl.ds(pl.multiple_of(side_ref[0] * half, half), half)
    step = 256
    for n, weight_ref in enumerate(weight_refs):
        width = weight_ref.shape[1]
        for column in range(0, width, step):
            out_ref[:, n * width + column : n * width + column + step] = jnp.dot(
                hidden_ref[: out_ref.shape[0]],
                weight_ref[rows, column : column + step],
                preferred_element_type=F32,
            )


def own_down(side, hidden, weights, count):
    width = sum(weight.shape[1] for weight in weights)
    vmem = pl.BlockSpec(memory_space=pltpu.VMEM)
    return pl.pallas_call(
        own_down_kernel,
        out_shape=pltpu.VMEM((count, width), F32),
        in_specs=[pl.BlockSpec(memory_space=pltpu.SMEM), vmem, [vmem] * len(weights)],
        out_specs=vmem,
        compiler_params=pltpu.CompilerParams(vmem_limit_bytes=VMEM_SOME),
        cost_estimate=SMALL,
        name="down_own",
    )(side, in_vmem(hidden), [in_vmem(weight) for weight in weights])


def cuts(rows, parts):
    size = rows.shape[0] // parts
    return [rows[n * size : (n + 1) * size] for n in range(parts)]


def peer_down_kernel(
    side_ref, partial_ref, hidden_ref, weight_refs, share_ref, *out_refs
):
    count, half = partial_ref.shape[0], hidden_ref.shape[1]
    rows = pl.ds(pl.multiple_of((1 - side_ref[0]) * half, half), half)
    step = 256
    for n, weight_ref in enumerate(weight_refs):
        width = weight_ref.shape[1]
        for column in range(0, width, step):
            span = slice(n * width + column, n * width + column + step)
            produced = partial_ref[:, span] + jnp.dot(
                hidden_ref[:count],
                weight_ref[rows, column : column + step],
                preferred_element_type=F32,
            )
            result = produced.astype(BF16).astype(F32) * share_ref[:, :1]
            for out_ref, cut in zip(out_refs, cuts(result, len(out_refs))):
                out_ref[:, span] = cut.astype(BF16)


def peer_down(side, partial, hidden, weights, share, parts):
    count, width = partial.shape
    vmem = pl.BlockSpec(memory_space=pltpu.VMEM)
    return pl.pallas_call(
        peer_down_kernel,
        out_shape=(pltpu.VMEM((count // parts, width), BF16),) * parts,
        in_specs=[pl.BlockSpec(memory_space=pltpu.SMEM), vmem, vmem, [vmem] * len(weights), vmem],
        out_specs=(vmem,) * parts,
        compiler_params=pltpu.CompilerParams(vmem_limit_bytes=VMEM_SOME),
        cost_estimate=SMALL,
        name="down_peer",
    )(side, in_vmem(partial), hidden, [in_vmem(weight) for weight in weights], in_vmem(share))


def add_kernel(terms, *refs):
    term_refs, out_refs = refs[:terms], refs[terms:]
    total = term_refs[0][...].astype(F32)
    for term_ref in term_refs[1:]:
        total = total + term_ref[...].astype(F32)
    width = total.shape[1]
    for out_ref, cut in zip(out_refs, cuts(total, len(out_refs))):
        out_ref[:, :width] = cut.astype(out_ref.dtype)
        if out_ref.shape[1] > width:
            out_ref[:, width:] = jnp.zeros((cut.shape[0], out_ref.shape[1] - width), out_ref.dtype)


def add_and_cut(kept, arrived, parts, spare=0):
    count, width = kept[0].shape
    vmem = pl.BlockSpec(memory_space=pltpu.VMEM)
    shape = pltpu.VMEM((count // parts, width + spare), BF16)
    return pl.pallas_call(
        functools.partial(add_kernel, len(kept + arrived)),
        out_shape=(shape,) * parts,
        in_specs=[vmem] * len(kept + arrived),
        out_specs=(vmem,) * parts,
        compiler_params=pltpu.CompilerParams(vmem_limit_bytes=VMEM_SOME),
        cost_estimate=SMALL,
        name="add_and_cut",
    )(*[in_vmem(part) for part in kept], *arrived)


def join_kernel(parts, far_ref, *refs):
    near_refs, out_refs = refs[:-parts], refs[-parts:]
    size = far_ref.shape[0] // parts
    near = near_refs[0][...].astype(F32)
    for near_ref in near_refs[1:]:
        near = near + near_ref[...].astype(F32)
    far = far_ref[:, : near.shape[1]].astype(F32)
    for n, out_ref in enumerate(out_refs):
        rows = slice(n * size, (n + 1) * size)
        out_ref[...] = jnp.concatenate([near[rows], far[rows]], axis=0).astype(BF16)


def join(near, far, parts):
    count, width = near[0].shape
    vmem = pl.BlockSpec(memory_space=pltpu.VMEM)
    return pl.pallas_call(
        functools.partial(join_kernel, parts),
        out_shape=(pltpu.VMEM((2 * count // parts, width), BF16),) * parts,
        in_specs=[vmem] * (1 + len(near)),
        out_specs=(vmem,) * parts,
        compiler_params=pltpu.CompilerParams(vmem_limit_bytes=VMEM_SOME),
        cost_estimate=SMALL,
        name="join",
    )(far, *near)


def finish_kernel(side_ref, mixed_ref, *refs):
    block_refs, out_ref = refs[:-1], refs[-1]
    rows, width = mixed_ref.shape
    total = block_refs[0][...].astype(F32)
    for block_ref in block_refs[1:]:
        total = total + block_ref[...].astype(F32)
    near, far = total[:rows], total[rows:]
    first = side_ref[0] == 0
    half = width // 2
    for n, part in enumerate((jnp.where(first, near, far), jnp.where(first, far, near))):
        span = slice(n * half, (n + 1) * half)
        out_ref[:, span] = (mixed_ref[:, span].astype(F32) + part).astype(BF16)


def finish(side, mixed, blocks):
    vmem = pl.BlockSpec(memory_space=pltpu.VMEM)
    return pl.pallas_call(
        finish_kernel,
        out_shape=jax.ShapeDtypeStruct(mixed.shape, BF16),
        in_specs=[pl.BlockSpec(memory_space=pltpu.SMEM)] + [vmem] * (1 + len(blocks)),
        out_specs=vmem,
        compiler_params=pltpu.CompilerParams(vmem_limit_bytes=VMEM_SOME),
        name="finish",
    )(side, mixed, *blocks)


def dense(payload, mixed, codes):
    gate_codes, gate_scales, up_codes, up_scales, down_codes, down_scales = codes
    groups = lax.axis_size("dp")
    experts = lax.axis_size("expert")
    devices = groups * experts
    core, line, layer, plane = 1, 2, 4, experts
    layers = experts // layer
    side = lax.axis_index("dp").reshape(1).astype(jnp.int32)
    place = lax.axis_index("expert").reshape(1).astype(jnp.int32)

    def swap(block, offset):
        return lax.ppermute(block, ("dp", "expert"), [(i, i ^ offset) for i in range(devices)])

    side, place, gate_scales, down_scales, payload = lax.optimization_barrier(
        (side, place, gate_scales, down_scales, payload)
    )
    units = gate_codes.shape[1]
    half = down_codes.shape[1] // 2
    blocks = [swap(payload, z * layer) for z in range(1, layers)]
    w_gate, w_down = unpack_weights(
        (gate_codes, gate_scales, 0, units), (down_codes, down_scales, 0, half)
    )
    blocks, w_gate = lax.optimization_barrier((blocks, w_gate))
    stack = jnp.concatenate([payload] + blocks, axis=0)
    up_scales, stack = lax.optimization_barrier((up_scales, stack))
    beside, above, stack_pair = swap(stack, plane), swap(stack, line), swap(stack, core)
    (w_up,) = unpack_weights((up_codes, up_scales, 0, units))
    above, stack_pair, w_up = lax.optimization_barrier((above, stack_pair, w_up))
    across, above_pair = swap(above, plane), swap(above, core)
    above_pair, beside = lax.optimization_barrier((above_pair, beside))
    beside_pair = swap(beside, core)
    hidden_own, share_own = hidden_units(
        [stack, stack_pair, above, above_pair], w_gate, w_up, place, SPARE
    )
    other_peer = swap(hidden_own, plane)
    down_scales, hidden_own = lax.optimization_barrier((down_scales, hidden_own))
    (w_more,) = unpack_weights((down_codes, down_scales, half, half))
    across, w_more = lax.optimization_barrier((across, w_more))
    w_down = [w_down, w_more]
    hidden_other, share_other = hidden_units(
        [beside, beside_pair, across, swap(across, core)], w_gate, w_up, place
    )
    own_peer = swap(hidden_other, plane)

    count = share_own.shape[0]
    partial_other = own_down(side, hidden_other, w_down, count)
    partial_own = own_down(side, hidden_own, w_down, count)
    def over_core_and_line(keep_near, send_near, keep_far, send_far):
        (onward,) = add_and_cut([keep_far], [swap(send_far, core)], 1)
        return [keep_near, swap(send_near, core), swap(onward, line)]

    other = over_core_and_line(
        *peer_down(side, partial_other, other_peer, w_down, share_other, 4)
    )
    (onward,) = add_and_cut(other[:1], other[1:], 1, LANES)
    far = swap(onward, plane)
    near = over_core_and_line(*peer_down(side, partial_own, own_peer, w_down, share_own, 4))
    blocks = join([in_vmem(near[0])] + near[1:], far, layers)
    blocks = [blocks[0]] + [swap(blocks[z], z * layer) for z in range(1, layers)]
    return finish(side, mixed, blocks)


def slot_table(routes, experts, capacity):
    flattened = routes.reshape(-1)
    onehot = (flattened[:, None] == jnp.arange(experts, dtype=jnp.int32)[None, :]).astype(jnp.int32)
    ranking = jnp.sum((jnp.cumsum(onehot, axis=0) - 1) * onehot, axis=1)
    return (flattened * capacity + ranking).reshape(routes.shape)


def dispatch(block, slots, width):
    targets = jnp.arange(width, dtype=jnp.int32)
    placing = jnp.sum((slots[None, :, :] == targets[:, None, None]).astype(F32), axis=2)
    return jnp.dot(placing.astype(BF16), block, preferred_element_type=F32).astype(BF16)


def unpack(codes, scales):
    quarter, width = codes.shape
    divisors = jnp.array([1.0, 1.0 / 16, 1.0 / 256, 1.0 / 4096], F32)[:, None, None]
    lifted = jnp.floor(codes[None, :, :] * divisors)
    levels = lifted - 16.0 * jnp.floor(lifted * (1.0 / 16)) - 8.0
    height = 4 * quarter
    grouped = levels.reshape(height // GROUP, GROUP, width) * scales.astype(F32)[:, None, :]
    return grouped.reshape(height, width).astype(BF16)


def routed(normed, mixed, routes, route_weights, codes, capacity):
    gate_codes, gate_scales, up_codes, up_scales, down_codes, down_scales = codes
    experts = lax.axis_size("expert")
    groups = lax.axis_size("dp")
    row_count, width = mixed.shape
    own_slots = slot_table(routes, experts, capacity)
    w_gate = unpack(gate_codes, gate_scales)
    w_up = unpack(up_codes, up_scales)
    w_down = unpack(down_codes, down_scales)
    local_units = w_gate.shape[1]
    peer_rows = lax.all_gather(normed, "dp", axis=0, tiled=True).reshape(groups, row_count, width)
    peer_routes = lax.all_gather(routes, "dp", axis=0, tiled=True).reshape(groups, row_count, TOP)

    def build(block, table):
        return dispatch(block, slot_table(table, experts, capacity), experts * capacity)

    outgoing = jax.vmap(build)(peer_rows, peer_routes).reshape(groups, experts, capacity, width)
    items = lax.all_to_all(outgoing, "expert", split_axis=1, concat_axis=1, tiled=True)
    inputs = items.reshape(-1, width)
    gate = jnp.dot(inputs, w_gate, preferred_element_type=F32)
    upward = jnp.dot(inputs, w_up, preferred_element_type=F32)
    hidden = (jax.nn.silu(gate) * upward).astype(BF16).reshape(-1, local_units)
    produced = jnp.dot(
        lax.all_gather(hidden, "dp", axis=1, tiled=True), w_down, preferred_element_type=F32
    ).astype(BF16)
    produced = produced.reshape(groups, -1, produced.shape[1])
    returned = lax.all_to_all(
        lax.all_to_all(produced, "dp", split_axis=0, concat_axis=2, tiled=True),
        "expert",
        split_axis=1,
        concat_axis=0,
        tiled=True,
    )
    shares = route_weights / jnp.sum(route_weights, axis=1, keepdims=True)
    targets = jnp.arange(experts * capacity, dtype=jnp.int32)
    spreading = jnp.sum(
        jnp.where(own_slots[:, :, None] == targets[None, None, :], shares[:, :, None], 0.0), axis=1
    )
    combined = jnp.dot(
        spreading, returned.reshape(-1, width).astype(F32), precision=lax.Precision.HIGHEST
    )
    return (mixed.astype(F32) + combined).astype(BF16)


def body(
    queries,
    new_kv,
    cache_keys,
    cache_values,
    lengths,
    residual,
    norm_gain,
    routes,
    route_weights,
    *packed,
):
    experts = lax.axis_size("expert")
    groups = lax.axis_size("dp")
    row_count = queries.shape[0]
    capacity = min(row_count, max(2, 2 * row_count * TOP // experts))
    every = (
        capacity == row_count
        and groups == 2
        and experts <= LANES // 2
        and experts % 4 == 0
        and experts & (experts - 1) == 0
    )
    mixed, payload = front(
        queries,
        new_kv,
        cache_keys,
        cache_values,
        lengths,
        residual,
        norm_gain,
        routes,
        route_weights,
        LANES if every else 0,
    )
    codes = [array[0] for array in packed]
    if every:
        return dense(payload, mixed, codes)
    return routed(payload, mixed, routes, route_weights, codes, capacity)


def solution(mesh):
    return jax.shard_map(
        body,
        mesh=mesh,
        in_specs=(
            P(("dp", "expert"), None),
            P(("dp", "expert"), None, None),
            P(("dp", "expert"), None, None),
            P(("dp", "expert"), None, None),
            P(("dp", "expert")),
            P(("dp", "expert"), None),
            P(),
            P(("dp", "expert"), None),
            P(("dp", "expert"), None),
            P("expert", None, "dp"),
            P("expert", None, "dp"),
            P("expert", None, "dp"),
            P("expert", None, "dp"),
            P("expert", None, "dp"),
            P("expert", None, "dp"),
        ),
        out_specs=P(("dp", "expert"), None),
        check_vma=False,
    )
```

```python
import functools

import jax
import jax.numpy as jnp
from jax import lax
from jax.experimental import pallas as pl
from jax.experimental.pallas import tpu as pltpu
from jax.sharding import PartitionSpec as P

HEAD_DIM = 128
GROUP = 128
TOP = 8
LANES = 128
VMEM_LIMIT = 56 * 2**20
VMEM_SOME = 16 * 2**20
VMEM_MORE = 24 * 2**20
SPARE = 16
SMALL = pl.CostEstimate(flops=1, bytes_accessed=1, transcendentals=0)
F32 = jnp.float32
BF16 = jnp.bfloat16


def front_kernel(
    lengths_ref,
    queries_ref,
    new_kv_ref,
    keys_ref,
    values_ref,
    residual_ref,
    gain_ref,
    routes_ref,
    weights_ref,
    mixed_ref,
    payload_ref,
):
    rows, cache, kv_width = keys_ref.shape
    width = queries_ref.shape[1]
    kv_heads = kv_width // HEAD_DIM
    per = width // kv_width
    scaling = HEAD_DIM ** (-0.5)
    row_id = lax.broadcasted_iota(jnp.int32, (rows, rows * cache), 0)
    lane_id = lax.broadcasted_iota(jnp.int32, (rows, rows * cache), 1)
    bound = jnp.zeros((rows, rows * cache), jnp.int32)
    for r in range(rows):
        bound = jnp.where(row_id == r, r * cache + lengths_ref[r], bound)
    valid = (lane_id >= row_id * cache) & (lane_id < bound)
    earlier, current = [], []
    for j in range(kv_heads):
        span = slice(j * HEAD_DIM, (j + 1) * HEAD_DIM)
        heads = range(j * per, (j + 1) * per)
        queried = jnp.concatenate(
            [queries_ref[:, h * HEAD_DIM : (h + 1) * HEAD_DIM].astype(F32) for h in heads], axis=0
        )
        keys = keys_ref[:, :, span].reshape(rows * cache, HEAD_DIM)
        earlier.append(
            lax.dot_general(
                queried.astype(BF16), keys, (((1,), (1,)), ((), ())), preferred_element_type=F32
            )
        )
        fresh_key = new_kv_ref[:, 0, span].astype(F32)
        current.append(queried.reshape(per, rows, HEAD_DIM) * fresh_key[None])
    earlier = jnp.concatenate(earlier, axis=0).reshape(kv_heads * per, rows, rows * cache)
    earlier = jnp.where(valid[None], earlier * scaling, -1e30)
    current = jnp.sum(jnp.concatenate(current, axis=0), axis=-1, keepdims=True) * scaling
    largest = jnp.maximum(jnp.max(earlier, axis=-1, keepdims=True), current)
    earlier_w = jnp.where(valid[None], jnp.exp(earlier - largest), 0.0)
    current_w = jnp.exp(current - largest)
    inverse = 1.0 / (jnp.sum(earlier_w, axis=-1, keepdims=True) + current_w)
    earlier_p = (earlier_w * inverse).astype(BF16).reshape(kv_heads * per * rows, rows * cache)
    current_p = (current_w * inverse).astype(BF16).astype(F32)
    total = jnp.zeros((rows, HEAD_DIM), F32)
    for j in range(kv_heads):
        span = slice(j * HEAD_DIM, (j + 1) * HEAD_DIM)
        values = values_ref[:, :, span].reshape(rows * cache, HEAD_DIM)
        fresh_value = new_kv_ref[:, 1, span].astype(F32)
        attended = jnp.dot(
            earlier_p[j * per * rows : (j + 1) * per * rows], values, preferred_element_type=F32
        )
        attended = attended.reshape(per, rows, HEAD_DIM)
        attended = attended + current_p[j * per : (j + 1) * per] * fresh_value[None]
        for g in range(per):
            h = j * per + g
            place = slice(h * HEAD_DIM, (h + 1) * HEAD_DIM)
            mixed = (
                residual_ref[:, place].astype(F32) + attended[g].astype(BF16).astype(F32)
            ).astype(BF16)
            mixed_ref[:, place] = mixed
            widened = mixed.astype(F32)
            total = total + widened * widened
    meansq = jnp.sum(total, axis=-1, keepdims=True) * (1.0 / width)
    inverse = lax.rsqrt(meansq + 1e-06)
    payload_ref[:, :width] = (
        mixed_ref[...].astype(F32) * inverse * gain_ref[...].astype(F32).reshape(1, width)
    ).astype(BF16)
    if payload_ref.shape[1] > width:
        shares = weights_ref[...] / jnp.sum(weights_ref[...], axis=1, keepdims=True)
        lane = lax.broadcasted_iota(jnp.int32, (rows, LANES), 1)
        expert = jnp.where(lane < LANES // 2, lane, lane - LANES // 2)
        table = jnp.zeros((rows, LANES), F32)
        for k in range(routes_ref.shape[1]):
            table = table + jnp.where(
                routes_ref[:, k : k + 1] == expert, shares[:, k : k + 1], 0.0
            )
        high = table.astype(BF16).astype(F32)
        payload_ref[:, width:] = jnp.where(lane < LANES // 2, high, table - high).astype(BF16)


def front(queries, new_kv, keys, values, lengths, residual, gain, routes, weights, extra):
    rows, width = queries.shape
    vmem = pl.BlockSpec(memory_space=pltpu.VMEM)
    return pl.pallas_call(
        front_kernel,
        out_shape=(
            jax.ShapeDtypeStruct((rows, width), BF16),
            jax.ShapeDtypeStruct((rows, width + extra), BF16),
        ),
        in_specs=[pl.BlockSpec(memory_space=pltpu.SMEM)] + [vmem] * 8,
        out_specs=(vmem, vmem),
        compiler_params=pltpu.CompilerParams(vmem_limit_bytes=VMEM_LIMIT),
        cost_estimate=SMALL,
        name="front",
    )(lengths, queries, new_kv, keys, values, residual, gain, routes, weights)


def in_vmem(array):
    return pltpu.with_memory_space_constraint(array, pltpu.VMEM)


def in_hbm(array):
    return pltpu.with_memory_space_constraint(array, pltpu.HBM)


def unpacking(
    firsts, codes_refs, scales_hbms, out_refs, words_refs, scales_refs, sems, scales_sem, ahead
):
    def copy_scales(n):
        columns = pl.ds(firsts[n], words_refs[n].shape[1])
        return pltpu.make_async_copy(
            scales_hbms[n].at[:, columns], scales_refs[n], scales_sem.at[n]
        )

    def fetch(turn):
        n, group = turns[turn]
        rows = pl.ds(group * GROUP, GROUP)
        columns = pl.ds(firsts[n], words_refs[n].shape[1])
        return pltpu.make_async_copy(
            codes_refs[n].at[rows, columns], words_refs[n].at[rows, :], sems.at[turn]
        )

    turns = [
        (n, group)
        for n, words_ref in enumerate(words_refs)
        for group in range(words_ref.shape[0] // GROUP)
    ]
    def start():
        copy_scales(0).start()
        for turn in range(min(ahead, len(turns))):
            fetch(turn).start()
        for n in range(1, len(firsts)):
            copy_scales(n).start()

    def run():
        for turn, (n, group) in enumerate(turns):
            words_ref, out_ref = words_refs[n], out_refs[n]
            quarter, width = words_ref.shape
            groups = quarter // GROUP
            step = 256 if width % 256 == 0 else LANES
            if turn + ahead < len(turns):
                fetch(turn + ahead).start()
            if group == 0:
                copy_scales(n).wait()
                scales = scales_refs[n][...].astype(F32)
            fetch(turn).wait()
            for column in range(0, width, step):
                spans = [
                    jnp.broadcast_to(
                        scales[k * groups + group : k * groups + group + 1, column : column + step],
                        (16, step),
                    ).astype(BF16)
                    for k in range(4)
                ]

                def chunk(
                    i, carry, group=group, column=column, spans=spans, words_ref=words_ref, out_ref=out_ref
                ):
                    start = pl.multiple_of(group * GROUP + i * 16, 16)
                    words = words_ref[pl.ds(start, 16), column : column + step].astype(jnp.int32)
                    for k in range(4):
                        digit = words if k == 0 else lax.shift_right_logical(words, 4 * k)
                        if k < 3:
                            digit = digit & 15
                        level = digit.astype(F32).astype(BF16) - jnp.asarray(8, BF16)
                        out_ref[pl.ds(k * quarter + start, 16), column : column + step] = (
                            level * spans[k]
                        )
                    return carry

                lax.fori_loop(0, GROUP // 16, chunk, 0, unroll=True)

    return start, run


def unpack_kernel(firsts, codes_refs, scales_hbms, *refs):
    start, run = unpacking(
        firsts, codes_refs, scales_hbms, refs[: len(firsts)], *refs[len(firsts) :], 3
    )
    start()
    run()


def unpack_shapes(jobs):
    shapes = [(codes.shape[0], width) for codes, _, _, width in jobs]
    turns = sum(quarter // GROUP for quarter, _ in shapes)
    outs = [pltpu.VMEM((4 * quarter, width), BF16) for quarter, width in shapes]
    scratch = [
        [pltpu.VMEM(shape, F32) for shape in shapes],
        [pltpu.VMEM((4 * quarter // GROUP, width), BF16) for quarter, width in shapes],
        pltpu.SemaphoreType.DMA((turns,)),
        pltpu.SemaphoreType.DMA((len(jobs),)),
    ]
    return outs, scratch


def unpack_weights(*jobs):
    hbm = pl.BlockSpec(memory_space=pltpu.HBM)
    vmem = pl.BlockSpec(memory_space=pltpu.VMEM)
    outs, scratch = unpack_shapes(jobs)
    return pl.pallas_call(
        functools.partial(unpack_kernel, tuple(job[2] for job in jobs)),
        out_shape=outs,
        in_specs=[[hbm] * len(jobs)] * 2,
        out_specs=[vmem] * len(jobs),
        scratch_shapes=scratch,
        compiler_params=pltpu.CompilerParams(vmem_limit_bytes=VMEM_MORE),
        cost_estimate=SMALL,
        name="unpack_weights",
    )([in_hbm(job[0]) for job in jobs], [in_hbm(job[1]) for job in jobs])


def hidden_kernel(firsts, place_ref, pieces, gate_ref, up_ref, codes_refs, scales_hbms, *refs):
    extra = len(firsts)
    out_ref, share_ref, *refs = refs
    more_refs, (rows_ref, *refs) = refs[:extra], refs[extra:]
    if extra:
        start, run = unpacking(firsts, codes_refs, scales_hbms, more_refs, *refs, 4)
        start()
    depth, width = gate_ref.shape
    block = pieces[0].shape[0]
    count = block * len(pieces)
    for n, piece in enumerate(pieces):
        rows_ref[n * block : (n + 1) * block, :] = piece[:, :depth]
    step = 256
    for column in range(0, width, step):
        span = slice(column, column + step)
        gate = jnp.dot(rows_ref[...], gate_ref[:, span], preferred_element_type=F32)
        upward = jnp.dot(rows_ref[...], up_ref[:, span], preferred_element_type=F32)
        out_ref[:count, span] = (gate / (1.0 + jnp.exp(-gate)) * upward).astype(BF16)
    if out_ref.shape[0] > count:
        out_ref[count:, :] = jnp.zeros((out_ref.shape[0] - count, width), BF16)
    for n, piece in enumerate(pieces):
        table = piece[:, depth:].astype(F32)
        lane = lax.broadcasted_iota(jnp.int32, table.shape, 1)
        mine = place_ref[0]
        chosen = (lane == mine) | (lane == mine + LANES // 2)
        share = jnp.sum(jnp.where(chosen, table, 0.0), axis=1, keepdims=True)
        share_ref[n * block : (n + 1) * block, :] = jnp.broadcast_to(share, table.shape)
    if extra:
        run()


def hidden_units(pieces, w_gate, w_up, place, spare=0, jobs=()):
    block, padded = pieces[0].shape
    count = block * len(pieces)
    depth, width = w_gate.shape
    hbm = pl.BlockSpec(memory_space=pltpu.HBM)
    vmem = pl.BlockSpec(memory_space=pltpu.VMEM)
    outs, scratch = unpack_shapes(jobs)
    return pl.pallas_call(
        functools.partial(hidden_kernel, tuple(job[2] for job in jobs)),
        out_shape=[
            pltpu.VMEM((count + spare, width), BF16),
            pltpu.VMEM((count, LANES), F32),
            *outs,
        ],
        in_specs=[
            pl.BlockSpec(memory_space=pltpu.SMEM),
            [vmem] * len(pieces),
            vmem,
            vmem,
            [hbm] * len(jobs),
            [hbm] * len(jobs),
        ],
        out_specs=[vmem] * (2 + len(jobs)),
        scratch_shapes=[pltpu.VMEM((count, depth), BF16), *(scratch if jobs else [])],
        compiler_params=pltpu.CompilerParams(vmem_limit_bytes=VMEM_MORE),
        cost_estimate=SMALL,
        name="gate_up",
    )(
        place,
        list(pieces),
        in_vmem(w_gate),
        in_vmem(w_up),
        [in_hbm(job[0]) for job in jobs],
        [in_hbm(job[1]) for job in jobs],
    )


def own_down_kernel(side_ref, hidden_ref, weight_refs, out_ref):
    half = hidden_ref.shape[1]
    rows = pl.ds(pl.multiple_of(side_ref[0] * half, half), half)
    step = 256
    for n, weight_ref in enumerate(weight_refs):
        width = weight_ref.shape[1]
        for column in range(0, width, step):
            out_ref[:, n * width + column : n * width + column + step] = jnp.dot(
                hidden_ref[: out_ref.shape[0]],
                weight_ref[rows, column : column + step],
                preferred_element_type=F32,
            )


def own_down(side, hidden, weights, count):
    width = sum(weight.shape[1] for weight in weights)
    vmem = pl.BlockSpec(memory_space=pltpu.VMEM)
    return pl.pallas_call(
        own_down_kernel,
        out_shape=pltpu.VMEM((count, width), F32),
        in_specs=[pl.BlockSpec(memory_space=pltpu.SMEM), vmem, [vmem] * len(weights)],
        out_specs=vmem,
        compiler_params=pltpu.CompilerParams(vmem_limit_bytes=VMEM_SOME),
        cost_estimate=SMALL,
        name="down_own",
    )(side, in_vmem(hidden), [in_vmem(weight) for weight in weights])


def peer_down_kernel(side_ref, partial_ref, hidden_ref, weight_refs, share_ref, *out_refs):
    count, half = partial_ref.shape[0], hidden_ref.shape[1]
    rows = pl.ds(pl.multiple_of((1 - side_ref[0]) * half, half), half)
    step = 256
    cut = count // len(out_refs)
    for n, weight_ref in enumerate(weight_refs):
        width = weight_ref.shape[1]
        for column in range(0, width, step):
            span = slice(n * width + column, n * width + column + step)
            produced = partial_ref[:, span] + jnp.dot(
                hidden_ref[:count],
                weight_ref[rows, column : column + step],
                preferred_element_type=F32,
            )
            result = (produced.astype(BF16).astype(F32) * share_ref[:, :1]).astype(BF16)
            for m, out_ref in enumerate(out_refs):
                out_ref[:, span] = result[m * cut : (m + 1) * cut]


def peer_down(side, partial, hidden, weights, share, parts):
    count, width = partial.shape
    vmem = pl.BlockSpec(memory_space=pltpu.VMEM)
    return pl.pallas_call(
        peer_down_kernel,
        out_shape=(pltpu.VMEM((count // parts, width), BF16),) * parts,
        in_specs=[pl.BlockSpec(memory_space=pltpu.SMEM), vmem, vmem, [vmem] * len(weights), vmem],
        out_specs=(vmem,) * parts,
        compiler_params=pltpu.CompilerParams(vmem_limit_bytes=VMEM_SOME),
        cost_estimate=SMALL,
        name="down_peer",
    )(side, in_vmem(partial), hidden, [in_vmem(weight) for weight in weights], in_vmem(share))


def halve_kernel(terms, *refs):
    term_refs, out_refs = refs[:terms], refs[terms:]
    total = term_refs[0][...].astype(F32)
    for term_ref in term_refs[1:]:
        total = total + term_ref[...].astype(F32)
    size = total.shape[0] // len(out_refs)
    for n, out_ref in enumerate(out_refs):
        out_ref[...] = total[n * size : (n + 1) * size].astype(out_ref.dtype)


def add_and_cut(kept, arrived, parts):
    count, width = kept[0].shape
    vmem = pl.BlockSpec(memory_space=pltpu.VMEM)
    shape = pltpu.VMEM((count // parts, width), BF16)
    return pl.pallas_call(
        functools.partial(halve_kernel, len(kept + arrived)),
        out_shape=(shape,) * parts,
        in_specs=[vmem] * len(kept + arrived),
        out_specs=(vmem,) * parts,
        compiler_params=pltpu.CompilerParams(vmem_limit_bytes=VMEM_SOME),
        cost_estimate=SMALL,
        name="add_and_cut",
    )(*[in_vmem(part) for part in kept], *arrived)


def join_kernel(parts, far_ref, *refs):
    near_refs, out_refs = refs[:-parts], refs[-parts:]
    size = far_ref.shape[0] // parts
    near = near_refs[0][...].astype(F32)
    for near_ref in near_refs[1:]:
        near = near + near_ref[...].astype(F32)
    far = far_ref[...].astype(F32)
    for n, out_ref in enumerate(out_refs):
        rows = slice(n * size, (n + 1) * size)
        out_ref[...] = jnp.concatenate([near[rows], far[rows]], axis=0).astype(BF16)


def join(near, far, parts):
    count, width = far.shape
    vmem = pl.BlockSpec(memory_space=pltpu.VMEM)
    return pl.pallas_call(
        functools.partial(join_kernel, parts),
        out_shape=(pltpu.VMEM((2 * count // parts, width), BF16),) * parts,
        in_specs=[vmem] * (1 + len(near)),
        out_specs=(vmem,) * parts,
        compiler_params=pltpu.CompilerParams(vmem_limit_bytes=VMEM_SOME),
        cost_estimate=SMALL,
        name="join",
    )(far, *near)


def finish_kernel(side_ref, mixed_ref, *refs):
    block_refs, out_ref = refs[:-1], refs[-1]
    rows, width = mixed_ref.shape
    total = block_refs[0][...].astype(F32)
    for block_ref in block_refs[1:]:
        total = total + block_ref[...].astype(F32)
    near, far = total[:rows], total[rows:]
    first = side_ref[0] == 0
    half = width // 2
    for n, part in enumerate((jnp.where(first, near, far), jnp.where(first, far, near))):
        span = slice(n * half, (n + 1) * half)
        out_ref[:, span] = (mixed_ref[:, span].astype(F32) + part).astype(BF16)


def finish(side, mixed, blocks):
    vmem = pl.BlockSpec(memory_space=pltpu.VMEM)
    return pl.pallas_call(
        finish_kernel,
        out_shape=jax.ShapeDtypeStruct(mixed.shape, BF16),
        in_specs=[pl.BlockSpec(memory_space=pltpu.SMEM)] + [vmem] * (1 + len(blocks)),
        out_specs=vmem,
        compiler_params=pltpu.CompilerParams(vmem_limit_bytes=VMEM_SOME),
        name="finish",
    )(side, mixed, *blocks)


def dense(payload, mixed, codes):
    gate_codes, gate_scales, up_codes, up_scales, down_codes, down_scales = codes
    groups = lax.axis_size("dp")
    experts = lax.axis_size("expert")
    devices = groups * experts
    core, line, layer, plane = 1, 2, 4, experts
    layers = experts // layer
    side = lax.axis_index("dp").reshape(1).astype(jnp.int32)
    place = lax.axis_index("expert").reshape(1).astype(jnp.int32)

    def swap(block, offset):
        return lax.ppermute(block, ("dp", "expert"), [(i, i ^ offset) for i in range(devices)])

    side, place, gate_scales, down_scales, payload = lax.optimization_barrier(
        (side, place, gate_scales, down_scales, payload)
    )
    units = gate_codes.shape[1]
    half = down_codes.shape[1] // 2
    blocks = [swap(payload, z * layer) for z in range(1, layers)]
    w_gate, w_down = unpack_weights(
        (gate_codes, gate_scales, 0, units), (down_codes, down_scales, 0, half)
    )
    blocks, w_gate = lax.optimization_barrier((blocks, w_gate))
    stack = jnp.concatenate([payload] + blocks, axis=0)
    up_scales, stack = lax.optimization_barrier((up_scales, stack))
    beside, above, stack_pair = swap(stack, plane), swap(stack, line), swap(stack, core)
    (w_up,) = unpack_weights((up_codes, up_scales, 0, units))
    above, stack_pair, w_up = lax.optimization_barrier((above, stack_pair, w_up))
    across, above_pair = swap(above, plane), swap(above, core)
    above_pair, beside = lax.optimization_barrier((above_pair, beside))
    beside_pair = swap(beside, core)
    hidden_own, share_own, w_more = hidden_units(
        [stack, stack_pair, above, above_pair],
        w_gate,
        w_up,
        place,
        SPARE,
        [(down_codes, down_scales, half, half)],
    )
    other_peer = swap(hidden_own, plane)
    across, w_more = lax.optimization_barrier((across, w_more))
    w_down = [w_down, w_more]
    hidden_other, share_other = hidden_units(
        [beside, beside_pair, across, swap(across, core)], w_gate, w_up, place
    )
    own_peer = swap(hidden_other, plane)

    count = share_own.shape[0]
    partial_other = own_down(side, hidden_other, w_down, count)
    partial_own = own_down(side, hidden_own, w_down, count)
    keep, send = peer_down(side, partial_other, other_peer, w_down, share_other, 2)
    keep, send = add_and_cut([keep], [swap(send, line)], 2)
    (onward,) = add_and_cut([keep], [swap(send, core)], 1)
    far = swap(onward, plane)
    keep_near, send_near, keep_far, send_far = peer_down(
        side, partial_own, own_peer, w_down, share_own, 4
    )
    (onward,) = add_and_cut([keep_far], [swap(send_far, core)], 1)
    near = [in_vmem(keep_near), swap(send_near, core), swap(onward, line)]
    blocks = join(near, far, layers)
    blocks = [blocks[0]] + [swap(blocks[z], z * layer) for z in range(1, layers)]
    return finish(side, mixed, blocks)


def slot_table(routes, experts, capacity):
    flattened = routes.reshape(-1)
    onehot = (flattened[:, None] == jnp.arange(experts, dtype=jnp.int32)[None, :]).astype(jnp.int32)
    ranking = jnp.sum((jnp.cumsum(onehot, axis=0) - 1) * onehot, axis=1)
    return (flattened * capacity + ranking).reshape(routes.shape)


def dispatch(block, slots, width):
    targets = jnp.arange(width, dtype=jnp.int32)
    placing = jnp.sum((slots[None, :, :] == targets[:, None, None]).astype(F32), axis=2)
    return jnp.dot(placing.astype(BF16), block, preferred_element_type=F32).astype(BF16)


def unpack(codes, scales):
    quarter, width = codes.shape
    divisors = jnp.array([1.0, 1.0 / 16, 1.0 / 256, 1.0 / 4096], F32)[:, None, None]
    lifted = jnp.floor(codes[None, :, :] * divisors)
    levels = lifted - 16.0 * jnp.floor(lifted * (1.0 / 16)) - 8.0
    height = 4 * quarter
    grouped = levels.reshape(height // GROUP, GROUP, width) * scales.astype(F32)[:, None, :]
    return grouped.reshape(height, width).astype(BF16)


def routed(normed, mixed, routes, route_weights, codes, capacity):
    gate_codes, gate_scales, up_codes, up_scales, down_codes, down_scales = codes
    experts = lax.axis_size("expert")
    groups = lax.axis_size("dp")
    row_count, width = mixed.shape
    own_slots = slot_table(routes, experts, capacity)
    w_gate = unpack(gate_codes, gate_scales)
    w_up = unpack(up_codes, up_scales)
    w_down = unpack(down_codes, down_scales)
    local_units = w_gate.shape[1]
    peer_rows = lax.all_gather(normed, "dp", axis=0, tiled=True).reshape(groups, row_count, width)
    peer_routes = lax.all_gather(routes, "dp", axis=0, tiled=True).reshape(groups, row_count, TOP)

    def build(block, table):
        return dispatch(block, slot_table(table, experts, capacity), experts * capacity)

    outgoing = jax.vmap(build)(peer_rows, peer_routes).reshape(groups, experts, capacity, width)
    items = lax.all_to_all(outgoing, "expert", split_axis=1, concat_axis=1, tiled=True)
    inputs = items.reshape(-1, width)
    gate = jnp.dot(inputs, w_gate, preferred_element_type=F32)
    upward = jnp.dot(inputs, w_up, preferred_element_type=F32)
    hidden = (jax.nn.silu(gate) * upward).astype(BF16).reshape(-1, local_units)
    produced = jnp.dot(
        lax.all_gather(hidden, "dp", axis=1, tiled=True), w_down, preferred_element_type=F32
    ).astype(BF16)
    produced = produced.reshape(groups, -1, produced.shape[1])
    returned = lax.all_to_all(
        lax.all_to_all(produced, "dp", split_axis=0, concat_axis=2, tiled=True),
        "expert",
        split_axis=1,
        concat_axis=0,
        tiled=True,
    )
    shares = route_weights / jnp.sum(route_weights, axis=1, keepdims=True)
    targets = jnp.arange(experts * capacity, dtype=jnp.int32)
    spreading = jnp.sum(
        jnp.where(own_slots[:, :, None] == targets[None, None, :], shares[:, :, None], 0.0), axis=1
    )
    combined = jnp.dot(
        spreading, returned.reshape(-1, width).astype(F32), precision=lax.Precision.HIGHEST
    )
    return (mixed.astype(F32) + combined).astype(BF16)


def body(
    queries,
    new_kv,
    cache_keys,
    cache_values,
    lengths,
    residual,
    norm_gain,
    routes,
    route_weights,
    *packed,
):
    experts = lax.axis_size("expert")
    groups = lax.axis_size("dp")
    row_count = queries.shape[0]
    capacity = min(row_count, max(2, 2 * row_count * TOP // experts))
    every = (
        capacity == row_count
        and groups == 2
        and experts <= LANES // 2
        and experts % 4 == 0
        and experts & (experts - 1) == 0
    )
    mixed, payload = front(
        queries,
        new_kv,
        cache_keys,
        cache_values,
        lengths,
        residual,
        norm_gain,
        routes,
        route_weights,
        LANES if every else 0,
    )
    codes = [array[0] for array in packed]
    if every:
        return dense(payload, mixed, codes)
    return routed(payload, mixed, routes, route_weights, codes, capacity)


def solution(mesh):
    return jax.shard_map(
        body,
        mesh=mesh,
        in_specs=(
            P(("dp", "expert"), None),
            P(("dp", "expert"), None, None),
            P(("dp", "expert"), None, None),
            P(("dp", "expert"), None, None),
            P(("dp", "expert")),
            P(("dp", "expert"), None),
            P(),
            P(("dp", "expert"), None),
            P(("dp", "expert"), None),
            P("expert", None, "dp"),
            P("expert", None, "dp"),
            P("expert", None, "dp"),
            P("expert", None, "dp"),
            P("expert", None, "dp"),
            P("expert", None, "dp"),
        ),
        out_specs=P(("dp", "expert"), None),
        check_vma=False,
    )
```

```python
import functools

import jax
import jax.numpy as jnp
from jax import lax
from jax.experimental import pallas as pl
from jax.experimental.pallas import tpu as pltpu
from jax.sharding import PartitionSpec as P

HEAD_DIM = 128
GROUP = 128
TOP = 8
LANES = 128
VMEM_LIMIT = 56 * 2**20
VMEM_SOME = 16 * 2**20
VMEM_MORE = 24 * 2**20
SPARE = 16
SMALL = pl.CostEstimate(flops=1, bytes_accessed=1, transcendentals=0)
F32 = jnp.float32
BF16 = jnp.bfloat16


def front_kernel(
    lengths_ref,
    queries_ref,
    new_kv_ref,
    keys_ref,
    values_ref,
    residual_ref,
    gain_ref,
    routes_ref,
    weights_ref,
    mixed_ref,
    payload_ref,
):
    rows, cache, kv_width = keys_ref.shape
    width = queries_ref.shape[1]
    kv_heads = kv_width // HEAD_DIM
    per = width // kv_width
    scaling = HEAD_DIM ** (-0.5)
    row_id = lax.broadcasted_iota(jnp.int32, (rows, rows * cache), 0)
    lane_id = lax.broadcasted_iota(jnp.int32, (rows, rows * cache), 1)
    bound = jnp.zeros((rows, rows * cache), jnp.int32)
    for r in range(rows):
        bound = jnp.where(row_id == r, r * cache + lengths_ref[r], bound)
    valid = (lane_id >= row_id * cache) & (lane_id < bound)
    earlier, current = [], []
    for j in range(kv_heads):
        span = slice(j * HEAD_DIM, (j + 1) * HEAD_DIM)
        heads = range(j * per, (j + 1) * per)
        queried = jnp.concatenate(
            [queries_ref[:, h * HEAD_DIM : (h + 1) * HEAD_DIM].astype(F32) for h in heads], axis=0
        )
        keys = keys_ref[:, :, span].reshape(rows * cache, HEAD_DIM)
        earlier.append(
            lax.dot_general(
                queried.astype(BF16), keys, (((1,), (1,)), ((), ())), preferred_element_type=F32
            )
        )
        fresh_key = new_kv_ref[:, 0, span].astype(F32)
        current.append(queried.reshape(per, rows, HEAD_DIM) * fresh_key[None])
    earlier = jnp.concatenate(earlier, axis=0).reshape(kv_heads * per, rows, rows * cache)
    earlier = jnp.where(valid[None], earlier * scaling, -1e30)
    current = jnp.sum(jnp.concatenate(current, axis=0), axis=-1, keepdims=True) * scaling
    largest = jnp.maximum(jnp.max(earlier, axis=-1, keepdims=True), current)
    earlier_w = jnp.where(valid[None], jnp.exp(earlier - largest), 0.0)
    current_w = jnp.exp(current - largest)
    inverse = 1.0 / (jnp.sum(earlier_w, axis=-1, keepdims=True) + current_w)
    earlier_p = (earlier_w * inverse).astype(BF16).reshape(kv_heads * per * rows, rows * cache)
    current_p = (current_w * inverse).astype(BF16).astype(F32)
    total = jnp.zeros((rows, HEAD_DIM), F32)
    for j in range(kv_heads):
        span = slice(j * HEAD_DIM, (j + 1) * HEAD_DIM)
        values = values_ref[:, :, span].reshape(rows * cache, HEAD_DIM)
        fresh_value = new_kv_ref[:, 1, span].astype(F32)
        attended = jnp.dot(
            earlier_p[j * per * rows : (j + 1) * per * rows], values, preferred_element_type=F32
        )
        attended = attended.reshape(per, rows, HEAD_DIM)
        attended = attended + current_p[j * per : (j + 1) * per] * fresh_value[None]
        for g in range(per):
            h = j * per + g
            place = slice(h * HEAD_DIM, (h + 1) * HEAD_DIM)
            mixed = (
                residual_ref[:, place].astype(F32) + attended[g].astype(BF16).astype(F32)
            ).astype(BF16)
            mixed_ref[:, place] = mixed
            widened = mixed.astype(F32)
            total = total + widened * widened
    meansq = jnp.sum(total, axis=-1, keepdims=True) * (1.0 / width)
    inverse = lax.rsqrt(meansq + 1e-06)
    payload_ref[:, :width] = (
        mixed_ref[...].astype(F32) * inverse * gain_ref[...].astype(F32).reshape(1, width)
    ).astype(BF16)
    if payload_ref.shape[1] > width:
        shares = weights_ref[...] / jnp.sum(weights_ref[...], axis=1, keepdims=True)
        lane = lax.broadcasted_iota(jnp.int32, (rows, LANES), 1)
        expert = jnp.where(lane < LANES // 2, lane, lane - LANES // 2)
        table = jnp.zeros((rows, LANES), F32)
        for k in range(routes_ref.shape[1]):
            table = table + jnp.where(
                routes_ref[:, k : k + 1] == expert, shares[:, k : k + 1], 0.0
            )
        high = table.astype(BF16).astype(F32)
        payload_ref[:, width:] = jnp.where(lane < LANES // 2, high, table - high).astype(BF16)


def front(queries, new_kv, keys, values, lengths, residual, gain, routes, weights, extra):
    rows, width = queries.shape
    vmem = pl.BlockSpec(memory_space=pltpu.VMEM)
    shape = pltpu.VMEM if extra else jax.ShapeDtypeStruct
    return pl.pallas_call(
        front_kernel,
        out_shape=(shape((rows, width), BF16), shape((rows, width + extra), BF16)),
        in_specs=[pl.BlockSpec(memory_space=pltpu.SMEM)] + [vmem] * 8,
        out_specs=(vmem, vmem),
        compiler_params=pltpu.CompilerParams(vmem_limit_bytes=VMEM_LIMIT),
        cost_estimate=SMALL,
        name="front",
    )(lengths, queries, new_kv, keys, values, residual, gain, routes, weights)


def in_vmem(array):
    return pltpu.with_memory_space_constraint(array, pltpu.VMEM)


def in_hbm(array):
    return pltpu.with_memory_space_constraint(array, pltpu.HBM)


def unpack_kernel(firsts, codes_refs, scales_hbms, *refs):
    out_refs, (words_refs, scales_refs, sems, scales_sem) = refs[: len(firsts)], refs[len(firsts) :]

    def copy_scales(n):
        columns = pl.ds(firsts[n], words_refs[n].shape[1])
        return pltpu.make_async_copy(
            scales_hbms[n].at[:, columns], scales_refs[n], scales_sem.at[n]
        )

    def fetch(turn):
        n, group = turns[turn]
        rows = pl.ds(group * GROUP, GROUP)
        columns = pl.ds(firsts[n], words_refs[n].shape[1])
        return pltpu.make_async_copy(
            codes_refs[n].at[rows, columns], words_refs[n].at[rows, :], sems.at[turn]
        )

    turns = [
        (n, group)
        for n, words_ref in enumerate(words_refs)
        for group in range(words_ref.shape[0] // GROUP)
    ]
    ahead = 3
    copy_scales(0).start()
    for turn in range(min(ahead, len(turns))):
        fetch(turn).start()
    for n in range(1, len(firsts)):
        copy_scales(n).start()
    for turn, (n, group) in enumerate(turns):
        words_ref, out_ref = words_refs[n], out_refs[n]
        quarter, width = words_ref.shape
        groups = quarter // GROUP
        step = 256 if width % 256 == 0 else LANES
        if turn + ahead < len(turns):
            fetch(turn + ahead).start()
        if group == 0:
            copy_scales(n).wait()
            scales = scales_refs[n][...].astype(F32)
        fetch(turn).wait()
        for column in range(0, width, step):
            spans = [
                jnp.broadcast_to(
                    scales[k * groups + group : k * groups + group + 1, column : column + step],
                    (16, step),
                ).astype(BF16)
                for k in range(4)
            ]

            def chunk(
                i, carry, group=group, column=column, spans=spans, words_ref=words_ref, out_ref=out_ref
            ):
                start = pl.multiple_of(group * GROUP + i * 16, 16)
                words = words_ref[pl.ds(start, 16), column : column + step].astype(jnp.int32)
                for k in range(4):
                    digit = words if k == 0 else lax.shift_right_logical(words, 4 * k)
                    if k < 3:
                        digit = digit & 15
                    level = digit.astype(F32).astype(BF16) - jnp.asarray(8, BF16)
                    out_ref[pl.ds(k * quarter + start, 16), column : column + step] = (
                        level * spans[k]
                    )
                return carry

            lax.fori_loop(0, GROUP // 16, chunk, 0, unroll=True)


def unpack_weights(*jobs):
    hbm = pl.BlockSpec(memory_space=pltpu.HBM)
    vmem = pl.BlockSpec(memory_space=pltpu.VMEM)
    shapes = [(codes.shape[0], width) for codes, _, _, width in jobs]
    turns = sum(quarter // GROUP for quarter, _ in shapes)
    return pl.pallas_call(
        functools.partial(unpack_kernel, tuple(job[2] for job in jobs)),
        out_shape=[pltpu.VMEM((4 * quarter, width), BF16) for quarter, width in shapes],
        in_specs=[[hbm] * len(jobs)] * 2,
        out_specs=[vmem] * len(jobs),
        scratch_shapes=[
            [pltpu.VMEM(shape, F32) for shape in shapes],
            [pltpu.VMEM((4 * quarter // GROUP, width), BF16) for quarter, width in shapes],
            pltpu.SemaphoreType.DMA((turns,)),
            pltpu.SemaphoreType.DMA((len(jobs),)),
        ],
        compiler_params=pltpu.CompilerParams(vmem_limit_bytes=VMEM_MORE),
        cost_estimate=SMALL,
        name="unpack_weights",
    )([in_hbm(job[0]) for job in jobs], [in_hbm(job[1]) for job in jobs])


def hidden_kernel(place_ref, *refs):
    pieces, (gate_ref, up_ref, out_ref, share_ref, rows_ref) = refs[:-5], refs[-5:]
    depth, width = gate_ref.shape
    block = pieces[0].shape[0]
    count = block * len(pieces)
    for n, piece in enumerate(pieces):
        rows_ref[n * block : (n + 1) * block, :] = piece[:, :depth]
        table = piece[:, depth:].astype(F32)
        lane = lax.broadcasted_iota(jnp.int32, table.shape, 1)
        mine = place_ref[0]
        chosen = (lane == mine) | (lane == mine + LANES // 2)
        share = jnp.sum(jnp.where(chosen, table, 0.0), axis=1, keepdims=True)
        share_ref[n * block : (n + 1) * block, :] = jnp.broadcast_to(share, table.shape)
    step = 256
    for column in range(0, width, step):
        span = slice(column, column + step)
        gate = jnp.dot(rows_ref[...], gate_ref[:, span], preferred_element_type=F32)
        upward = jnp.dot(rows_ref[...], up_ref[:, span], preferred_element_type=F32)
        out_ref[:count, span] = (gate / (1.0 + jnp.exp(-gate)) * upward).astype(BF16)
    if out_ref.shape[0] > count:
        out_ref[count:, :] = jnp.zeros((out_ref.shape[0] - count, width), BF16)


def hidden_units(pieces, w_gate, w_up, place, spare=0):
    block, padded = pieces[0].shape
    count = block * len(pieces)
    depth, width = w_gate.shape
    vmem = pl.BlockSpec(memory_space=pltpu.VMEM)
    return pl.pallas_call(
        hidden_kernel,
        out_shape=(pltpu.VMEM((count + spare, width), BF16), pltpu.VMEM((count, LANES), F32)),
        in_specs=[pl.BlockSpec(memory_space=pltpu.SMEM)] + [vmem] * (len(pieces) + 2),
        out_specs=(vmem, vmem),
        scratch_shapes=[pltpu.VMEM((count, depth), BF16)],
        compiler_params=pltpu.CompilerParams(vmem_limit_bytes=VMEM_SOME),
        cost_estimate=SMALL,
        name="gate_up",
    )(place, *pieces, in_vmem(w_gate), in_vmem(w_up))


def own_down_kernel(side_ref, hidden_ref, weight_refs, out_ref):
    half = hidden_ref.shape[1]
    rows = pl.ds(pl.multiple_of(side_ref[0] * half, half), half)
    step = 256
    for n, weight_ref in enumerate(weight_refs):
        width = weight_ref.shape[1]
        for column in range(0, width, step):
            out_ref[:, n * width + column : n * width + column + step] = jnp.dot(
                hidden_ref[: out_ref.shape[0]],
                weight_ref[rows, column : column + step],
                preferred_element_type=F32,
            )


def own_down(side, hidden, weights, count):
    width = sum(weight.shape[1] for weight in weights)
    vmem = pl.BlockSpec(memory_space=pltpu.VMEM)
    return pl.pallas_call(
        own_down_kernel,
        out_shape=pltpu.VMEM((count, width), F32),
        in_specs=[pl.BlockSpec(memory_space=pltpu.SMEM), vmem, [vmem] * len(weights)],
        out_specs=vmem,
        compiler_params=pltpu.CompilerParams(vmem_limit_bytes=VMEM_SOME),
        cost_estimate=SMALL,
        name="down_own",
    )(side, in_vmem(hidden), [in_vmem(weight) for weight in weights])


def peer_down_kernel(side_ref, partial_ref, hidden_ref, weight_refs, share_ref, *out_refs):
    count, half = partial_ref.shape[0], hidden_ref.shape[1]
    rows = pl.ds(pl.multiple_of((1 - side_ref[0]) * half, half), half)
    step = 256
    cut = count // len(out_refs)
    for n, weight_ref in enumerate(weight_refs):
        width = weight_ref.shape[1]
        for column in range(0, width, step):
            span = slice(n * width + column, n * width + column + step)
            produced = partial_ref[:, span] + jnp.dot(
                hidden_ref[:count],
                weight_ref[rows, column : column + step],
                preferred_element_type=F32,
            )
            result = (produced.astype(BF16).astype(F32) * share_ref[:, :1]).astype(BF16)
            for m, out_ref in enumerate(out_refs):
                out_ref[:, span] = result[m * cut : (m + 1) * cut]


def peer_down(side, partial, hidden, weights, share, parts):
    count, width = partial.shape
    vmem = pl.BlockSpec(memory_space=pltpu.VMEM)
    return pl.pallas_call(
        peer_down_kernel,
        out_shape=(pltpu.VMEM((count // parts, width), BF16),) * parts,
        in_specs=[pl.BlockSpec(memory_space=pltpu.SMEM), vmem, vmem, [vmem] * len(weights), vmem],
        out_specs=(vmem,) * parts,
        compiler_params=pltpu.CompilerParams(vmem_limit_bytes=VMEM_SOME),
        cost_estimate=SMALL,
        name="down_peer",
    )(side, in_vmem(partial), hidden, [in_vmem(weight) for weight in weights], in_vmem(share))


def halve_kernel(terms, *refs):
    term_refs, out_refs = refs[:terms], refs[terms:]
    total = term_refs[0][...].astype(F32)
    for term_ref in term_refs[1:]:
        total = total + term_ref[...].astype(F32)
    size = total.shape[0] // len(out_refs)
    for n, out_ref in enumerate(out_refs):
        out_ref[...] = total[n * size : (n + 1) * size].astype(out_ref.dtype)


def add_and_cut(kept, arrived, parts):
    count, width = kept[0].shape
    vmem = pl.BlockSpec(memory_space=pltpu.VMEM)
    shape = pltpu.VMEM((count // parts, width), BF16)
    return pl.pallas_call(
        functools.partial(halve_kernel, len(kept + arrived)),
        out_shape=(shape,) * parts,
        in_specs=[vmem] * len(kept + arrived),
        out_specs=(vmem,) * parts,
        compiler_params=pltpu.CompilerParams(vmem_limit_bytes=VMEM_SOME),
        cost_estimate=SMALL,
        name="add_and_cut",
    )(*[in_vmem(part) for part in kept], *arrived)


def join_kernel(parts, far_ref, *refs):
    near_refs, out_refs = refs[:-parts], refs[-parts:]
    size = far_ref.shape[0] // parts
    near = near_refs[0][...].astype(F32)
    for near_ref in near_refs[1:]:
        near = near + near_ref[...].astype(F32)
    far = far_ref[...].astype(F32)
    for n, out_ref in enumerate(out_refs):
        rows = slice(n * size, (n + 1) * size)
        out_ref[...] = jnp.concatenate([near[rows], far[rows]], axis=0).astype(BF16)


def join(near, far, parts):
    count, width = far.shape
    vmem = pl.BlockSpec(memory_space=pltpu.VMEM)
    return pl.pallas_call(
        functools.partial(join_kernel, parts),
        out_shape=(pltpu.VMEM((2 * count // parts, width), BF16),) * parts,
        in_specs=[vmem] * (1 + len(near)),
        out_specs=(vmem,) * parts,
        compiler_params=pltpu.CompilerParams(vmem_limit_bytes=VMEM_SOME),
        cost_estimate=SMALL,
        name="join",
    )(far, *near)


def finish_kernel(side_ref, mixed_ref, *refs):
    block_refs, out_ref = refs[:-1], refs[-1]
    rows, width = mixed_ref.shape
    total = block_refs[0][...].astype(F32)
    for block_ref in block_refs[1:]:
        total = total + block_ref[...].astype(F32)
    near, far = total[:rows], total[rows:]
    first = side_ref[0] == 0
    half = width // 2
    for n, part in enumerate((jnp.where(first, near, far), jnp.where(first, far, near))):
        span = slice(n * half, (n + 1) * half)
        out_ref[:, span] = (mixed_ref[:, span].astype(F32) + part).astype(BF16)


def finish(side, mixed, blocks):
    vmem = pl.BlockSpec(memory_space=pltpu.VMEM)
    return pl.pallas_call(
        finish_kernel,
        out_shape=jax.ShapeDtypeStruct(mixed.shape, BF16),
        in_specs=[pl.BlockSpec(memory_space=pltpu.SMEM)] + [vmem] * (1 + len(blocks)),
        out_specs=vmem,
        compiler_params=pltpu.CompilerParams(vmem_limit_bytes=VMEM_SOME),
        name="finish",
    )(side, mixed, *blocks)


def dense(payload, mixed, codes):
    gate_codes, gate_scales, up_codes, up_scales, down_codes, down_scales = codes
    groups = lax.axis_size("dp")
    experts = lax.axis_size("expert")
    devices = groups * experts
    core, line, layer, plane = 1, 2, 4, experts
    layers = experts // layer
    side = lax.axis_index("dp").reshape(1).astype(jnp.int32)
    place = lax.axis_index("expert").reshape(1).astype(jnp.int32)

    def swap(block, offset):
        return lax.ppermute(block, ("dp", "expert"), [(i, i ^ offset) for i in range(devices)])

    side, place, gate_scales, down_scales, payload = lax.optimization_barrier(
        (side, place, gate_scales, down_scales, payload)
    )
    units = gate_codes.shape[1]
    half = down_codes.shape[1] // 2
    blocks = [swap(payload, z * layer) for z in range(1, layers)]
    w_gate, w_down = unpack_weights(
        (gate_codes, gate_scales, 0, units), (down_codes, down_scales, 0, half)
    )
    blocks, w_gate = lax.optimization_barrier((blocks, w_gate))
    stack = jnp.concatenate([payload] + blocks, axis=0)
    up_scales, stack = lax.optimization_barrier((up_scales, stack))
    beside, above, stack_pair = swap(stack, plane), swap(stack, line), swap(stack, core)
    (w_up,) = unpack_weights((up_codes, up_scales, 0, units))
    above, stack_pair, w_up = lax.optimization_barrier((above, stack_pair, w_up))
    across, above_pair = swap(above, plane), swap(above, core)
    above_pair, beside = lax.optimization_barrier((above_pair, beside))
    beside_pair = swap(beside, core)
    hidden_own, share_own = hidden_units(
        [stack, stack_pair, above, above_pair], w_gate, w_up, place, SPARE
    )
    other_peer = swap(hidden_own, plane)
    down_scales, hidden_own = lax.optimization_barrier((down_scales, hidden_own))
    (w_more,) = unpack_weights((down_codes, down_scales, half, half))
    across, w_more = lax.optimization_barrier((across, w_more))
    w_down = [w_down, w_more]
    hidden_other, share_other = hidden_units(
        [beside, beside_pair, across, swap(across, core)], w_gate, w_up, place
    )
    own_peer = swap(hidden_other, plane)

    count = share_own.shape[0]
    partial_other = own_down(side, hidden_other, w_down, count)
    partial_own = own_down(side, hidden_own, w_down, count)
    keep, send = peer_down(side, partial_other, other_peer, w_down, share_other, 2)
    keep, send = add_and_cut([keep], [swap(send, line)], 2)
    (onward,) = add_and_cut([keep], [swap(send, core)], 1)
    far = swap(onward, plane)
    keep_near, send_near, keep_far, send_far = peer_down(
        side, partial_own, own_peer, w_down, share_own, 4
    )
    (onward,) = add_and_cut([keep_far], [swap(send_far, core)], 1)
    near = [in_vmem(keep_near), swap(send_near, core), swap(onward, line)]
    blocks = join(near, far, layers)
    blocks = [blocks[0]] + [swap(blocks[z], z * layer) for z in range(1, layers)]
    return finish(side, mixed, blocks)


def slot_table(routes, experts, capacity):
    flattened = routes.reshape(-1)
    onehot = (flattened[:, None] == jnp.arange(experts, dtype=jnp.int32)[None, :]).astype(jnp.int32)
    ranking = jnp.sum((jnp.cumsum(onehot, axis=0) - 1) * onehot, axis=1)
    return (flattened * capacity + ranking).reshape(routes.shape)


def dispatch(block, slots, width):
    targets = jnp.arange(width, dtype=jnp.int32)
    placing = jnp.sum((slots[None, :, :] == targets[:, None, None]).astype(F32), axis=2)
    return jnp.dot(placing.astype(BF16), block, preferred_element_type=F32).astype(BF16)


def unpack(codes, scales):
    quarter, width = codes.shape
    divisors = jnp.array([1.0, 1.0 / 16, 1.0 / 256, 1.0 / 4096], F32)[:, None, None]
    lifted = jnp.floor(codes[None, :, :] * divisors)
    levels = lifted - 16.0 * jnp.floor(lifted * (1.0 / 16)) - 8.0
    height = 4 * quarter
    grouped = levels.reshape(height // GROUP, GROUP, width) * scales.astype(F32)[:, None, :]
    return grouped.reshape(height, width).astype(BF16)


def routed(normed, mixed, routes, route_weights, codes, capacity):
    gate_codes, gate_scales, up_codes, up_scales, down_codes, down_scales = codes
    experts = lax.axis_size("expert")
    groups = lax.axis_size("dp")
    row_count, width = mixed.shape
    own_slots = slot_table(routes, experts, capacity)
    w_gate = unpack(gate_codes, gate_scales)
    w_up = unpack(up_codes, up_scales)
    w_down = unpack(down_codes, down_scales)
    local_units = w_gate.shape[1]
    peer_rows = lax.all_gather(normed, "dp", axis=0, tiled=True).reshape(groups, row_count, width)
    peer_routes = lax.all_gather(routes, "dp", axis=0, tiled=True).reshape(groups, row_count, TOP)

    def build(block, table):
        return dispatch(block, slot_table(table, experts, capacity), experts * capacity)

    outgoing = jax.vmap(build)(peer_rows, peer_routes).reshape(groups, experts, capacity, width)
    items = lax.all_to_all(outgoing, "expert", split_axis=1, concat_axis=1, tiled=True)
    inputs = items.reshape(-1, width)
    gate = jnp.dot(inputs, w_gate, preferred_element_type=F32)
    upward = jnp.dot(inputs, w_up, preferred_element_type=F32)
    hidden = (jax.nn.silu(gate) * upward).astype(BF16).reshape(-1, local_units)
    produced = jnp.dot(
        lax.all_gather(hidden, "dp", axis=1, tiled=True), w_down, preferred_element_type=F32
    ).astype(BF16)
    produced = produced.reshape(groups, -1, produced.shape[1])
    returned = lax.all_to_all(
        lax.all_to_all(produced, "dp", split_axis=0, concat_axis=2, tiled=True),
        "expert",
        split_axis=1,
        concat_axis=0,
        tiled=True,
    )
    shares = route_weights / jnp.sum(route_weights, axis=1, keepdims=True)
    targets = jnp.arange(experts * capacity, dtype=jnp.int32)
    spreading = jnp.sum(
        jnp.where(own_slots[:, :, None] == targets[None, None, :], shares[:, :, None], 0.0), axis=1
    )
    combined = jnp.dot(
        spreading, returned.reshape(-1, width).astype(F32), precision=lax.Precision.HIGHEST
    )
    return (mixed.astype(F32) + combined).astype(BF16)


def body(
    queries,
    new_kv,
    cache_keys,
    cache_values,
    lengths,
    residual,
    norm_gain,
    routes,
    route_weights,
    *packed,
):
    experts = lax.axis_size("expert")
    groups = lax.axis_size("dp")
    row_count = queries.shape[0]
    capacity = min(row_count, max(2, 2 * row_count * TOP // experts))
    every = (
        capacity == row_count
        and groups == 2
        and experts <= LANES // 2
        and experts % 4 == 0
        and experts & (experts - 1) == 0
    )
    mixed, payload = front(
        queries,
        new_kv,
        cache_keys,
        cache_values,
        lengths,
        residual,
        norm_gain,
        routes,
        route_weights,
        LANES if every else 0,
    )
    codes = [array[0] for array in packed]
    if every:
        return dense(payload, mixed, codes)
    return routed(payload, mixed, routes, route_weights, codes, capacity)


def solution(mesh):
    return jax.shard_map(
        body,
        mesh=mesh,
        in_specs=(
            P(("dp", "expert"), None),
            P(("dp", "expert"), None, None),
            P(("dp", "expert"), None, None),
            P(("dp", "expert"), None, None),
            P(("dp", "expert")),
            P(("dp", "expert"), None),
            P(),
            P(("dp", "expert"), None),
            P(("dp", "expert"), None),
            P("expert", None, "dp"),
            P("expert", None, "dp"),
            P("expert", None, "dp"),
            P("expert", None, "dp"),
            P("expert", None, "dp"),
            P("expert", None, "dp"),
        ),
        out_specs=P(("dp", "expert"), None),
        check_vma=False,
    )
```

```python
import functools

import jax
import jax.numpy as jnp
from jax import lax
from jax.experimental import pallas as pl
from jax.experimental.pallas import tpu as pltpu
from jax.sharding import PartitionSpec as P

HEAD_DIM = 128
GROUP = 128
TOP = 8
LANES = 128
VMEM_LIMIT = 56 * 2**20
VMEM_SOME = 16 * 2**20
VMEM_MORE = 24 * 2**20
SPARE = 16
SMALL = pl.CostEstimate(flops=1, bytes_accessed=1, transcendentals=0)
F32 = jnp.float32
BF16 = jnp.bfloat16


def front_kernel(
    lengths_ref,
    queries_ref,
    new_kv_ref,
    keys_ref,
    values_ref,
    residual_ref,
    gain_ref,
    routes_ref,
    weights_ref,
    mixed_ref,
    payload_ref,
):
    rows, cache, kv_width = keys_ref.shape
    width = queries_ref.shape[1]
    kv_heads = kv_width // HEAD_DIM
    per = width // kv_width
    scaling = HEAD_DIM ** (-0.5)
    row_id = lax.broadcasted_iota(jnp.int32, (rows, rows * cache), 0)
    lane_id = lax.broadcasted_iota(jnp.int32, (rows, rows * cache), 1)
    bound = jnp.zeros((rows, rows * cache), jnp.int32)
    for r in range(rows):
        bound = jnp.where(row_id == r, r * cache + lengths_ref[r], bound)
    valid = (lane_id >= row_id * cache) & (lane_id < bound)
    earlier, current = [], []
    for j in range(kv_heads):
        span = slice(j * HEAD_DIM, (j + 1) * HEAD_DIM)
        heads = range(j * per, (j + 1) * per)
        queried = jnp.concatenate(
            [queries_ref[:, h * HEAD_DIM : (h + 1) * HEAD_DIM].astype(F32) for h in heads], axis=0
        )
        keys = keys_ref[:, :, span].reshape(rows * cache, HEAD_DIM)
        earlier.append(
            lax.dot_general(
                queried.astype(BF16), keys, (((1,), (1,)), ((), ())), preferred_element_type=F32
            )
        )
        fresh_key = new_kv_ref[:, 0, span].astype(F32)
        current.append(queried.reshape(per, rows, HEAD_DIM) * fresh_key[None])
    earlier = jnp.concatenate(earlier, axis=0).reshape(kv_heads * per, rows, rows * cache)
    earlier = jnp.where(valid[None], earlier * scaling, -1e30)
    current = jnp.sum(jnp.concatenate(current, axis=0), axis=-1, keepdims=True) * scaling
    largest = jnp.maximum(jnp.max(earlier, axis=-1, keepdims=True), current)
    earlier_w = jnp.where(valid[None], jnp.exp(earlier - largest), 0.0)
    current_w = jnp.exp(current - largest)
    inverse = 1.0 / (jnp.sum(earlier_w, axis=-1, keepdims=True) + current_w)
    earlier_p = (earlier_w * inverse).astype(BF16).reshape(kv_heads * per * rows, rows * cache)
    current_p = (current_w * inverse).astype(BF16).astype(F32)
    total = jnp.zeros((rows, HEAD_DIM), F32)
    for j in range(kv_heads):
        span = slice(j * HEAD_DIM, (j + 1) * HEAD_DIM)
        values = values_ref[:, :, span].reshape(rows * cache, HEAD_DIM)
        fresh_value = new_kv_ref[:, 1, span].astype(F32)
        attended = jnp.dot(
            earlier_p[j * per * rows : (j + 1) * per * rows], values, preferred_element_type=F32
        )
        attended = attended.reshape(per, rows, HEAD_DIM)
        attended = attended + current_p[j * per : (j + 1) * per] * fresh_value[None]
        for g in range(per):
            h = j * per + g
            place = slice(h * HEAD_DIM, (h + 1) * HEAD_DIM)
            mixed = (
                residual_ref[:, place].astype(F32) + attended[g].astype(BF16).astype(F32)
            ).astype(BF16)
            mixed_ref[:, place] = mixed
            widened = mixed.astype(F32)
            total = total + widened * widened
    meansq = jnp.sum(total, axis=-1, keepdims=True) * (1.0 / width)
    inverse = lax.rsqrt(meansq + 1e-06)
    payload_ref[:, :width] = (
        mixed_ref[...].astype(F32) * inverse * gain_ref[...].astype(F32).reshape(1, width)
    ).astype(BF16)
    if payload_ref.shape[1] > width:
        shares = weights_ref[...] / jnp.sum(weights_ref[...], axis=1, keepdims=True)
        lane = lax.broadcasted_iota(jnp.int32, (rows, LANES), 1)
        expert = jnp.where(lane < LANES // 2, lane, lane - LANES // 2)
        table = jnp.zeros((rows, LANES), F32)
        for k in range(routes_ref.shape[1]):
            table = table + jnp.where(
                routes_ref[:, k : k + 1] == expert, shares[:, k : k + 1], 0.0
            )
        high = table.astype(BF16).astype(F32)
        payload_ref[:, width:] = jnp.where(lane < LANES // 2, high, table - high).astype(BF16)


def front(queries, new_kv, keys, values, lengths, residual, gain, routes, weights, extra):
    rows, width = queries.shape
    vmem = pl.BlockSpec(memory_space=pltpu.VMEM)
    shape = pltpu.VMEM if extra else jax.ShapeDtypeStruct
    return pl.pallas_call(
        front_kernel,
        out_shape=(shape((rows, width), BF16), shape((rows, width + extra), BF16)),
        in_specs=[pl.BlockSpec(memory_space=pltpu.SMEM)] + [vmem] * 8,
        out_specs=(vmem, vmem),
        compiler_params=pltpu.CompilerParams(vmem_limit_bytes=VMEM_LIMIT),
        cost_estimate=SMALL,
        name="front",
    )(lengths, queries, new_kv, keys, values, residual, gain, routes, weights)


def in_vmem(array):
    return pltpu.with_memory_space_constraint(array, pltpu.VMEM)


def in_hbm(array):
    return pltpu.with_memory_space_constraint(array, pltpu.HBM)


def unpack_kernel(firsts, codes_refs, scales_hbms, *refs):
    out_refs, (words_refs, scales_refs, sems, scales_sem) = refs[: len(firsts)], refs[len(firsts) :]

    def copy_scales(n):
        columns = pl.ds(firsts[n], words_refs[n].shape[1])
        return pltpu.make_async_copy(
            scales_hbms[n].at[:, columns], scales_refs[n], scales_sem.at[n]
        )

    def fetch(turn):
        n, group = turns[turn]
        rows = pl.ds(group * GROUP, GROUP)
        columns = pl.ds(firsts[n], words_refs[n].shape[1])
        return pltpu.make_async_copy(
            codes_refs[n].at[rows, columns], words_refs[n].at[rows, :], sems.at[turn]
        )

    turns = [
        (n, group)
        for n, words_ref in enumerate(words_refs)
        for group in range(words_ref.shape[0] // GROUP)
    ]
    ahead = 3
    copy_scales(0).start()
    for turn in range(min(ahead, len(turns))):
        fetch(turn).start()
    for n in range(1, len(firsts)):
        copy_scales(n).start()
    for turn, (n, group) in enumerate(turns):
        words_ref, out_ref = words_refs[n], out_refs[n]
        quarter, width = words_ref.shape
        groups = quarter // GROUP
        step = 256 if width % 256 == 0 else LANES
        if turn + ahead < len(turns):
            fetch(turn + ahead).start()
        if group == 0:
            copy_scales(n).wait()
            scales = scales_refs[n][...].astype(F32)
        fetch(turn).wait()
        for column in range(0, width, step):
            spans = [
                jnp.broadcast_to(
                    scales[k * groups + group : k * groups + group + 1, column : column + step],
                    (16, step),
                ).astype(BF16)
                for k in range(4)
            ]

            def chunk(
                i, carry, group=group, column=column, spans=spans, words_ref=words_ref, out_ref=out_ref
            ):
                start = pl.multiple_of(group * GROUP + i * 16, 16)
                words = words_ref[pl.ds(start, 16), column : column + step].astype(jnp.int32)
                for k in range(4):
                    digit = words if k == 0 else lax.shift_right_logical(words, 4 * k)
                    if k < 3:
                        digit = digit & 15
                    level = digit.astype(F32).astype(BF16) - jnp.asarray(8, BF16)
                    out_ref[pl.ds(k * quarter + start, 16), column : column + step] = (
                        level * spans[k]
                    )
                return carry

            lax.fori_loop(0, GROUP // 16, chunk, 0, unroll=True)


def unpack_weights(*jobs):
    hbm = pl.BlockSpec(memory_space=pltpu.HBM)
    vmem = pl.BlockSpec(memory_space=pltpu.VMEM)
    shapes = [(codes.shape[0], width) for codes, _, _, width in jobs]
    turns = sum(quarter // GROUP for quarter, _ in shapes)
    return pl.pallas_call(
        functools.partial(unpack_kernel, tuple(job[2] for job in jobs)),
        out_shape=[pltpu.VMEM((4 * quarter, width), BF16) for quarter, width in shapes],
        in_specs=[[hbm] * len(jobs)] * 2,
        out_specs=[vmem] * len(jobs),
        scratch_shapes=[
            [pltpu.VMEM(shape, F32) for shape in shapes],
            [pltpu.VMEM((4 * quarter // GROUP, width), BF16) for quarter, width in shapes],
            pltpu.SemaphoreType.DMA((turns,)),
            pltpu.SemaphoreType.DMA((len(jobs),)),
        ],
        compiler_params=pltpu.CompilerParams(vmem_limit_bytes=VMEM_MORE),
        cost_estimate=SMALL,
        name="unpack_weights",
    )([in_hbm(job[0]) for job in jobs], [in_hbm(job[1]) for job in jobs])


def hidden_kernel(place_ref, *refs):
    pieces, (gate_ref, up_ref, out_ref, share_ref, rows_ref) = refs[:-5], refs[-5:]
    depth, width = gate_ref.shape
    block = pieces[0].shape[0]
    count = block * len(pieces)
    for n, piece in enumerate(pieces):
        rows_ref[n * block : (n + 1) * block, :] = piece[:, :depth]
        table = piece[:, depth:].astype(F32)
        lane = lax.broadcasted_iota(jnp.int32, table.shape, 1)
        mine = place_ref[0]
        chosen = (lane == mine) | (lane == mine + LANES // 2)
        share = jnp.sum(jnp.where(chosen, table, 0.0), axis=1, keepdims=True)
        share_ref[n * block : (n + 1) * block, :] = jnp.broadcast_to(share, table.shape)
    step = 256
    for column in range(0, width, step):
        span = slice(column, column + step)
        gate = jnp.dot(rows_ref[...], gate_ref[:, span], preferred_element_type=F32)
        upward = jnp.dot(rows_ref[...], up_ref[:, span], preferred_element_type=F32)
        out_ref[:count, span] = (gate / (1.0 + jnp.exp(-gate)) * upward).astype(BF16)
    if out_ref.shape[0] > count:
        out_ref[count:, :] = jnp.zeros((out_ref.shape[0] - count, width), BF16)


def hidden_units(pieces, w_gate, w_up, place, spare=0):
    block, padded = pieces[0].shape
    count = block * len(pieces)
    depth, width = w_gate.shape
    vmem = pl.BlockSpec(memory_space=pltpu.VMEM)
    return pl.pallas_call(
        hidden_kernel,
        out_shape=(pltpu.VMEM((count + spare, width), BF16), pltpu.VMEM((count, LANES), F32)),
        in_specs=[pl.BlockSpec(memory_space=pltpu.SMEM)] + [vmem] * (len(pieces) + 2),
        out_specs=(vmem, vmem),
        scratch_shapes=[pltpu.VMEM((count, depth), BF16)],
        compiler_params=pltpu.CompilerParams(vmem_limit_bytes=VMEM_SOME),
        cost_estimate=SMALL,
        name="gate_up",
    )(place, *pieces, in_vmem(w_gate), in_vmem(w_up))


def own_down_kernel(side_ref, hidden_ref, weight_refs, out_ref):
    half = hidden_ref.shape[1]
    rows = pl.ds(pl.multiple_of(side_ref[0] * half, half), half)
    step = 256
    for n, weight_ref in enumerate(weight_refs):
        width = weight_ref.shape[1]
        for column in range(0, width, step):
            out_ref[:, n * width + column : n * width + column + step] = jnp.dot(
                hidden_ref[: out_ref.shape[0]],
                weight_ref[rows, column : column + step],
                preferred_element_type=F32,
            )


def own_down(side, hidden, weights, count):
    width = sum(weight.shape[1] for weight in weights)
    vmem = pl.BlockSpec(memory_space=pltpu.VMEM)
    return pl.pallas_call(
        own_down_kernel,
        out_shape=pltpu.VMEM((count, width), F32),
        in_specs=[pl.BlockSpec(memory_space=pltpu.SMEM), vmem, [vmem] * len(weights)],
        out_specs=vmem,
        compiler_params=pltpu.CompilerParams(vmem_limit_bytes=VMEM_SOME),
        cost_estimate=SMALL,
        name="down_own",
    )(side, in_vmem(hidden), [in_vmem(weight) for weight in weights])


def peer_down_kernel(side_ref, partial_ref, hidden_ref, weight_refs, share_ref, *out_refs):
    count, half = partial_ref.shape[0], hidden_ref.shape[1]
    rows = pl.ds(pl.multiple_of((1 - side_ref[0]) * half, half), half)
    step = 256
    cut = count // len(out_refs)
    for n, weight_ref in enumerate(weight_refs):
        width = weight_ref.shape[1]
        for column in range(0, width, step):
            span = slice(n * width + column, n * width + column + step)
            produced = partial_ref[:, span] + jnp.dot(
                hidden_ref[:count],
                weight_ref[rows, column : column + step],
                preferred_element_type=F32,
            )
            result = (produced.astype(BF16).astype(F32) * share_ref[:, :1]).astype(BF16)
            for m, out_ref in enumerate(out_refs):
                out_ref[:, span] = result[m * cut : (m + 1) * cut]


def peer_down(side, partial, hidden, weights, share, parts):
    count, width = partial.shape
    vmem = pl.BlockSpec(memory_space=pltpu.VMEM)
    return pl.pallas_call(
        peer_down_kernel,
        out_shape=(pltpu.VMEM((count // parts, width), BF16),) * parts,
        in_specs=[pl.BlockSpec(memory_space=pltpu.SMEM), vmem, vmem, [vmem] * len(weights), vmem],
        out_specs=(vmem,) * parts,
        compiler_params=pltpu.CompilerParams(vmem_limit_bytes=VMEM_SOME),
        cost_estimate=SMALL,
        name="down_peer",
    )(side, in_vmem(partial), hidden, [in_vmem(weight) for weight in weights], in_vmem(share))


def halve_kernel(terms, *refs):
    term_refs, out_refs = refs[:terms], refs[terms:]
    total = term_refs[0][...].astype(F32)
    for term_ref in term_refs[1:]:
        total = total + term_ref[...].astype(F32)
    size = total.shape[0] // len(out_refs)
    for n, out_ref in enumerate(out_refs):
        out_ref[...] = total[n * size : (n + 1) * size].astype(out_ref.dtype)


def add_and_cut(kept, arrived, parts):
    count, width = kept[0].shape
    vmem = pl.BlockSpec(memory_space=pltpu.VMEM)
    shape = pltpu.VMEM((count // parts, width), BF16)
    return pl.pallas_call(
        functools.partial(halve_kernel, len(kept + arrived)),
        out_shape=(shape,) * parts,
        in_specs=[vmem] * len(kept + arrived),
        out_specs=(vmem,) * parts,
        compiler_params=pltpu.CompilerParams(vmem_limit_bytes=VMEM_SOME),
        cost_estimate=SMALL,
        name="add_and_cut",
    )(*[in_vmem(part) for part in kept], *arrived)


def join_kernel(parts, far_ref, *refs):
    near_refs, out_refs = refs[:-parts], refs[-parts:]
    size = far_ref.shape[0] // parts
    near = near_refs[0][...].astype(F32)
    for near_ref in near_refs[1:]:
        near = near + near_ref[...].astype(F32)
    far = far_ref[...].astype(F32)
    for n, out_ref in enumerate(out_refs):
        rows = slice(n * size, (n + 1) * size)
        out_ref[...] = jnp.concatenate([near[rows], far[rows]], axis=0).astype(BF16)


def join(near, far, parts):
    count, width = far.shape
    vmem = pl.BlockSpec(memory_space=pltpu.VMEM)
    return pl.pallas_call(
        functools.partial(join_kernel, parts),
        out_shape=(pltpu.VMEM((2 * count // parts, width), BF16),) * parts,
        in_specs=[vmem] * (1 + len(near)),
        out_specs=(vmem,) * parts,
        compiler_params=pltpu.CompilerParams(vmem_limit_bytes=VMEM_SOME),
        cost_estimate=SMALL,
        name="join",
    )(far, *near)


def finish_kernel(side_ref, mixed_ref, *refs):
    block_refs, out_ref = refs[:-1], refs[-1]
    rows, width = mixed_ref.shape
    total = block_refs[0][...].astype(F32)
    for block_ref in block_refs[1:]:
        total = total + block_ref[...].astype(F32)
    near, far = total[:rows], total[rows:]
    first = side_ref[0] == 0
    half = width // 2
    for n, part in enumerate((jnp.where(first, near, far), jnp.where(first, far, near))):
        span = slice(n * half, (n + 1) * half)
        out_ref[:, span] = (mixed_ref[:, span].astype(F32) + part).astype(BF16)


def finish(side, mixed, blocks):
    vmem = pl.BlockSpec(memory_space=pltpu.VMEM)
    return pl.pallas_call(
        finish_kernel,
        out_shape=jax.ShapeDtypeStruct(mixed.shape, BF16),
        in_specs=[pl.BlockSpec(memory_space=pltpu.SMEM)] + [vmem] * (1 + len(blocks)),
        out_specs=vmem,
        compiler_params=pltpu.CompilerParams(vmem_limit_bytes=VMEM_SOME),
        name="finish",
    )(side, mixed, *blocks)


def dense(payload, mixed, codes):
    gate_codes, gate_scales, up_codes, up_scales, down_codes, down_scales = codes
    groups = lax.axis_size("dp")
    experts = lax.axis_size("expert")
    devices = groups * experts
    core, line, layer, plane = 1, 2, 4, experts
    layers = experts // layer
    side = lax.axis_index("dp").reshape(1).astype(jnp.int32)
    place = lax.axis_index("expert").reshape(1).astype(jnp.int32)

    def swap(block, offset):
        return lax.ppermute(block, ("dp", "expert"), [(i, i ^ offset) for i in range(devices)])

    side, place, gate_scales, down_scales, payload = lax.optimization_barrier(
        (side, place, gate_scales, down_scales, payload)
    )
    units = gate_codes.shape[1]
    half = down_codes.shape[1] // 2
    order = sorted(range(1, layers), key=lambda z: -z.bit_length())
    moved = {z: swap(payload, z * layer) for z in order}
    blocks = [moved[z] for z in range(1, layers)]
    w_gate, w_down = unpack_weights(
        (gate_codes, gate_scales, 0, units), (down_codes, down_scales, 0, half)
    )
    blocks, w_gate = lax.optimization_barrier((blocks, w_gate))
    stack = jnp.concatenate([payload] + blocks, axis=0)
    up_scales, stack = lax.optimization_barrier((up_scales, stack))
    beside, above, stack_pair = swap(stack, plane), swap(stack, line), swap(stack, core)
    (w_up,) = unpack_weights((up_codes, up_scales, 0, units))
    above, stack_pair, w_up = lax.optimization_barrier((above, stack_pair, w_up))
    across, above_pair = swap(above, plane), swap(above, core)
    above_pair, beside = lax.optimization_barrier((above_pair, beside))
    beside_pair = swap(beside, core)
    hidden_own, share_own = hidden_units(
        [stack, stack_pair, above, above_pair], w_gate, w_up, place, SPARE
    )
    other_peer = swap(hidden_own, plane)
    down_scales, hidden_own = lax.optimization_barrier((down_scales, hidden_own))
    (w_more,) = unpack_weights((down_codes, down_scales, half, half))
    across, w_more = lax.optimization_barrier((across, w_more))
    w_down = [w_down, w_more]
    hidden_other, share_other = hidden_units(
        [beside, beside_pair, across, swap(across, core)], w_gate, w_up, place
    )
    own_peer = swap(hidden_other, plane)

    count = share_own.shape[0]
    partial_other = own_down(side, hidden_other, w_down, count)
    partial_own = own_down(side, hidden_own, w_down, count)
    keep, send = peer_down(side, partial_other, other_peer, w_down, share_other, 2)
    keep, send = add_and_cut([keep], [swap(send, line)], 2)
    (onward,) = add_and_cut([keep], [swap(send, core)], 1)
    far = swap(onward, plane)
    keep_near, send_near, keep_far, send_far = peer_down(
        side, partial_own, own_peer, w_down, share_own, 4
    )
    (onward,) = add_and_cut([keep_far], [swap(send_far, core)], 1)
    near = [in_vmem(keep_near), swap(send_near, core), swap(onward, line)]
    blocks = join(near, far, layers)
    blocks = [blocks[0]] + [swap(blocks[z], z * layer) for z in order]
    return finish(side, mixed, blocks)


def slot_table(routes, experts, capacity):
    flattened = routes.reshape(-1)
    onehot = (flattened[:, None] == jnp.arange(experts, dtype=jnp.int32)[None, :]).astype(jnp.int32)
    ranking = jnp.sum((jnp.cumsum(onehot, axis=0) - 1) * onehot, axis=1)
    return (flattened * capacity + ranking).reshape(routes.shape)


def dispatch(block, slots, width):
    targets = jnp.arange(width, dtype=jnp.int32)
    placing = jnp.sum((slots[None, :, :] == targets[:, None, None]).astype(F32), axis=2)
    return jnp.dot(placing.astype(BF16), block, preferred_element_type=F32).astype(BF16)


def unpack(codes, scales):
    quarter, width = codes.shape
    divisors = jnp.array([1.0, 1.0 / 16, 1.0 / 256, 1.0 / 4096], F32)[:, None, None]
    lifted = jnp.floor(codes[None, :, :] * divisors)
    levels = lifted - 16.0 * jnp.floor(lifted * (1.0 / 16)) - 8.0
    height = 4 * quarter
    grouped = levels.reshape(height // GROUP, GROUP, width) * scales.astype(F32)[:, None, :]
    return grouped.reshape(height, width).astype(BF16)


def routed(normed, mixed, routes, route_weights, codes, capacity):
    gate_codes, gate_scales, up_codes, up_scales, down_codes, down_scales = codes
    experts = lax.axis_size("expert")
    groups = lax.axis_size("dp")
    row_count, width = mixed.shape
    own_slots = slot_table(routes, experts, capacity)
    w_gate = unpack(gate_codes, gate_scales)
    w_up = unpack(up_codes, up_scales)
    w_down = unpack(down_codes, down_scales)
    local_units = w_gate.shape[1]
    peer_rows = lax.all_gather(normed, "dp", axis=0, tiled=True).reshape(groups, row_count, width)
    peer_routes = lax.all_gather(routes, "dp", axis=0, tiled=True).reshape(groups, row_count, TOP)

    def build(block, table):
        return dispatch(block, slot_table(table, experts, capacity), experts * capacity)

    outgoing = jax.vmap(build)(peer_rows, peer_routes).reshape(groups, experts, capacity, width)
    items = lax.all_to_all(outgoing, "expert", split_axis=1, concat_axis=1, tiled=True)
    inputs = items.reshape(-1, width)
    gate = jnp.dot(inputs, w_gate, preferred_element_type=F32)
    upward = jnp.dot(inputs, w_up, preferred_element_type=F32)
    hidden = (jax.nn.silu(gate) * upward).astype(BF16).reshape(-1, local_units)
    produced = jnp.dot(
        lax.all_gather(hidden, "dp", axis=1, tiled=True), w_down, preferred_element_type=F32
    ).astype(BF16)
    produced = produced.reshape(groups, -1, produced.shape[1])
    returned = lax.all_to_all(
        lax.all_to_all(produced, "dp", split_axis=0, concat_axis=2, tiled=True),
        "expert",
        split_axis=1,
        concat_axis=0,
        tiled=True,
    )
    shares = route_weights / jnp.sum(route_weights, axis=1, keepdims=True)
    targets = jnp.arange(experts * capacity, dtype=jnp.int32)
    spreading = jnp.sum(
        jnp.where(own_slots[:, :, None] == targets[None, None, :], shares[:, :, None], 0.0), axis=1
    )
    combined = jnp.dot(
        spreading, returned.reshape(-1, width).astype(F32), precision=lax.Precision.HIGHEST
    )
    return (mixed.astype(F32) + combined).astype(BF16)


def body(
    queries,
    new_kv,
    cache_keys,
    cache_values,
    lengths,
    residual,
    norm_gain,
    routes,
    route_weights,
    *packed,
):
    experts = lax.axis_size("expert")
    groups = lax.axis_size("dp")
    row_count = queries.shape[0]
    capacity = min(row_count, max(2, 2 * row_count * TOP // experts))
    every = (
        capacity == row_count
        and groups == 2
        and experts <= LANES // 2
        and experts % 4 == 0
        and experts & (experts - 1) == 0
    )
    mixed, payload = front(
        queries,
        new_kv,
        cache_keys,
        cache_values,
        lengths,
        residual,
        norm_gain,
        routes,
        route_weights,
        LANES if every else 0,
    )
    codes = [array[0] for array in packed]
    if every:
        return dense(payload, mixed, codes)
    return routed(payload, mixed, routes, route_weights, codes, capacity)


def solution(mesh):
    return jax.shard_map(
        body,
        mesh=mesh,
        in_specs=(
            P(("dp", "expert"), None),
            P(("dp", "expert"), None, None),
            P(("dp", "expert"), None, None),
            P(("dp", "expert"), None, None),
            P(("dp", "expert")),
            P(("dp", "expert"), None),
            P(),
            P(("dp", "expert"), None),
            P(("dp", "expert"), None),
            P("expert", None, "dp"),
            P("expert", None, "dp"),
            P("expert", None, "dp"),
            P("expert", None, "dp"),
            P("expert", None, "dp"),
            P("expert", None, "dp"),
        ),
        out_specs=P(("dp", "expert"), None),
        check_vma=False,
    )
```

```python
import functools

import jax
import jax.numpy as jnp
from jax import lax
from jax.experimental import pallas as pl
from jax.experimental.pallas import tpu as pltpu
from jax.sharding import PartitionSpec as P

HEAD_DIM = 128
GROUP = 128
TOP = 8
LANES = 128
VMEM_LIMIT = 56 * 2**20
VMEM_SOME = 16 * 2**20
VMEM_MORE = 24 * 2**20
SPARE = 16
SMALL = pl.CostEstimate(flops=1, bytes_accessed=1, transcendentals=0)
F32 = jnp.float32
BF16 = jnp.bfloat16


def front_kernel(
    lengths_ref,
    queries_ref,
    new_kv_ref,
    keys_ref,
    values_ref,
    residual_ref,
    gain_ref,
    routes_ref,
    weights_ref,
    mixed_ref,
    payload_ref,
):
    rows, cache, kv_width = keys_ref.shape
    width = queries_ref.shape[1]
    kv_heads = kv_width // HEAD_DIM
    per = width // kv_width
    scaling = HEAD_DIM ** (-0.5)
    row_id = lax.broadcasted_iota(jnp.int32, (rows, rows * cache), 0)
    lane_id = lax.broadcasted_iota(jnp.int32, (rows, rows * cache), 1)
    bound = jnp.zeros((rows, rows * cache), jnp.int32)
    for r in range(rows):
        bound = jnp.where(row_id == r, r * cache + lengths_ref[r], bound)
    valid = (lane_id >= row_id * cache) & (lane_id < bound)
    earlier, current = [], []
    for j in range(kv_heads):
        span = slice(j * HEAD_DIM, (j + 1) * HEAD_DIM)
        heads = range(j * per, (j + 1) * per)
        queried = jnp.concatenate(
            [queries_ref[:, h * HEAD_DIM : (h + 1) * HEAD_DIM].astype(F32) for h in heads], axis=0
        )
        keys = keys_ref[:, :, span].reshape(rows * cache, HEAD_DIM)
        earlier.append(
            lax.dot_general(
                queried.astype(BF16), keys, (((1,), (1,)), ((), ())), preferred_element_type=F32
            )
        )
        fresh_key = new_kv_ref[:, 0, span].astype(F32)
        current.append(queried.reshape(per, rows, HEAD_DIM) * fresh_key[None])
    earlier = jnp.concatenate(earlier, axis=0).reshape(kv_heads * per, rows, rows * cache)
    earlier = jnp.where(valid[None], earlier * scaling, -1e30)
    current = jnp.sum(jnp.concatenate(current, axis=0), axis=-1, keepdims=True) * scaling
    largest = jnp.maximum(jnp.max(earlier, axis=-1, keepdims=True), current)
    earlier_w = jnp.where(valid[None], jnp.exp(earlier - largest), 0.0)
    current_w = jnp.exp(current - largest)
    inverse = 1.0 / (jnp.sum(earlier_w, axis=-1, keepdims=True) + current_w)
    earlier_p = (earlier_w * inverse).astype(BF16).reshape(kv_heads * per * rows, rows * cache)
    current_p = (current_w * inverse).astype(BF16).astype(F32)
    total = jnp.zeros((rows, HEAD_DIM), F32)
    for j in range(kv_heads):
        span = slice(j * HEAD_DIM, (j + 1) * HEAD_DIM)
        values = values_ref[:, :, span].reshape(rows * cache, HEAD_DIM)
        fresh_value = new_kv_ref[:, 1, span].astype(F32)
        attended = jnp.dot(
            earlier_p[j * per * rows : (j + 1) * per * rows], values, preferred_element_type=F32
        )
        attended = attended.reshape(per, rows, HEAD_DIM)
        attended = attended + current_p[j * per : (j + 1) * per] * fresh_value[None]
        for g in range(per):
            h = j * per + g
            place = slice(h * HEAD_DIM, (h + 1) * HEAD_DIM)
            mixed = (
                residual_ref[:, place].astype(F32) + attended[g].astype(BF16).astype(F32)
            ).astype(BF16)
            mixed_ref[:, place] = mixed
            widened = mixed.astype(F32)
            total = total + widened * widened
    meansq = jnp.sum(total, axis=-1, keepdims=True) * (1.0 / width)
    inverse = lax.rsqrt(meansq + 1e-06)
    payload_ref[:, :width] = (
        mixed_ref[...].astype(F32) * inverse * gain_ref[...].astype(F32).reshape(1, width)
    ).astype(BF16)
    if payload_ref.shape[1] > width:
        shares = weights_ref[...] / jnp.sum(weights_ref[...], axis=1, keepdims=True)
        lane = lax.broadcasted_iota(jnp.int32, (rows, LANES), 1)
        expert = jnp.where(lane < LANES // 2, lane, lane - LANES // 2)
        table = jnp.zeros((rows, LANES), F32)
        for k in range(routes_ref.shape[1]):
            table = table + jnp.where(
                routes_ref[:, k : k + 1] == expert, shares[:, k : k + 1], 0.0
            )
        high = table.astype(BF16).astype(F32)
        payload_ref[:, width:] = jnp.where(lane < LANES // 2, high, table - high).astype(BF16)


def front(queries, new_kv, keys, values, lengths, residual, gain, routes, weights, extra):
    rows, width = queries.shape
    vmem = pl.BlockSpec(memory_space=pltpu.VMEM)
    shape = pltpu.VMEM if extra else jax.ShapeDtypeStruct
    return pl.pallas_call(
        front_kernel,
        out_shape=(shape((rows, width), BF16), shape((rows, width + extra), BF16)),
        in_specs=[pl.BlockSpec(memory_space=pltpu.SMEM)] + [vmem] * 8,
        out_specs=(vmem, vmem),
        compiler_params=pltpu.CompilerParams(vmem_limit_bytes=VMEM_LIMIT),
        cost_estimate=SMALL,
        name="front",
    )(lengths, queries, new_kv, keys, values, residual, gain, routes, weights)


def in_vmem(array):
    return pltpu.with_memory_space_constraint(array, pltpu.VMEM)


def in_hbm(array):
    return pltpu.with_memory_space_constraint(array, pltpu.HBM)


def unpack_kernel(firsts, codes_refs, scales_hbms, *refs):
    out_refs, (words_refs, scales_refs, sems, scales_sem) = refs[: len(firsts)], refs[len(firsts) :]

    def copy_scales(n):
        columns = pl.ds(firsts[n], words_refs[n].shape[1])
        return pltpu.make_async_copy(
            scales_hbms[n].at[:, columns], scales_refs[n], scales_sem.at[n]
        )

    def fetch(turn):
        n, group = turns[turn]
        rows = pl.ds(group * GROUP, GROUP)
        columns = pl.ds(firsts[n], words_refs[n].shape[1])
        return pltpu.make_async_copy(
            codes_refs[n].at[rows, columns], words_refs[n].at[rows, :], sems.at[turn]
        )

    turns = [
        (n, group)
        for n, words_ref in enumerate(words_refs)
        for group in range(words_ref.shape[0] // GROUP)
    ]
    ahead = 3
    copy_scales(0).start()
    for turn in range(min(ahead, len(turns))):
        fetch(turn).start()
    for n in range(1, len(firsts)):
        copy_scales(n).start()
    for turn, (n, group) in enumerate(turns):
        words_ref, out_ref = words_refs[n], out_refs[n]
        quarter, width = words_ref.shape
        groups = quarter // GROUP
        step = 256 if width % 256 == 0 else LANES
        if turn + ahead < len(turns):
            fetch(turn + ahead).start()
        if group == 0:
            copy_scales(n).wait()
            scales = scales_refs[n][...].astype(F32)
        fetch(turn).wait()
        for column in range(0, width, step):
            spans = [
                jnp.broadcast_to(
                    scales[k * groups + group : k * groups + group + 1, column : column + step],
                    (16, step),
                ).astype(BF16)
                for k in range(4)
            ]

            def chunk(
                i, carry, group=group, column=column, spans=spans, words_ref=words_ref, out_ref=out_ref
            ):
                start = pl.multiple_of(group * GROUP + i * 16, 16)
                words = words_ref[pl.ds(start, 16), column : column + step].astype(jnp.int32)
                for k in range(4):
                    digit = words if k == 0 else lax.shift_right_logical(words, 4 * k)
                    if k < 3:
                        digit = digit & 15
                    level = digit.astype(F32).astype(BF16) - jnp.asarray(8, BF16)
                    out_ref[pl.ds(k * quarter + start, 16), column : column + step] = (
                        level * spans[k]
                    )
                return carry

            lax.fori_loop(0, GROUP // 16, chunk, 0, unroll=True)


def unpack_weights(*jobs):
    hbm = pl.BlockSpec(memory_space=pltpu.HBM)
    vmem = pl.BlockSpec(memory_space=pltpu.VMEM)
    shapes = [(codes.shape[0], width) for codes, _, _, width in jobs]
    turns = sum(quarter // GROUP for quarter, _ in shapes)
    return pl.pallas_call(
        functools.partial(unpack_kernel, tuple(job[2] for job in jobs)),
        out_shape=[pltpu.VMEM((4 * quarter, width), BF16) for quarter, width in shapes],
        in_specs=[[hbm] * len(jobs)] * 2,
        out_specs=[vmem] * len(jobs),
        scratch_shapes=[
            [pltpu.VMEM(shape, F32) for shape in shapes],
            [pltpu.VMEM((4 * quarter // GROUP, width), BF16) for quarter, width in shapes],
            pltpu.SemaphoreType.DMA((turns,)),
            pltpu.SemaphoreType.DMA((len(jobs),)),
        ],
        compiler_params=pltpu.CompilerParams(vmem_limit_bytes=VMEM_MORE),
        cost_estimate=SMALL,
        name="unpack_weights",
    )([in_hbm(job[0]) for job in jobs], [in_hbm(job[1]) for job in jobs])


def hidden_kernel(place_ref, *refs):
    pieces, (gate_ref, up_ref, out_ref, share_ref, rows_ref) = refs[:-5], refs[-5:]
    depth, width = gate_ref.shape
    block = pieces[0].shape[0]
    count = block * len(pieces)
    for n, piece in enumerate(pieces):
        rows_ref[n * block : (n + 1) * block, :] = piece[:, :depth]
        table = piece[:, depth:].astype(F32)
        lane = lax.broadcasted_iota(jnp.int32, table.shape, 1)
        mine = place_ref[0]
        chosen = (lane == mine) | (lane == mine + LANES // 2)
        share = jnp.sum(jnp.where(chosen, table, 0.0), axis=1, keepdims=True)
        share_ref[n * block : (n + 1) * block, :] = jnp.broadcast_to(share, table.shape)
    step = 256
    for column in range(0, width, step):
        span = slice(column, column + step)
        gate = jnp.dot(rows_ref[...], gate_ref[:, span], preferred_element_type=F32)
        upward = jnp.dot(rows_ref[...], up_ref[:, span], preferred_element_type=F32)
        out_ref[:count, span] = (gate / (1.0 + jnp.exp(-gate)) * upward).astype(BF16)
    if out_ref.shape[0] > count:
        out_ref[count:, :] = jnp.zeros((out_ref.shape[0] - count, width), BF16)


def hidden_units(pieces, w_gate, w_up, place, spare=0):
    block, padded = pieces[0].shape
    count = block * len(pieces)
    depth, width = w_gate.shape
    vmem = pl.BlockSpec(memory_space=pltpu.VMEM)
    return pl.pallas_call(
        hidden_kernel,
        out_shape=(pltpu.VMEM((count + spare, width), BF16), pltpu.VMEM((count, LANES), F32)),
        in_specs=[pl.BlockSpec(memory_space=pltpu.SMEM)] + [vmem] * (len(pieces) + 2),
        out_specs=(vmem, vmem),
        scratch_shapes=[pltpu.VMEM((count, depth), BF16)],
        compiler_params=pltpu.CompilerParams(vmem_limit_bytes=VMEM_SOME),
        cost_estimate=SMALL,
        name="gate_up",
    )(place, *pieces, in_vmem(w_gate), in_vmem(w_up))


def own_down_kernel(side_ref, hidden_ref, weight_refs, out_ref):
    half = hidden_ref.shape[1]
    rows = pl.ds(pl.multiple_of(side_ref[0] * half, half), half)
    step = 256
    for n, weight_ref in enumerate(weight_refs):
        width = weight_ref.shape[1]
        for column in range(0, width, step):
            out_ref[:, n * width + column : n * width + column + step] = jnp.dot(
                hidden_ref[: out_ref.shape[0]],
                weight_ref[rows, column : column + step],
                preferred_element_type=F32,
            )


def own_down(side, hidden, weights, count):
    width = sum(weight.shape[1] for weight in weights)
    vmem = pl.BlockSpec(memory_space=pltpu.VMEM)
    return pl.pallas_call(
        own_down_kernel,
        out_shape=pltpu.VMEM((count, width), F32),
        in_specs=[pl.BlockSpec(memory_space=pltpu.SMEM), vmem, [vmem] * len(weights)],
        out_specs=vmem,
        compiler_params=pltpu.CompilerParams(vmem_limit_bytes=VMEM_SOME),
        cost_estimate=SMALL,
        name="down_own",
    )(side, in_vmem(hidden), [in_vmem(weight) for weight in weights])


def peer_down_kernel(side_ref, partial_ref, hidden_ref, weight_refs, share_ref, *out_refs):
    count, half = partial_ref.shape[0], hidden_ref.shape[1]
    rows = pl.ds(pl.multiple_of((1 - side_ref[0]) * half, half), half)
    step = 256
    cut = count // len(out_refs)
    for n, weight_ref in enumerate(weight_refs):
        width = weight_ref.shape[1]
        for column in range(0, width, step):
            span = slice(n * width + column, n * width + column + step)
            produced = partial_ref[:, span] + jnp.dot(
                hidden_ref[:count],
                weight_ref[rows, column : column + step],
                preferred_element_type=F32,
            )
            result = (produced.astype(BF16).astype(F32) * share_ref[:, :1]).astype(BF16)
            for m, out_ref in enumerate(out_refs):
                out_ref[:, span] = result[m * cut : (m + 1) * cut]


def peer_down(side, partial, hidden, weights, share, parts):
    count, width = partial.shape
    vmem = pl.BlockSpec(memory_space=pltpu.VMEM)
    return pl.pallas_call(
        peer_down_kernel,
        out_shape=(pltpu.VMEM((count // parts, width), BF16),) * parts,
        in_specs=[pl.BlockSpec(memory_space=pltpu.SMEM), vmem, vmem, [vmem] * len(weights), vmem],
        out_specs=(vmem,) * parts,
        compiler_params=pltpu.CompilerParams(vmem_limit_bytes=VMEM_SOME),
        cost_estimate=SMALL,
        name="down_peer",
    )(side, in_vmem(partial), hidden, [in_vmem(weight) for weight in weights], in_vmem(share))


def halve_kernel(terms, *refs):
    term_refs, out_refs = refs[:terms], refs[terms:]
    total = term_refs[0][...].astype(F32)
    for term_ref in term_refs[1:]:
        total = total + term_ref[...].astype(F32)
    size = total.shape[0] // len(out_refs)
    for n, out_ref in enumerate(out_refs):
        out_ref[...] = total[n * size : (n + 1) * size].astype(out_ref.dtype)


def add_and_cut(kept, arrived, parts):
    count, width = kept[0].shape
    vmem = pl.BlockSpec(memory_space=pltpu.VMEM)
    shape = pltpu.VMEM((count // parts, width), BF16)
    return pl.pallas_call(
        functools.partial(halve_kernel, len(kept + arrived)),
        out_shape=(shape,) * parts,
        in_specs=[vmem] * len(kept + arrived),
        out_specs=(vmem,) * parts,
        compiler_params=pltpu.CompilerParams(vmem_limit_bytes=VMEM_SOME),
        cost_estimate=SMALL,
        name="add_and_cut",
    )(*[in_vmem(part) for part in kept], *arrived)


def join_kernel(parts, far_ref, *refs):
    near_refs, out_refs = refs[:-parts], refs[-parts:]
    size = far_ref.shape[0] // parts
    near = near_refs[0][...].astype(F32)
    for near_ref in near_refs[1:]:
        near = near + near_ref[...].astype(F32)
    far = far_ref[...].astype(F32)
    for n, out_ref in enumerate(out_refs):
        rows = slice(n * size, (n + 1) * size)
        out_ref[...] = jnp.concatenate([near[rows], far[rows]], axis=0).astype(BF16)


def join(near, far, parts):
    count, width = far.shape
    vmem = pl.BlockSpec(memory_space=pltpu.VMEM)
    return pl.pallas_call(
        functools.partial(join_kernel, parts),
        out_shape=(pltpu.VMEM((2 * count // parts, width), BF16),) * parts,
        in_specs=[vmem] * (1 + len(near)),
        out_specs=(vmem,) * parts,
        compiler_params=pltpu.CompilerParams(vmem_limit_bytes=VMEM_SOME),
        cost_estimate=SMALL,
        name="join",
    )(far, *near)


def finish_kernel(side_ref, mixed_ref, *refs):
    block_refs, out_ref = refs[:-1], refs[-1]
    rows, width = mixed_ref.shape
    total = block_refs[0][...].astype(F32)
    for block_ref in block_refs[1:]:
        total = total + block_ref[...].astype(F32)
    near, far = total[:rows], total[rows:]
    first = side_ref[0] == 0
    half = width // 2
    for n, part in enumerate((jnp.where(first, near, far), jnp.where(first, far, near))):
        span = slice(n * half, (n + 1) * half)
        out_ref[:, span] = (mixed_ref[:, span].astype(F32) + part).astype(BF16)


def finish(side, mixed, blocks):
    vmem = pl.BlockSpec(memory_space=pltpu.VMEM)
    return pl.pallas_call(
        finish_kernel,
        out_shape=jax.ShapeDtypeStruct(mixed.shape, BF16),
        in_specs=[pl.BlockSpec(memory_space=pltpu.SMEM)] + [vmem] * (1 + len(blocks)),
        out_specs=vmem,
        compiler_params=pltpu.CompilerParams(vmem_limit_bytes=VMEM_SOME),
        name="finish",
    )(side, mixed, *blocks)


def dense(payload, mixed, codes):
    gate_codes, gate_scales, up_codes, up_scales, down_codes, down_scales = codes
    groups = lax.axis_size("dp")
    experts = lax.axis_size("expert")
    devices = groups * experts
    core, line, layer, plane = 1, 2, 4, experts
    layers = experts // layer
    side = lax.axis_index("dp").reshape(1).astype(jnp.int32)
    place = lax.axis_index("expert").reshape(1).astype(jnp.int32)

    def swap(block, offset):
        return lax.ppermute(block, ("dp", "expert"), [(i, i ^ offset) for i in range(devices)])

    side, place, gate_scales, down_scales, payload = lax.optimization_barrier(
        (side, place, gate_scales, down_scales, payload)
    )
    units = gate_codes.shape[1]
    half = down_codes.shape[1] // 2
    order = sorted(range(1, layers), key=lambda z: -z.bit_length())
    blocks = [swap(payload, z * layer) for z in order]
    w_gate, w_down = unpack_weights(
        (gate_codes, gate_scales, 0, units), (down_codes, down_scales, 0, half)
    )
    blocks, w_gate = lax.optimization_barrier((blocks, w_gate))
    stack = jnp.concatenate([payload] + blocks, axis=0)
    up_scales, stack = lax.optimization_barrier((up_scales, stack))
    beside, above, stack_pair = swap(stack, plane), swap(stack, line), swap(stack, core)
    (w_up,) = unpack_weights((up_codes, up_scales, 0, units))
    above, stack_pair, w_up = lax.optimization_barrier((above, stack_pair, w_up))
    across, above_pair = swap(above, plane), swap(above, core)
    above_pair, beside = lax.optimization_barrier((above_pair, beside))
    beside_pair = swap(beside, core)
    hidden_own, share_own = hidden_units(
        [stack, stack_pair, above, above_pair], w_gate, w_up, place, SPARE
    )
    other_peer = swap(hidden_own, plane)
    down_scales, hidden_own = lax.optimization_barrier((down_scales, hidden_own))
    (w_more,) = unpack_weights((down_codes, down_scales, half, half))
    across, w_more = lax.optimization_barrier((across, w_more))
    w_down = [w_down, w_more]
    hidden_other, share_other = hidden_units(
        [beside, beside_pair, across, swap(across, core)], w_gate, w_up, place
    )
    own_peer = swap(hidden_other, plane)

    count = share_own.shape[0]
    partial_other = own_down(side, hidden_other, w_down, count)
    partial_own = own_down(side, hidden_own, w_down, count)
    keep, send = peer_down(side, partial_other, other_peer, w_down, share_other, 2)
    keep, send = add_and_cut([keep], [swap(send, line)], 2)
    (onward,) = add_and_cut([keep], [swap(send, core)], 1)
    far = swap(onward, plane)
    keep_near, send_near, keep_far, send_far = peer_down(
        side, partial_own, own_peer, w_down, share_own, 4
    )
    (onward,) = add_and_cut([keep_far], [swap(send_far, core)], 1)
    near = [in_vmem(keep_near), swap(send_near, core), swap(onward, line)]
    blocks = join(near, far, layers)
    blocks = [blocks[0]] + [swap(block, z * layer) for block, z in zip(blocks[1:], order)]
    return finish(side, mixed, blocks)


def slot_table(routes, experts, capacity):
    flattened = routes.reshape(-1)
    onehot = (flattened[:, None] == jnp.arange(experts, dtype=jnp.int32)[None, :]).astype(jnp.int32)
    ranking = jnp.sum((jnp.cumsum(onehot, axis=0) - 1) * onehot, axis=1)
    return (flattened * capacity + ranking).reshape(routes.shape)


def dispatch(block, slots, width):
    targets = jnp.arange(width, dtype=jnp.int32)
    placing = jnp.sum((slots[None, :, :] == targets[:, None, None]).astype(F32), axis=2)
    return jnp.dot(placing.astype(BF16), block, preferred_element_type=F32).astype(BF16)


def unpack(codes, scales):
    quarter, width = codes.shape
    divisors = jnp.array([1.0, 1.0 / 16, 1.0 / 256, 1.0 / 4096], F32)[:, None, None]
    lifted = jnp.floor(codes[None, :, :] * divisors)
    levels = lifted - 16.0 * jnp.floor(lifted * (1.0 / 16)) - 8.0
    height = 4 * quarter
    grouped = levels.reshape(height // GROUP, GROUP, width) * scales.astype(F32)[:, None, :]
    return grouped.reshape(height, width).astype(BF16)


def routed(normed, mixed, routes, route_weights, codes, capacity):
    gate_codes, gate_scales, up_codes, up_scales, down_codes, down_scales = codes
    experts = lax.axis_size("expert")
    groups = lax.axis_size("dp")
    row_count, width = mixed.shape
    own_slots = slot_table(routes, experts, capacity)
    w_gate = unpack(gate_codes, gate_scales)
    w_up = unpack(up_codes, up_scales)
    w_down = unpack(down_codes, down_scales)
    local_units = w_gate.shape[1]
    peer_rows = lax.all_gather(normed, "dp", axis=0, tiled=True).reshape(groups, row_count, width)
    peer_routes = lax.all_gather(routes, "dp", axis=0, tiled=True).reshape(groups, row_count, TOP)

    def build(block, table):
        return dispatch(block, slot_table(table, experts, capacity), experts * capacity)

    outgoing = jax.vmap(build)(peer_rows, peer_routes).reshape(groups, experts, capacity, width)
    items = lax.all_to_all(outgoing, "expert", split_axis=1, concat_axis=1, tiled=True)
    inputs = items.reshape(-1, width)
    gate = jnp.dot(inputs, w_gate, preferred_element_type=F32)
    upward = jnp.dot(inputs, w_up, preferred_element_type=F32)
    hidden = (jax.nn.silu(gate) * upward).astype(BF16).reshape(-1, local_units)
    produced = jnp.dot(
        lax.all_gather(hidden, "dp", axis=1, tiled=True), w_down, preferred_element_type=F32
    ).astype(BF16)
    produced = produced.reshape(groups, -1, produced.shape[1])
    returned = lax.all_to_all(
        lax.all_to_all(produced, "dp", split_axis=0, concat_axis=2, tiled=True),
        "expert",
        split_axis=1,
        concat_axis=0,
        tiled=True,
    )
    shares = route_weights / jnp.sum(route_weights, axis=1, keepdims=True)
    targets = jnp.arange(experts * capacity, dtype=jnp.int32)
    spreading = jnp.sum(
        jnp.where(own_slots[:, :, None] == targets[None, None, :], shares[:, :, None], 0.0), axis=1
    )
    combined = jnp.dot(
        spreading, returned.reshape(-1, width).astype(F32), precision=lax.Precision.HIGHEST
    )
    return (mixed.astype(F32) + combined).astype(BF16)


def body(
    queries,
    new_kv,
    cache_keys,
    cache_values,
    lengths,
    residual,
    norm_gain,
    routes,
    route_weights,
    *packed,
):
    experts = lax.axis_size("expert")
    groups = lax.axis_size("dp")
    row_count = queries.shape[0]
    capacity = min(row_count, max(2, 2 * row_count * TOP // experts))
    every = (
        capacity == row_count
        and groups == 2
        and experts <= LANES // 2
        and experts % 4 == 0
        and experts & (experts - 1) == 0
    )
    mixed, payload = front(
        queries,
        new_kv,
        cache_keys,
        cache_values,
        lengths,
        residual,
        norm_gain,
        routes,
        route_weights,
        LANES if every else 0,
    )
    codes = [array[0] for array in packed]
    if every:
        return dense(payload, mixed, codes)
    return routed(payload, mixed, routes, route_weights, codes, capacity)


def solution(mesh):
    return jax.shard_map(
        body,
        mesh=mesh,
        in_specs=(
            P(("dp", "expert"), None),
            P(("dp", "expert"), None, None),
            P(("dp", "expert"), None, None),
            P(("dp", "expert"), None, None),
            P(("dp", "expert")),
            P(("dp", "expert"), None),
            P(),
            P(("dp", "expert"), None),
            P(("dp", "expert"), None),
            P("expert", None, "dp"),
            P("expert", None, "dp"),
            P("expert", None, "dp"),
            P("expert", None, "dp"),
            P("expert", None, "dp"),
            P("expert", None, "dp"),
        ),
        out_specs=P(("dp", "expert"), None),
        check_vma=False,
    )
```
